256 devices in a mesh: src: 8 (over x_hi, y), tgt: 32 (over z, x_lo, core).
Axes of the slice: x: 4 (x_hi: 2, x_lo: 2; x = x_hi * 2 + x_lo), y: 4, z: 8, core: 2. Of those that a mesh axis runs over, the one named last changes fastest.
Arguments:
- sources: bfloat16 [16384, 256], P('tgt')
- targets: bfloat16 [131072, 256], P(('src', 'tgt'))
- target_potential: float32 [131072], P(('src', 'tgt')), may hold values from -24 to 24
- active: int32 [128, 512], P('tgt'), may hold values from 0 to 1023, as said below
Outputs:
- potential: float32 [16384], P('tgt')
- transport_map: float32 [16384, 256], P('tgt')
The draws below stay inside these ranges and needn't reach their ends.
Inputs may be any that keep to these rules, and one draw needn't show every extreme that they name: `active`: row b lists 512 different target block numbers, the first of them b % 1024.
All inputs are finite; a program needn't handle non-finite values.
Results may differ from the reference program's by a relative error of at most 0.008.
Values may be sent and summed in bfloat16 or wider, within the bound.
A program may use at most 64 MiB of HBM per device.

```python
import math
import jax
import jax.numpy as jnp
from jax import lax

D = 256
BLOCK = 128
SOURCES = 16384
TARGETS = 131072
SBLK = 128
NTB = 1024
TOP = 512


def shared_targets(key):
    key_base = jax.random.fold_in(key, 0)
    base = jax.random.normal(key_base, (TARGETS, D), jnp.float32)
    base = base.reshape(NTB, BLOCK, D)
    first = base[:, 0]
    second = base[:, 1]
    base = base.at[:, 0].set(first).at[:, 1].set(second)
    return base.reshape(TARGETS, D)


def draw_targets(key, part):
    values = shared_targets(key)
    return values.astype(jnp.bfloat16)


def draw_sources(key, part):
    own = jax.random.fold_in(key, 7)
    values = jax.random.normal(own, (SOURCES, D), jnp.float32)
    return values.astype(jnp.bfloat16)


def draw_active(key, part):
    own = jax.random.fold_in(key, 11)
    keys = jax.random.split(own, SBLK)
    diagonal = (jnp.arange(SBLK) % NTB).astype(jnp.int32)

    def one_row(row_key, home):
        order = jax.random.permutation(row_key, NTB - 1).astype(jnp.int32)[:TOP - 1]
        order = jnp.where(order >= home, order + 1, order)
        return jnp.concatenate([home[None], order]).astype(jnp.int32)
    return jax.vmap(one_row)(keys, diagonal)


def shard_levels(rng, extent, pieces, smallest, top_value):
    level, own = 1.0, jax.random.fold_in(rng, 6)
    for axis_at, shards_of in pieces:
        steps = jnp.exp(jax.random.uniform(jax.random.fold_in(own, axis_at), (shards_of,), jnp.float32, smallest / len(pieces), top_value / len(pieces)))
        level = level * jnp.repeat(steps, extent[axis_at] // shards_of).reshape([-1 if axis == axis_at else 1 for axis in range(len(extent))])
    return level


def bell_draw(stream_key, dims, scale, bound, shards=(), kind=jnp.bfloat16):
    drawn = jax.random.normal(stream_key, dims, jnp.float32) * scale
    if len(shards) > 0:
        drawn = shard_levels(stream_key, dims, shards, -0.22, 0.18) * drawn
    return jnp.clip(drawn, min=-bound, max=bound).astype(kind)


def setup_inputs(seed: int = 0) -> dict:
    streams_of = jax.random.split(jax.random.key(seed), 5)
    sources = draw_sources(jax.random.fold_in(streams_of[4], 71), 0)
    targets = draw_targets(jax.random.fold_in(streams_of[4], 71), 0)
    target_potential = bell_draw(streams_of[2], (TARGETS,), 4.0, 24.0, ((0, 256),), jnp.float32)
    active = draw_active(jax.random.fold_in(streams_of[4], 71), 0)
    return dict(sources=sources, targets=targets, target_potential=target_potential, active=active)


def reference(sources, targets, target_potential, active):
    eps = 0.5 * math.sqrt(D)
    target_float = targets.astype(jnp.float32)
    shifted = target_potential - 0.5 * lax.optimization_barrier(jnp.sum(target_float * target_float, axis=1))
    target_blocks = targets.reshape(NTB, BLOCK, D)
    shifted_blocks = shifted.reshape(NTB, BLOCK)
    source_blocks = sources.reshape(SBLK, BLOCK, D)

    def one_block(items):
        source_rows, listed = items
        chosen = target_blocks[listed].reshape(TOP * BLOCK, D)
        chosen_shift = shifted_blocks[listed].reshape(TOP * BLOCK)
        scores = lax.dot_general(source_rows, chosen, (((1,), (1,)), ((), ())), preferred_element_type=jnp.float32)
        scores = (scores + chosen_shift[None, :]) / eps
        top_row = lax.optimization_barrier(jnp.max(scores, axis=1))
        weights = jnp.exp(scores - top_row[:, None])
        total = lax.optimization_barrier(jnp.sum(weights, axis=1))
        numer = jnp.dot(weights.astype(jnp.bfloat16), chosen, preferred_element_type=jnp.float32)
        source_float = source_rows.astype(jnp.float32)
        value = 0.5 * lax.optimization_barrier(jnp.sum(source_float * source_float, axis=1)) - eps * (top_row + jnp.log(total))
        return (value, numer / total[:, None])
    values, images = lax.map(one_block, (source_blocks, active))
    return (values.reshape(SOURCES), images.reshape(SOURCES, D))
```

```python
import functools
import math

import jax
import jax.numpy as jnp
from jax import lax
from jax.experimental import pallas as pl
from jax.experimental.pallas import tpu as pltpu
from jax.sharding import PartitionSpec as P

MESH = pl.DeviceIdType.MESH
F32 = jnp.float32
BF16 = jnp.bfloat16
LOWEST = -1e38


def kernel(sizes, src_hbm, tgt_hbm, pot_hbm, act_hbm, val_ref, map_ref,
           src, pot, act, local, held, scores, weights, top, total, numer, mask, norm, stat, gotstat, gotnum, factor, gotval,
           recv, send_z, send_x, send_s, rs_recv, rs_send, ag_recv, ag_send):
    nsrc, ntgt, eps = sizes
    rows, width = src_hbm.shape
    piece = tgt_hbm.shape[0] // 2
    block = 128
    tile = 256
    rounds = ntgt // 4
    nz = ntgt // 4
    share = rows // nsrc
    sblocks = rows // block
    unit = math.log2(math.e) / eps

    s = lax.axis_index("src")
    t = lax.axis_index("tgt")
    half = nsrc // 2
    x_hi, y = s // half, s % half
    z, x_lo, core = t // 4, (t // 2) % 2, t % 2
    up = (s, (t + 4) % ntgt)
    down = (s, (t + ntgt - 4) % ntgt)
    twin = (s, z * 4 + x_lo * 2 + 1 - core)
    side_a = (s, z * 4 + (1 - x_lo) * 2 + core)
    side_b = ((1 - x_hi) * half + y, z * 4 + (1 - x_lo) * 2 + core)
    others = [((s + d) % nsrc, t) for d in range(1, nsrc)]

    barrier = pltpu.get_barrier_semaphore()
    for device in [up, down, twin, side_a, side_b] + others:
        pl.semaphore_signal(barrier, inc=1, device_id=device, device_id_type=MESH)

    loads = [
        pltpu.make_async_copy(tgt_hbm.at[part * piece:(part + 1) * piece, :],
                              held.at[0, 1 - part, 0:piece, :], local.at[part])
        for part in range(2)
    ] + [
        pltpu.make_async_copy(pot_hbm, pot, local.at[2]),
        pltpu.make_async_copy(src_hbm, src, local.at[3]),
        pltpu.make_async_copy(act_hbm, act, local.at[4]),
    ]
    for load in loads:
        load.start()

    def remote(source, target, ssem, rsem, device):
        return pltpu.make_async_remote_copy(
            src_ref=source, dst_ref=target, send_sem=ssem, recv_sem=rsem, device_id=device, device_id_type=MESH
        )

    def send_up(k, lane, to):
        return remote(held.at[k, lane], held.at[to, 0], send_z.at[0, to], recv.at[to, 0], up)

    def send_down(k, lane, to):
        return remote(held.at[k, lane], held.at[to, 1], send_z.at[1, to], recv.at[to, 1], down)

    def send_a(k, lane):
        return remote(held.at[k, lane], held.at[k + 1, 2], send_x.at[0, k + 1], recv.at[k + 1, 2], side_a)

    def send_b(k, lane):
        return remote(held.at[k, lane], held.at[k + 1, 3], send_x.at[1, k + 1], recv.at[k + 1, 3], side_b)

    def send_twin(k, lane):
        return remote(held.at[k, lane], held.at[k, lane + 4], send_s.at[k, lane], recv.at[k, lane + 4], twin)

    def arrived(k, lane):
        remote(held.at[k, lane], held.at[k, lane], send_z.at[0, 0], recv.at[k, lane], up).wait_recv()

    ones = jnp.ones((8, width), BF16)
    across = (((1,), (1,)), ((), ()))

    def half_norms(block_rows):
        wide = block_rows.astype(F32)
        square = 0.5 * (wide * wide)
        high = square.astype(BF16)
        low = (square - high.astype(F32)).astype(BF16)
        return lax.dot_general(ones, high, across, preferred_element_type=F32) + lax.dot_general(
            ones, low, across, preferred_element_type=F32
        )

    for part in range(2):
        loads[part].wait()
        if part == 0:
            loads[2].wait()
        data = held[0, 1 - part, 0:piece, :]
        shifted = (pot[0:1, part * piece:(part + 1) * piece] - half_norms(data)[0:1, :]) * unit
        high = shifted.astype(BF16).astype(F32)
        middle = (shifted - high).astype(BF16).astype(F32)
        low = shifted - high - middle
        row = lax.broadcasted_iota(jnp.int32, (16, piece), 0)
        extra = jnp.where(row == 0, high, jnp.where(row == 1, middle, jnp.where(row == 2, low, 0.0)))
        held[0, 1 - part, piece:piece + 16, :] = extra.astype(BF16)

    pl.semaphore_wait(barrier, 5 + nsrc - 1)
    send_up(0, 1, 1).start()
    send_down(0, 0, 1).start()
    send_a(0, 1).start()
    send_b(0, 0).start()
    send_up(0, 0, 2).start()
    send_down(0, 1, 2).start()
    send_twin(0, 0).start()
    send_twin(0, 1).start()

    loads[3].wait()
    loads[4].wait()

    slots = (rounds + 1) * 8 * 2
    place = lax.broadcasted_iota(jnp.int32, (slots, block), 0)
    part_h, lane, k = place % 2, (place // 2) % 8, place // 16
    own_core = jnp.where(lane < 4, core, 1 - core)
    kind = lane % 4
    from_side = kind >= 2
    k = jnp.where(from_side, k - 1, k)
    odd = k % 2
    distance = (k + 1) // 2
    below = jnp.where(kind == 0, 1, jnp.where(kind == 1, 0, jnp.where(kind == 2, odd, 1 - odd)))
    letter = jnp.where(kind == 0, 1 - odd, jnp.where(kind == 1, odd, kind - 2))
    z_from = (z + jnp.where(below == 1, nz - distance, distance)) % nz
    x_lo_from = jnp.where(from_side, 1 - x_lo, x_lo)
    x_hi_from = jnp.where(kind == 3, 1 - x_hi, x_hi)
    owner = (x_hi_from * half + y) * ntgt + z_from * 4 + x_lo_from * 2 + own_core
    number = owner * 4 + letter * 2 + part_h
    for b in range(sblocks):
        hit = jnp.zeros((slots, block), F32)
        for e in range(act.shape[1] // block):
            hit = jnp.where(number == act[b:b + 1, e * block:(e + 1) * block], 1.0, hit)
        mask[b] = jnp.broadcast_to(jnp.max(hit, axis=1, keepdims=True), (slots, block))

    for b in range(sblocks):
        norm[b:b + 1, :] = half_norms(src[b * block:(b + 1) * block, :])[0:1, :]

    top[...] = jnp.full(top.shape, LOWEST, F32)
    total[...] = jnp.zeros(total.shape, F32)
    numer[...] = jnp.zeros(numer.shape, F32)

    def absorb(groups):
        pieces = [(k, start, count) for k, start, count in groups]
        for r in range(0, rows, tile):
            blocks = range(r // block, (r + tile) // block)
            maxima = {b: top[b * block:(b + 1) * block, :] for b in blocks}
            i = 0
            for k, start, count in pieces:
                for lane in range(start, start + count, 2):
                    data = held[k, lane:lane + 2, 0:piece, :].reshape(2 * piece, width)
                    product = lax.dot_general(
                        src[r:r + tile, :], data, across, preferred_element_type=F32
                    ) * unit
                    for c in range(4):
                        near, h = lane + c // 2, c % 2
                        extra = held[k, near, piece:piece + 16, h * block:(h + 1) * block].astype(F32)
                        shift = jnp.sum(extra, axis=0, keepdims=True)
                        for b in blocks:
                            bit = mask[b, pl.ds((k * 8 + near) * 2 + h, 1), :]
                            bias = jnp.where(bit > 0.5, shift, LOWEST)
                            score = product[b * block - r:(b + 1) * block - r, c * block:(c + 1) * block] + bias
                            scores[b * block:(b + 1) * block, i * block:(i + 1) * block] = score
                            maxima[b] = jnp.maximum(maxima[b], score)
                        i += 1
            for b in blocks:
                at = slice(b * block, (b + 1) * block)
                new = jnp.broadcast_to(jnp.max(maxima[b], axis=1, keepdims=True), (block, block))
                scale = jnp.exp2(top[at, :] - new)
                top[at, :] = new
                summed = total[at, :] * scale
                for j in range(i):
                    weight = jnp.exp2(scores[at, j * block:(j + 1) * block] - new)
                    summed = summed + weight
                    weights[at, j * block:(j + 1) * block] = weight.astype(BF16)
                total[at, :] = summed
                numer[at, :] = numer[at, :] * jnp.concatenate([scale] * (width // block), axis=1)
            column = 0
            added = None
            for k, start, count in pieces:
                data = held[k, start:start + count, 0:piece, :].reshape(count * piece, width)
                term = jnp.dot(
                    weights[r:r + tile, column:column + count * piece], data, preferred_element_type=F32
                )
                added = term if added is None else added + term
                column += count * piece
            numer[r:r + tile, :] += added

    absorb([(0, 0, 2)])

    def one_round(k, early):
        odd = k % 2
        for lane, onward in ((0, send_up), (1, send_down)):
            arrived(k, lane)

            @pl.when(k + 2 < rounds)
            def _():
                onward(k, lane, k + 2).start()
        send_a(k, 1 - odd).start()
        send_b(k, odd).start()
        send_twin(k, 0).start()
        send_twin(k, 1).start()
        for lane in (2, 3):
            arrived(k, lane)
            send_twin(k, lane).start()
        for lane in (4, 5) if early else (4, 5, 6, 7):
            arrived(k - 1, lane)
        absorb([(k, 0, 4), (k - 1, 4, 2 if early else 4)])

    one_round(jnp.int32(1), True)

    def later(k, carry):
        one_round(k, False)
        return carry

    lax.fori_loop(2, rounds, later, 0)
    for lane in (4, 5, 6, 7):
        arrived(rounds - 1, lane)
    absorb([(rounds - 1, 4, 4)])
    for lane in (2, 3):
        arrived(rounds, lane)
        send_twin(rounds, lane).start()
    absorb([(rounds, 2, 2)])
    for lane in (6, 7):
        arrived(rounds, lane)
    absorb([(rounds, 6, 2)])

    column = lax.broadcasted_iota(jnp.int32, (block, block), 1)
    for b in range(sblocks):
        at = slice(b * block, (b + 1) * block)
        den = jnp.broadcast_to(jnp.sum(total[at, :], axis=1, keepdims=True), (block, block))
        stat[b] = jnp.where(column == 0, top[at, :], den).T[0:8, :]

    def give_stat(d):
        q = (s + d) % nsrc
        return remote(stat.at[q // 2], gotstat.at[d], rs_send.at[0, d], rs_recv.at[0, d], (q, t))

    def give_rows(d):
        q = (s + d) % nsrc
        return remote(numer.at[pl.ds(pl.multiple_of(q * share, share), share), :], gotnum.at[d],
                      rs_send.at[1, d], rs_recv.at[1, d], (q, t))

    for d in range(1, nsrc):
        give_stat(d).start()
        give_rows(d).start()
    gotstat[0] = stat[s // 2]
    mine = pl.ds(pl.multiple_of(s * share, share), share)
    for d in range(1, nsrc):
        give_stat(d).wait_recv()
    tops = jnp.concatenate([gotstat[d, 0:1, :] for d in range(nsrc)], axis=0)
    dens = jnp.concatenate([gotstat[d, 1:2, :] for d in range(nsrc)], axis=0)
    best = jnp.max(tops, axis=0, keepdims=True)
    scale = jnp.exp2(tops - best)
    den = jnp.sum(scale * dens, axis=0, keepdims=True)
    value = norm[pl.ds(s // 2, 1), :] - eps * (best * math.log(2.0) + jnp.log(den))
    gotval[s] = jnp.broadcast_to(value, (8, block))
    ratio = scale / den
    factor[...] = jnp.concatenate([ratio] + [jnp.zeros((block - nsrc, block), F32)], axis=0).T
    column = factor[pl.ds(pl.multiple_of((s % 2) * share, share), share), :]
    image = numer[mine, :] * column[:, 0:1]
    for d in range(1, nsrc):
        give_rows(d).wait_recv()
        image = image + gotnum[d] * column[:, d:d + 1]
    map_ref[mine, :] = image

    def spread(d):
        device = ((s + d) % nsrc, t)
        return (
            remote(gotval.at[s], gotval.at[s], ag_send.at[0, d], ag_recv.at[0, d], device),
            remote(map_ref.at[mine, :], map_ref.at[mine, :], ag_send.at[1, d], ag_recv.at[1, d], device),
        )

    def gathered(d):
        q = (s + nsrc - d) % nsrc
        device = ((s + d) % nsrc, t)
        theirs = pl.ds(pl.multiple_of(q * share, share), share)
        return (
            remote(gotval.at[q], gotval.at[q], ag_send.at[0, d], ag_recv.at[0, d], device),
            remote(map_ref.at[theirs, :], map_ref.at[theirs, :], ag_send.at[1, d], ag_recv.at[1, d], device),
        )

    for d in range(1, nsrc):
        for copy in spread(d):
            copy.start()

    for to in (1, 2):
        send_up(0, 0, to).wait_send()
        send_down(0, 0, to).wait_send()

    def drain(k, carry):
        @pl.when(k + 2 < rounds)
        def _():
            send_up(k, 0, k + 2).wait_send()
            send_down(k, 1, k + 2).wait_send()
        send_a(k, 0).wait_send()
        send_b(k, 0).wait_send()
        for lane in range(4):
            send_twin(k, lane).wait_send()
        return carry

    lax.fori_loop(1, rounds, drain, 0)
    send_a(0, 0).wait_send()
    send_b(0, 0).wait_send()
    for lane in (0, 1):
        send_twin(0, lane).wait_send()
    for lane in (2, 3):
        send_twin(rounds, lane).wait_send()
    for d in range(1, nsrc):
        give_stat(d).wait_send()
        give_rows(d).wait_send()
    for d in range(1, nsrc):
        for copy in gathered(d):
            copy.wait_recv()
        for copy in spread(d):
            copy.wait_send()
    lane = lax.broadcasted_iota(jnp.int32, (1, block), 1)
    for b in range(sblocks):
        val_ref[b:b + 1, :] = jnp.where(lane < share, gotval[2 * b, 0:1, :], gotval[2 * b + 1, 0:1, :])


def per_device(sources, targets, target_potential, active):
    rows, width = sources.shape
    count = targets.shape[0]
    nsrc, ntgt = lax.axis_size("src"), lax.axis_size("tgt")
    eps = 0.5 * math.sqrt(width)
    piece = count // 2
    rounds = ntgt // 4
    share = rows // nsrc
    sblocks = rows // 128
    dma = pltpu.SemaphoreType.DMA
    vmem = pl.BlockSpec(memory_space=pltpu.VMEM)
    value, image = pl.pallas_call(
        functools.partial(kernel, (nsrc, ntgt, eps)),
        out_shape=(
            jax.ShapeDtypeStruct((sblocks, 128), F32),
            jax.ShapeDtypeStruct((rows, width), F32),
        ),
        in_specs=[pl.BlockSpec(memory_space=pl.ANY)] * 4,
        out_specs=(vmem, vmem),
        scratch_shapes=[
            pltpu.VMEM((rows, width), BF16),
            pltpu.VMEM((1, count), F32),
            pltpu.VMEM(active.shape, jnp.int32),
            dma((5,)),
            pltpu.VMEM((rounds + 1, 8, piece + 16, width), BF16),
            pltpu.VMEM((rows, 8 * piece), F32),
            pltpu.VMEM((rows, 8 * piece), BF16),
            pltpu.VMEM((rows, 128), F32),
            pltpu.VMEM((rows, 128), F32),
            pltpu.VMEM((rows, width), F32),
            pltpu.VMEM((sblocks, (rounds + 1) * 16, 128), F32),
            pltpu.VMEM((sblocks, 128), F32),
            pltpu.VMEM((sblocks, 8, 128), F32),
            pltpu.VMEM((nsrc, 8, 128), F32),
            pltpu.VMEM((nsrc, share, width), F32),
            pltpu.VMEM((128, 128), F32),
            pltpu.VMEM((nsrc, 8, 128), F32),
            dma((rounds + 1, 8)),
            dma((2, rounds + 1)),
            dma((2, rounds + 1)),
            dma((rounds + 1, 4)),
            dma((2, nsrc)),
            dma((2, nsrc)),
            dma((2, nsrc)),
            dma((2, nsrc)),
        ],
        compiler_params=pltpu.CompilerParams(
            collective_id=0, has_side_effects=True, vmem_limit_bytes=60 * 1024 * 1024
        ),
    )(sources, targets, target_potential.reshape(1, count), active)
    return value.reshape(rows), image


def solution(mesh):
    return jax.shard_map(
        per_device,
        mesh=mesh,
        in_specs=(P("tgt", None), P(("src", "tgt"), None), P(("src", "tgt")), P("tgt", None)),
        out_specs=(P("tgt"), P("tgt", None)),
        check_vma=False,
    )
```

```python
import functools
import math

import jax
import jax.numpy as jnp
from jax import lax
from jax.experimental import pallas as pl
from jax.experimental.pallas import tpu as pltpu
from jax.sharding import PartitionSpec as P

MESH = pl.DeviceIdType.MESH
F32 = jnp.float32
BF16 = jnp.bfloat16
LOWEST = -1e38


def kernel(sizes, src_hbm, tgt_hbm, pot_hbm, act_hbm, val_ref, map_ref,
           src, pot, act, local, held, scores, weights, crossed, top, rescale, total, turned, pairtop, pairturned, numer, mask, norm, stat,
           gotstat, gotnum, factor, gotval, recv, send_z, send_x, pair_recv, pair_send, rs_recv, rs_send, ag_recv, ag_send):
    nsrc, ntgt, eps = sizes
    rows, width = src_hbm.shape
    piece = tgt_hbm.shape[0] // 2
    block = 128
    rounds = ntgt // 4
    nz = ntgt // 4
    share = rows // nsrc
    sblocks = rows // block
    blocks = 2 * sblocks
    to_two = math.log2(math.e)

    s = lax.axis_index("src")
    t = lax.axis_index("tgt")
    half = nsrc // 2
    x_hi, y = s // half, s % half
    z, x_lo, core = t // 4, (t // 2) % 2, t % 2
    up = (s, (t + 4) % ntgt)
    down = (s, (t + ntgt - 4) % ntgt)
    twin = (s, z * 4 + x_lo * 2 + 1 - core)
    side_a = (s, z * 4 + (1 - x_lo) * 2 + core)
    side_b = ((1 - x_hi) * half + y, z * 4 + (1 - x_lo) * 2 + core)
    others = [((s + d) % nsrc, t) for d in range(1, nsrc)]

    barrier = pltpu.get_barrier_semaphore()
    for device in [up, down, twin, side_a, side_b] + others:
        pl.semaphore_signal(barrier, inc=1, device_id=device, device_id_type=MESH)

    loads = [
        pltpu.make_async_copy(tgt_hbm.at[part * piece:(part + 1) * piece, :],
                              held.at[0, 1 - part, 0:piece, :], local.at[part])
        for part in range(2)
    ] + [
        pltpu.make_async_copy(pot_hbm, pot, local.at[2]),
        pltpu.make_async_copy(src_hbm, src.at[0:rows, :], local.at[3]),
        pltpu.make_async_copy(act_hbm, act.at[0], local.at[4]),
    ]
    for load in loads:
        load.start()

    def remote(source, target, ssem, rsem, device):
        return pltpu.make_async_remote_copy(
            src_ref=source, dst_ref=target, send_sem=ssem, recv_sem=rsem, device_id=device, device_id_type=MESH
        )

    def send_up(k, lane, to):
        return remote(held.at[k, lane], held.at[to, 0], send_z.at[0, to], recv.at[to, 0], up)

    def send_down(k, lane, to):
        return remote(held.at[k, lane], held.at[to, 1], send_z.at[1, to], recv.at[to, 1], down)

    def send_a(k, lane):
        return remote(held.at[k, lane], held.at[k, 2], send_x.at[0, k], recv.at[k, 2], side_a)

    def send_b(k, lane):
        return remote(held.at[k, lane], held.at[k, 3], send_x.at[1, k], recv.at[k, 3], side_b)

    share_sources = remote(src_hbm, src.at[rows:2 * rows, :], pair_send.at[0], pair_recv.at[0], twin)
    share_active = remote(act_hbm, act.at[1], pair_send.at[1], pair_recv.at[1], twin)

    def arrived(k, lane):
        remote(held.at[k, lane], held.at[k, lane], send_z.at[0, 0], recv.at[k, lane], up).wait_recv()

    ones = jnp.ones((8, width), BF16)
    across = (((1,), (1,)), ((), ()))

    def half_norms(block_rows):
        wide = block_rows.astype(F32)
        square = 0.5 * (wide * wide)
        high = square.astype(BF16)
        low = (square - high.astype(F32)).astype(BF16)
        return lax.dot_general(ones, high, across, preferred_element_type=F32) + lax.dot_general(
            ones, low, across, preferred_element_type=F32
        )

    own_row = lax.broadcasted_iota(jnp.int32, (8, piece), 0) == lax.broadcasted_iota(jnp.int32, (8, piece), 1) % 8
    chooser = jnp.where(
        lax.broadcasted_iota(jnp.int32, (piece, block), 0) // 8 == lax.broadcasted_iota(jnp.int32, (piece, block), 1),
        1.0, 0.0,
    ).astype(BF16)

    for part in range(2):
        loads[part].wait()
        if part == 0:
            loads[2].wait()
        data = held[0, 1 - part, 0:piece, :]
        shifted = (pot[0:1, part * piece:(part + 1) * piece] - half_norms(data)[0:1, :]) * (1.0 / eps)
        high = shifted.astype(BF16).astype(F32)
        middle = (shifted - high).astype(BF16).astype(F32)
        low = shifted - high - middle
        spread_out = [
            jnp.dot(jnp.where(own_row, jnp.broadcast_to(value, (8, piece)), 0.0).astype(BF16), chooser,
                    preferred_element_type=F32)
            for value in (high, middle, low)
        ]
        extra = jnp.concatenate([
            jnp.concatenate([spread_out[0], spread_out[1]], axis=1),
            jnp.concatenate([spread_out[2], jnp.zeros((8, block), F32)], axis=1),
        ], axis=0)
        held[0, 1 - part, piece:piece + 16, :] = extra.astype(BF16)

    pl.semaphore_wait(barrier, 5 + nsrc - 1)
    send_up(0, 1, 1).start()
    send_down(0, 0, 1).start()
    send_a(0, 1).start()
    send_b(0, 0).start()
    share_sources.start()
    share_active.start()
    send_up(0, 0, 2).start()
    send_down(0, 1, 2).start()

    loads[3].wait()
    loads[4].wait()

    for b in range(sblocks):
        norm[b:b + 1, :] = half_norms(src[b * block:(b + 1) * block, :])[0:1, :]

    slots = rounds * 4 * 2
    place = lax.broadcasted_iota(jnp.int32, (slots, block), 0)
    part_h, kind, k = place % 2, (place // 2) % 4, place // 8
    from_side = kind >= 2
    odd = k % 2
    distance = (k + 1) // 2
    below = jnp.where(kind == 0, 1, jnp.where(kind == 1, 0, jnp.where(kind == 2, odd, 1 - odd)))
    letter = jnp.where(kind == 0, 1 - odd, jnp.where(kind == 1, odd, kind - 2))
    z_from = (z + jnp.where(below == 1, nz - distance, distance)) % nz
    x_lo_from = jnp.where(from_side, 1 - x_lo, x_lo)
    x_hi_from = jnp.where(kind == 3, 1 - x_hi, x_hi)
    owner = (x_hi_from * half + y) * ntgt + z_from * 4 + x_lo_from * 2 + core
    number = owner * 4 + letter * 2 + part_h

    def set_mask(part):
        for b in range(sblocks):
            hit = jnp.zeros((slots, block), F32)
            for e in range(act.shape[2] // block):
                hit = jnp.where(number == act[part, b:b + 1, e * block:(e + 1) * block], 1.0, hit)
            mask[part * sblocks + b] = jnp.broadcast_to(jnp.max(hit, axis=1, keepdims=True), (slots, block))

    set_mask(0)
    top[...] = jnp.full(top.shape, LOWEST, F32)
    rescale[...] = jnp.ones(rescale.shape, F32)
    total[...] = jnp.zeros(total.shape, F32)
    turned[...] = jnp.zeros(turned.shape, F32)
    share_active.wait_recv()
    set_mask(1)
    share_sources.wait_recv()
    src[...] = (src[...].astype(F32) * (1.0 / eps)).astype(BF16)

    tile = scores.shape[2]
    per = block // 8

    def bit(k, lane, h, b):
        return mask[b, pl.ds((k * 4 + lane) * 2 + h, 1), :] > 0.5

    def score_piece(k, lane, n, maxima):
        product = lax.dot_general(
            held[k, lane, 0:piece, :], src[n * tile:(n + 1) * tile, :], across, preferred_element_type=F32
        )
        extra = held[k, lane, piece:piece + 16, :].astype(F32)
        shift = extra[0:8, 0:block] + extra[0:8, block:2 * block] + extra[8:16, 0:block]
        for h in range(piece // block):
            shifts = jnp.concatenate(
                [jnp.broadcast_to(shift[:, h * per + q:h * per + q + 1], (8, block)) for q in range(per)], axis=0
            )
            for c in range(tile // block):
                score = product[h * block:(h + 1) * block, c * block:(c + 1) * block] + shifts
                spot = lane * piece + h * block
                scores[n, spot:spot + block, c * block:(c + 1) * block] = score
                best = jnp.max(score.reshape(per, 8, block), axis=0)
                best = jnp.where(bit(k, lane, h, n * (tile // block) + c), best, LOWEST)
                maxima[c] = jnp.maximum(maxima[c], best)

    def weigh_piece(k, lane, n, tops, sums):
        for h in range(piece // block):
            for c in range(tile // block):
                spot = lane * piece + h * block
                against = jnp.where(bit(k, lane, h, n * (tile // block) + c), tops[c], -LOWEST)
                score = scores[n, spot:spot + block, c * block:(c + 1) * block]
                weight = jnp.exp2((score - against) * to_two)
                sums[c] = sums[c] + jnp.sum(weight.reshape(per, 8, block), axis=0)
                weights[n, spot:spot + block, c * block:(c + 1) * block] = weight.astype(BF16)

    def columns(n, c):
        return slice(n * tile + c * block, n * tile + (c + 1) * block)

    def absorb(fresh, ready):
        if ready is not None:
            for lane in range(4):
                crossed[:, lane * piece:(lane + 1) * piece] = held[ready, lane, 0:piece, :].T
        parts = range(tile // block)
        for n in range(2 * rows // tile):
            tops = [top[0:1, columns(n, c)] for c in parts]
            maxima = list(tops)
            scales = [rescale[0:1, columns(n, c)] for c in parts]
            sums = [total[:, columns(n, c)] * scales[c] for c in parts]
            added = None
            for lane in range(4):
                if ready is not None:
                    weigh_piece(ready, lane, n, tops, sums)
                if fresh is not None:
                    score_piece(fresh, lane, n, maxima)
                if ready is not None and lane % 2 == 1:
                    span = slice((lane - 1) * piece, (lane + 1) * piece)
                    term = jnp.dot(crossed[:, span], weights[n, span, :], preferred_element_type=F32)
                    added = term if added is None else added + term
            for c in parts:
                at = columns(n, c)
                if ready is not None:
                    total[:, at] = sums[c]
                    turned[:, at] = turned[:, at] * scales[c] + added[:, c * block:(c + 1) * block]
                if fresh is not None:
                    new = jnp.max(maxima[c], axis=0, keepdims=True)
                    rescale[0:1, at] = jnp.exp2((tops[c] - new) * to_two)
                    top[0:1, at] = new

    def pass_on(k):
        odd = k % 2
        for lane, onward in ((0, send_up), (1, send_down)):
            arrived(k, lane)

            @pl.when(k + 2 < rounds)
            def _():
                onward(k, lane, k + 2).start()
        send_a(k, 1 - odd).start()
        send_b(k, odd).start()

    def sides(k):
        for lane in (2, 3):
            arrived(k, lane)

    pass_on(jnp.int32(1))
    sides(0)
    absorb(0, None)

    def one_round(k, carry):
        pass_on(k)
        sides(k - 1)
        absorb(k - 1, k - 2)
        return carry

    lax.fori_loop(2, rounds, one_round, 0)
    absorb(None, rounds - 2)
    sides(rounds - 1)
    absorb(rounds - 1, None)
    absorb(None, rounds - 1)

    for b in range(blocks):
        at = slice(b * block, (b + 1) * block)
        total[0:1, at] = jnp.sum(total[:, at], axis=0, keepdims=True)
        top[1:2, at] = total[0:1, at]
    share_top = remote(top.at[:, rows:2 * rows], pairtop, pair_send.at[2], pair_recv.at[2], twin)
    share_turned = [
        remote(turned.at[:, (sblocks + b) * block:(sblocks + b + 1) * block], pairturned.at[b],
               pair_send.at[3 + b], pair_recv.at[3 + b], twin)
        for b in range(sblocks)
    ]
    share_top.start()
    for copy in share_turned:
        copy.start()
    share_top.wait_recv()

    for b in range(sblocks):
        at = slice(b * block, (b + 1) * block)
        best = jnp.maximum(top[0:1, at], pairtop[0:1, at])
        ours = jnp.exp2((top[0:1, at] - best) * to_two)
        theirs = jnp.exp2((pairtop[0:1, at] - best) * to_two)
        stat[b, 0:1, :] = best
        stat[b, 1:2, :] = top[1:2, at] * ours + pairtop[1:2, at] * theirs
        share_turned[b].wait_recv()
        numer[at, :] = (turned[:, at] * ours + pairturned[b] * theirs).T

    def give_stat(d):
        q = (s + d) % nsrc
        return remote(stat.at[q // 2], gotstat.at[d], rs_send.at[0, d], rs_recv.at[0, d], (q, t))

    def give_rows(d):
        q = (s + d) % nsrc
        return remote(numer.at[pl.ds(pl.multiple_of(q * share, share), share), :], gotnum.at[d],
                      rs_send.at[1, d], rs_recv.at[1, d], (q, t))

    for d in range(1, nsrc):
        give_stat(d).start()
        give_rows(d).start()
    gotstat[0] = stat[s // 2]
    mine = pl.ds(pl.multiple_of(s * share, share), share)
    for d in range(1, nsrc):
        give_stat(d).wait_recv()
    tops = jnp.concatenate([gotstat[d, 0:1, :] for d in range(nsrc)], axis=0)
    dens = jnp.concatenate([gotstat[d, 1:2, :] for d in range(nsrc)], axis=0)
    best = jnp.max(tops, axis=0, keepdims=True)
    scale = jnp.exp2((tops - best) * to_two)
    den = jnp.sum(scale * dens, axis=0, keepdims=True)
    value = norm[pl.ds(s // 2, 1), :] - eps * (best + jnp.log(den))
    gotval[s] = jnp.broadcast_to(value, (8, block))
    ratio = scale / den
    factor[...] = jnp.concatenate([ratio] + [jnp.zeros((block - nsrc, block), F32)], axis=0).T
    column = factor[pl.ds(pl.multiple_of((s % 2) * share, share), share), :]
    image = numer[mine, :] * column[:, 0:1]
    for d in range(1, nsrc):
        give_rows(d).wait_recv()
        image = image + gotnum[d] * column[:, d:d + 1]
    map_ref[mine, :] = image

    def spread(d):
        device = ((s + d) % nsrc, t)
        return (
            remote(gotval.at[s], gotval.at[s], ag_send.at[0, d], ag_recv.at[0, d], device),
            remote(map_ref.at[mine, :], map_ref.at[mine, :], ag_send.at[1, d], ag_recv.at[1, d], device),
        )

    def gathered(d):
        q = (s + nsrc - d) % nsrc
        device = ((s + d) % nsrc, t)
        theirs = pl.ds(pl.multiple_of(q * share, share), share)
        return (
            remote(gotval.at[q], gotval.at[q], ag_send.at[0, d], ag_recv.at[0, d], device),
            remote(map_ref.at[theirs, :], map_ref.at[theirs, :], ag_send.at[1, d], ag_recv.at[1, d], device),
        )

    for d in range(1, nsrc):
        for copy in spread(d):
            copy.start()

    for to in (1, 2):
        send_up(0, 0, to).wait_send()
        send_down(0, 0, to).wait_send()

    def drain(k, carry):
        @pl.when(k + 2 < rounds)
        def _():
            send_up(k, 0, k + 2).wait_send()
            send_down(k, 1, k + 2).wait_send()
        send_a(k, 0).wait_send()
        send_b(k, 0).wait_send()
        return carry

    lax.fori_loop(1, rounds, drain, 0)
    send_a(0, 0).wait_send()
    send_b(0, 0).wait_send()
    for copy in [share_sources, share_active, share_top] + share_turned:
        copy.wait_send()
    for d in range(1, nsrc):
        give_stat(d).wait_send()
        give_rows(d).wait_send()
    for d in range(1, nsrc):
        for copy in gathered(d):
            copy.wait_recv()
        for copy in spread(d):
            copy.wait_send()
    lane = lax.broadcasted_iota(jnp.int32, (1, block), 1)
    for b in range(sblocks):
        val_ref[b:b + 1, :] = jnp.where(lane < share, gotval[2 * b, 0:1, :], gotval[2 * b + 1, 0:1, :])


def per_device(sources, targets, target_potential, active):
    rows, width = sources.shape
    count = targets.shape[0]
    nsrc, ntgt = lax.axis_size("src"), lax.axis_size("tgt")
    eps = 0.5 * math.sqrt(width)
    piece = count // 2
    rounds = ntgt // 4
    share = rows // nsrc
    sblocks = rows // 128
    dma = pltpu.SemaphoreType.DMA
    vmem = pl.BlockSpec(memory_space=pltpu.VMEM)
    value, image = pl.pallas_call(
        functools.partial(kernel, (nsrc, ntgt, eps)),
        out_shape=(
            jax.ShapeDtypeStruct((sblocks, 128), F32),
            jax.ShapeDtypeStruct((rows, width), F32),
        ),
        in_specs=[pl.BlockSpec(memory_space=pltpu.HBM)] * 4,
        out_specs=(vmem, vmem),
        scratch_shapes=[
            pltpu.VMEM((2 * rows, width), BF16),
            pltpu.VMEM((1, count), F32),
            pltpu.VMEM((2,) + active.shape, jnp.int32),
            dma((5,)),
            pltpu.VMEM((rounds, 4, piece + 16, width), BF16),
            pltpu.VMEM((2 * rows // 256, 4 * piece, 256), F32),
            pltpu.VMEM((2 * rows // 256, 4 * piece, 256), BF16),
            pltpu.VMEM((width, 4 * piece), BF16),
            pltpu.VMEM((8, 2 * rows), F32),
            pltpu.VMEM((8, 2 * rows), F32),
            pltpu.VMEM((8, 2 * rows), F32),
            pltpu.VMEM((width, 2 * rows), F32),
            pltpu.VMEM((8, rows), F32),
            pltpu.VMEM((sblocks, width, 128), F32),
            pltpu.VMEM((rows, width), F32),
            pltpu.VMEM((2 * sblocks, rounds * 8, 128), F32),
            pltpu.VMEM((sblocks, 128), F32),
            pltpu.VMEM((sblocks, 8, 128), F32),
            pltpu.VMEM((nsrc, 8, 128), F32),
            pltpu.VMEM((nsrc, share, width), F32),
            pltpu.VMEM((128, 128), F32),
            pltpu.VMEM((nsrc, 8, 128), F32),
            dma((rounds, 4)),
            dma((2, rounds)),
            dma((2, rounds)),
            dma((3 + sblocks,)),
            dma((3 + sblocks,)),
            dma((2, nsrc)),
            dma((2, nsrc)),
            dma((2, nsrc)),
            dma((2, nsrc)),
        ],
        compiler_params=pltpu.CompilerParams(
            collective_id=0, has_side_effects=True, vmem_limit_bytes=56 * 1024 * 1024
        ),
    )(sources, targets, target_potential.reshape(1, count), active)
    return value.reshape(rows), image


def solution(mesh):
    return jax.shard_map(
        per_device,
        mesh=mesh,
        in_specs=(P("tgt", None), P(("src", "tgt"), None), P(("src", "tgt")), P("tgt", None)),
        out_specs=(P("tgt"), P("tgt", None)),
        check_vma=False,
    )
```

```python
import functools
import math

import jax
import jax.numpy as jnp
from jax import lax
from jax.experimental import pallas as pl
from jax.experimental.pallas import tpu as pltpu
from jax.sharding import PartitionSpec as P

MESH = pl.DeviceIdType.MESH
F32 = jnp.float32
BF16 = jnp.bfloat16
LOWEST = -1e38


def kernel(sizes, src_hbm, tgt_hbm, pot_hbm, act_hbm, code_ref, note_ref,
           src, pot, act, local, held, scores, weights, crossed, top, rescale, total, turned, pairtop, pairturned, coded, mask, norm, stat,
           gotstat, gotnum, factor, recv, send_z, send_x, pair_recv, pair_send, rs_recv, rs_send, ag_recv, ag_send):
    nsrc, ntgt, eps = sizes
    rows, width = src_hbm.shape
    piece = tgt_hbm.shape[0] // 2
    block = 128
    rounds = ntgt // 4
    nz = ntgt // 4
    share = rows // nsrc
    sblocks = rows // block
    blocks = 2 * sblocks
    to_two = math.log2(math.e)

    s = lax.axis_index("src")
    t = lax.axis_index("tgt")
    half = nsrc // 2
    x_hi, y = s // half, s % half
    z, x_lo, core = t // 4, (t // 2) % 2, t % 2
    up = (s, (t + 4) % ntgt)
    down = (s, (t + ntgt - 4) % ntgt)
    twin = (s, z * 4 + x_lo * 2 + 1 - core)
    side_a = (s, z * 4 + (1 - x_lo) * 2 + core)
    side_b = ((1 - x_hi) * half + y, z * 4 + (1 - x_lo) * 2 + core)
    others = [((s + d) % nsrc, t) for d in range(1, nsrc)]

    barrier = pltpu.get_barrier_semaphore()
    for device in [up, down, twin, side_a, side_b] + others:
        pl.semaphore_signal(barrier, inc=1, device_id=device, device_id_type=MESH)

    loads = [
        pltpu.make_async_copy(tgt_hbm.at[part * piece + h * block:part * piece + (h + 1) * block, :],
                              held.at[0, 1 - part, h * (block + 16):h * (block + 16) + block, :], local.at[part, h])
        for part in range(2) for h in range(2)
    ] + [
        pltpu.make_async_copy(pot_hbm, pot, local.at[2, 0]),
        pltpu.make_async_copy(src_hbm, src.at[0:rows, :], local.at[2, 1]),
        pltpu.make_async_copy(act_hbm, act.at[0], local.at[3, 0]),
    ]
    for load in loads:
        load.start()

    def remote(source, target, ssem, rsem, device):
        return pltpu.make_async_remote_copy(
            src_ref=source, dst_ref=target, send_sem=ssem, recv_sem=rsem, device_id=device, device_id_type=MESH
        )

    parts_of = (slice(0, block + 16), slice(block + 16, 2 * block + 16))

    def send_up(k, lane, to, g):
        return remote(held.at[k, lane, parts_of[g], :], held.at[to, 0, parts_of[g], :],
                      send_z.at[0, to, g], recv.at[to, 0, g], up)

    def send_down(k, lane, to, g):
        return remote(held.at[k, lane, parts_of[g], :], held.at[to, 1, parts_of[g], :],
                      send_z.at[1, to, g], recv.at[to, 1, g], down)

    def send_a(k, lane, g):
        return remote(held.at[k, lane, parts_of[g], :], held.at[k, 2, parts_of[g], :],
                      send_x.at[0, k, g], recv.at[k, 2, g], side_a)

    def send_b(k, lane, g):
        return remote(held.at[k, lane, parts_of[g], :], held.at[k, 3, parts_of[g], :],
                      send_x.at[1, k, g], recv.at[k, 3, g], side_b)

    share_sources = remote(src_hbm, src.at[rows:2 * rows, :], pair_send.at[0, 0], pair_recv.at[0, 0], twin)
    share_active = remote(act_hbm, act.at[1], pair_send.at[1, 0], pair_recv.at[1, 0], twin)

    def arrived(k, lane, g):
        here = held.at[k, lane, parts_of[g], :]
        remote(here, here, send_z.at[0, 0, g], recv.at[k, lane, g], up).wait_recv()

    def points(k, lane):
        return jnp.concatenate([held[k, lane, 0:block, :], held[k, lane, block + 16:2 * block + 16, :]], axis=0)

    ones = jnp.ones((8, width), BF16)
    across = (((1,), (1,)), ((), ()))

    def half_norms(block_rows):
        wide = block_rows.astype(F32)
        square = 0.5 * (wide * wide)
        high = square.astype(BF16)
        low = (square - high.astype(F32)).astype(BF16)
        return lax.dot_general(ones, high, across, preferred_element_type=F32) + lax.dot_general(
            ones, low, across, preferred_element_type=F32
        )

    own_row = lax.broadcasted_iota(jnp.int32, (8, piece), 0) == lax.broadcasted_iota(jnp.int32, (8, piece), 1) % 8
    chooser = jnp.where(
        lax.broadcasted_iota(jnp.int32, (piece, block), 0) // 8 == lax.broadcasted_iota(jnp.int32, (piece, block), 1),
        1.0, 0.0,
    ).astype(BF16)

    for part in range(2):
        loads[2 * part].wait()
        loads[2 * part + 1].wait()
        if part == 0:
            loads[4].wait()
        data = points(0, 1 - part)
        shifted = (pot[0:1, part * piece:(part + 1) * piece] - half_norms(data)[0:1, :]) * (1.0 / eps)
        high = shifted.astype(BF16).astype(F32)
        middle = (shifted - high).astype(BF16).astype(F32)
        low = shifted - high - middle
        spread_out = [
            jnp.dot(jnp.where(own_row, jnp.broadcast_to(value, (8, piece)), 0.0).astype(BF16), chooser,
                    preferred_element_type=F32)
            for value in (high, middle, low)
        ]
        extra = jnp.concatenate([
            jnp.concatenate([spread_out[0], spread_out[1]], axis=1),
            jnp.concatenate([spread_out[2], jnp.zeros((8, block), F32)], axis=1),
        ], axis=0)
        held[0, 1 - part, block:block + 16, :] = extra.astype(BF16)

    pl.semaphore_wait(barrier, 5 + nsrc - 1)
    for g in range(2):
        send_up(0, 1, 1, g).start()
        send_down(0, 0, 1, g).start()
        send_a(0, 1, g).start()
        send_b(0, 0, g).start()
    share_sources.start()
    share_active.start()
    for g in range(2):
        send_up(0, 0, 2, g).start()
        send_down(0, 1, 2, g).start()

    loads[5].wait()
    loads[6].wait()

    for b in range(sblocks):
        norm[b:b + 1, :] = half_norms(src[b * block:(b + 1) * block, :])[0:1, :]

    slots = rounds * 4 * 2
    place = lax.broadcasted_iota(jnp.int32, (slots, block), 0)
    part_h, kind, k = place % 2, (place // 2) % 4, place // 8
    from_side = kind >= 2
    odd = k % 2
    distance = (k + 1) // 2
    below = jnp.where(kind == 0, 1, jnp.where(kind == 1, 0, jnp.where(kind == 2, odd, 1 - odd)))
    letter = jnp.where(kind == 0, 1 - odd, jnp.where(kind == 1, odd, kind - 2))
    z_from = (z + jnp.where(below == 1, nz - distance, distance)) % nz
    x_lo_from = jnp.where(from_side, 1 - x_lo, x_lo)
    x_hi_from = jnp.where(kind == 3, 1 - x_hi, x_hi)
    owner = (x_hi_from * half + y) * ntgt + z_from * 4 + x_lo_from * 2 + core
    number = owner * 4 + letter * 2 + part_h

    def set_mask(part):
        for b in range(sblocks):
            hit = jnp.zeros((slots, block), F32)
            for e in range(act.shape[2] // block):
                hit = jnp.where(number == act[part, b:b + 1, e * block:(e + 1) * block], 1.0, hit)
            mask[part * sblocks + b] = jnp.broadcast_to(jnp.max(hit, axis=1, keepdims=True), (slots, block))

    set_mask(0)
    top[...] = jnp.full(top.shape, LOWEST, F32)
    rescale[...] = jnp.ones(rescale.shape, F32)
    total[...] = jnp.zeros(total.shape, F32)
    turned[...] = jnp.zeros(turned.shape, F32)
    share_active.wait_recv()
    set_mask(1)
    share_sources.wait_recv()
    src[...] = (src[...].astype(F32) * (1.0 / eps)).astype(BF16)

    tile = scores.shape[2]
    per = block // 8

    def bit(k, lane, h, b):
        return mask[b, pl.ds((k * 4 + lane) * 2 + h, 1), :] > 0.5

    def score_piece(k, lane, n, maxima):
        product = lax.dot_general(
            points(k, lane), src[n * tile:(n + 1) * tile, :], across, preferred_element_type=F32
        )
        extra = held[k, lane, block:block + 16, :].astype(F32)
        shift = extra[0:8, 0:block] + extra[0:8, block:2 * block] + extra[8:16, 0:block]
        for h in range(piece // block):
            shifts = jnp.concatenate(
                [jnp.broadcast_to(shift[:, h * per + q:h * per + q + 1], (8, block)) for q in range(per)], axis=0
            )
            for c in range(tile // block):
                score = product[h * block:(h + 1) * block, c * block:(c + 1) * block] + shifts
                spot = lane * piece + h * block
                scores[n, spot:spot + block, c * block:(c + 1) * block] = score
                best = jnp.max(score.reshape(per, 8, block), axis=0)
                best = jnp.where(bit(k, lane, h, n * (tile // block) + c), best, LOWEST)
                maxima[c] = jnp.maximum(maxima[c], best)

    def weigh_piece(k, lane, n, tops, sums):
        for h in range(piece // block):
            for c in range(tile // block):
                spot = lane * piece + h * block
                against = jnp.where(bit(k, lane, h, n * (tile // block) + c), tops[c], -LOWEST)
                score = scores[n, spot:spot + block, c * block:(c + 1) * block]
                weight = jnp.exp2((score - against) * to_two)
                sums[c] = sums[c] + jnp.sum(weight.reshape(per, 8, block), axis=0)
                weights[n, spot:spot + block, c * block:(c + 1) * block] = weight.astype(BF16)

    def columns(n, c):
        return slice(n * tile + c * block, n * tile + (c + 1) * block)

    def absorb(fresh, ready, tick=None, fresh_lanes=(0, 1, 2, 3), ready_lanes=(0, 1, 2, 3), order=(0, 1, 2, 3), after=None):
        if ready is not None:
            for lane in ready_lanes:
                crossed[:, lane * piece:(lane + 1) * piece] = points(ready, lane).T
        parts = range(tile // block)
        for n in order:
            if tick is not None:
                tick(n)
            tops = [top[0:1, columns(n, c)] for c in parts]
            maxima = list(tops)
            scales = [rescale[0:1, columns(n, c)] for c in parts]
            sums = [total[:, columns(n, c)] * scales[c] for c in parts]
            added = None
            for lane in range(4):
                if ready is not None and lane in ready_lanes:
                    weigh_piece(ready, lane, n, tops, sums)
                if fresh is not None and lane in fresh_lanes:
                    score_piece(fresh, lane, n, maxima)
                if ready is not None and lane in ready_lanes and lane % 2 == 1:
                    span = slice((lane - 1) * piece, (lane + 1) * piece)
                    term = jnp.dot(crossed[:, span], weights[n, span, :], preferred_element_type=F32)
                    added = term if added is None else added + term
            for c in parts:
                at = columns(n, c)
                if ready is not None:
                    total[:, at] = sums[c]
                    turned[:, at] = turned[:, at] * scales[c] + added[:, c * block:(c + 1) * block]
                if fresh is not None:
                    new = jnp.max(maxima[c], axis=0, keepdims=True)
                    rescale[0:1, at] = jnp.exp2((tops[c] - new) * to_two)
                    top[0:1, at] = new
            if after is not None:
                after(n)

    def pass_on(k, lane, g):
        onward = (send_up, send_down)[lane]
        arrived(k, lane, g)

        @pl.when(k + 2 < rounds)
        def _():
            onward(k, lane, k + 2, g).start()

        @pl.when(k % 2 == 1 - lane)
        def _():
            send_a(k, lane, g).start()

        @pl.when(k % 2 == lane)
        def _():
            send_b(k, lane, g).start()

    def sides(k):
        for lane in (2, 3):
            for g in range(2):
                arrived(k, lane, g)

    def tick_of(k):
        def tick(n):
            if n % 2 == 0:
                for lane in range(2):
                    pass_on(k, lane, n // 2)
        return tick

    for g in range(2):
        for lane in range(2):
            pass_on(jnp.int32(1), lane, g)
    sides(0)
    absorb(0, None, tick_of(jnp.int32(2)))

    def one_round(k, carry):
        sides(k - 2)
        absorb(k - 2, k - 3, tick_of(k))
        return carry

    lax.fori_loop(3, rounds, one_round, 0)
    sides(rounds - 2)
    absorb(rounds - 2, rounds - 3)
    absorb(rounds - 1, rounds - 2, fresh_lanes=(0, 1))
    absorb(None, rounds - 1, ready_lanes=(0, 1))
    sides(rounds - 1)
    absorb(rounds - 1, None, fresh_lanes=(2, 3))

    def pair_copies(i):
        at = slice(rows + i * tile, rows + (i + 1) * tile)
        return (
            remote(top.at[:, at], pairtop.at[i], pair_send.at[2, i], pair_recv.at[2, i], twin),
            remote(turned.at[:, at], pairturned.at[i], pair_send.at[3, i], pair_recv.at[3, i], twin),
        )

    def share_of(q):
        return pl.ds(pl.multiple_of(q * share, share), share)

    def give_stat(q, d):
        return remote(stat.at[q // 2], gotstat.at[d], rs_send.at[0, d], rs_recv.at[0, d], (q, t))

    def give_rows(q, d):
        return remote(coded.at[share_of(q), :], gotnum.at[d], rs_send.at[1, d], rs_recv.at[1, d], (q, t))

    def merge(b):
        i, inside = b // (tile // block), slice(b % (tile // block) * block, (b % (tile // block) + 1) * block)
        at = slice(b * block, (b + 1) * block)
        best = jnp.maximum(top[0:1, at], pairtop[i, 0:1, inside])
        ours = jnp.exp2((top[0:1, at] - best) * to_two)
        theirs = jnp.exp2((pairtop[i, 0:1, inside] - best) * to_two)
        both = turned[:, at] * ours + pairturned[i, :, inside] * theirs
        largest = jnp.maximum(jnp.max(jnp.abs(both), axis=0, keepdims=True), 2e-38)
        stat[b, 0:1, :] = best
        stat[b, 1:2, :] = top[1:2, at] * ours + pairtop[i, 1:2, inside] * theirs
        stat[b, 2:3, :] = largest
        coded[at, :] = jnp.round((both * (1.0 / largest) * 32767.0).T).astype(jnp.int32).astype(jnp.int16)
        for q in (2 * b, 2 * b + 1):
            d = (q - s + nsrc) % nsrc

            @pl.when(q != s)
            def _():
                give_stat(q, d).start()
                give_rows(q, d).start()

    def after(n):
        for c in range(tile // block):
            at = columns(n, c)
            top[1:2, at] = jnp.sum(total[:, at], axis=0, keepdims=True)
        own = rows // tile
        if n >= own:
            for copy in pair_copies(n - own):
                copy.start()
        else:
            for copy in pair_copies(n):
                copy.wait_recv()
            for c in range(tile // block):
                merge(n * (tile // block) + c)

    absorb(None, rounds - 1, ready_lanes=(2, 3), order=(2, 3, 0, 1), after=after)

    gotstat[0] = stat[s // 2]
    mine = share_of(s)
    for d in range(1, nsrc):
        give_stat((s + d) % nsrc, d).wait_recv()
    tops = jnp.concatenate([gotstat[d, 0:1, :] for d in range(nsrc)], axis=0)
    dens = jnp.concatenate([gotstat[d, 1:2, :] for d in range(nsrc)], axis=0)
    sizes_of = jnp.concatenate([gotstat[d, 2:3, :] for d in range(nsrc)], axis=0)
    best = jnp.max(tops, axis=0, keepdims=True)
    scale = jnp.exp2((tops - best) * to_two)
    den = jnp.sum(scale * dens, axis=0, keepdims=True)
    value = norm[pl.ds(s // 2, 1), :] - eps * (best + jnp.log(den))
    ratio = scale / den * sizes_of
    bound = jnp.maximum(jnp.sum(ratio, axis=0, keepdims=True), 2e-38)
    note_ref[s] = jnp.concatenate([value, bound, jnp.zeros((6, block), F32)], axis=0)
    factor[...] = jnp.concatenate(
        [ratio, 1.0 / bound, jnp.zeros((block - nsrc - 1, block), F32)], axis=0
    ).T

    def spread_note(d):
        return remote(note_ref.at[s], note_ref.at[s], ag_send.at[0, d], ag_recv.at[0, d], ((s + d) % nsrc, t))

    def spread_rows(d):
        return remote(code_ref.at[mine, :], code_ref.at[mine, :], ag_send.at[1, d], ag_recv.at[1, d],
                      ((s + d) % nsrc, t))

    for d in range(1, nsrc):
        spread_note(d).start()
    column = factor[pl.ds(pl.multiple_of((s % 2) * share, share), share), :]

    def decoded(codes):
        return codes.astype(jnp.int32).astype(F32) * (1.0 / 32767.0)

    image = decoded(coded[mine, :]) * column[:, 0:1]
    for d in range(1, nsrc):
        give_rows((s + d) % nsrc, d).wait_recv()
        image = image + decoded(gotnum[d]) * column[:, d:d + 1]
    code_ref[mine, :] = jnp.round(image * column[:, nsrc:nsrc + 1] * 32767.0).astype(jnp.int32).astype(jnp.int16)

    for d in range(1, nsrc):
        spread_rows(d).start()

    for g in range(2):
        for to in (1, 2):
            send_up(0, 0, to, g).wait_send()
            send_down(0, 0, to, g).wait_send()
        send_a(0, 1, g).wait_send()
        send_b(0, 0, g).wait_send()

    def drain(k, carry):
        for g in range(2):
            @pl.when(k + 2 < rounds)
            def _():
                send_up(k, 0, k + 2, g).wait_send()
                send_down(k, 1, k + 2, g).wait_send()
            send_a(k, 0, g).wait_send()
            send_b(k, 0, g).wait_send()
        return carry

    lax.fori_loop(1, rounds, drain, 0)
    for copy in (share_sources, share_active) + pair_copies(0) + pair_copies(1):
        copy.wait_send()
    for d in range(1, nsrc):
        give_stat((s + d) % nsrc, d).wait_send()
        give_rows((s + d) % nsrc, d).wait_send()
    for d in range(1, nsrc):
        q = (s + nsrc - d) % nsrc
        remote(note_ref.at[q], note_ref.at[q], ag_send.at[0, d], ag_recv.at[0, d], (q, t)).wait_recv()
        remote(code_ref.at[share_of(q), :], code_ref.at[share_of(q), :], ag_send.at[1, d], ag_recv.at[1, d],
               (q, t)).wait_recv()
        spread_note(d).wait_send()
        spread_rows(d).wait_send()


def decode(share, code_ref, note_ref, val_ref, map_ref):
    block = 128
    lane = lax.broadcasted_iota(jnp.int32, (1, block), 1)
    blocks = range(val_ref.shape[0])
    bounds = []
    for b in blocks:
        first, second = note_ref[2 * b], note_ref[2 * b + 1]
        val_ref[b:b + 1, :] = jnp.where(lane < share, first[0:1, :], second[0:1, :])
        bounds.append(jnp.where(lane < share, first[1:2, :], second[1:2, :]))
    column = jnp.concatenate(bounds + [jnp.zeros((block - len(bounds), block), F32)], axis=0).T
    for b in blocks:
        at = slice(b * block, (b + 1) * block)
        map_ref[at, :] = code_ref[at, :].astype(jnp.int32).astype(F32) * (1.0 / 32767.0) * column[:, b:b + 1]


def per_device(sources, targets, target_potential, active):
    rows, width = sources.shape
    count = targets.shape[0]
    nsrc, ntgt = lax.axis_size("src"), lax.axis_size("tgt")
    eps = 0.5 * math.sqrt(width)
    piece = count // 2
    rounds = ntgt // 4
    share = rows // nsrc
    sblocks = rows // 128
    dma = pltpu.SemaphoreType.DMA
    vmem = pl.BlockSpec(memory_space=pltpu.VMEM)
    codes, notes = pl.pallas_call(
        functools.partial(kernel, (nsrc, ntgt, eps)),
        out_shape=(
            jax.ShapeDtypeStruct((rows, width), jnp.int16),
            jax.ShapeDtypeStruct((nsrc, 8, 128), F32),
        ),
        in_specs=[pl.BlockSpec(memory_space=pltpu.HBM)] * 4,
        out_specs=(vmem, vmem),
        scratch_shapes=[
            pltpu.VMEM((2 * rows, width), BF16),
            pltpu.VMEM((1, count), F32),
            pltpu.VMEM((2,) + active.shape, jnp.int32),
            dma((4, 2)),
            pltpu.VMEM((rounds, 4, piece + 16, width), BF16),
            pltpu.VMEM((2 * rows // 256, 4 * piece, 256), F32),
            pltpu.VMEM((2 * rows // 256, 4 * piece, 256), BF16),
            pltpu.VMEM((width, 4 * piece), BF16),
            pltpu.VMEM((8, 2 * rows), F32),
            pltpu.VMEM((8, 2 * rows), F32),
            pltpu.VMEM((8, 2 * rows), F32),
            pltpu.VMEM((width, 2 * rows), F32),
            pltpu.VMEM((rows // 256, 8, 256), F32),
            pltpu.VMEM((rows // 256, width, 256), F32),
            pltpu.VMEM((rows, width), jnp.int16),
            pltpu.VMEM((2 * sblocks, rounds * 8, 128), F32),
            pltpu.VMEM((sblocks, 128), F32),
            pltpu.VMEM((sblocks, 8, 128), F32),
            pltpu.VMEM((nsrc, 8, 128), F32),
            pltpu.VMEM((nsrc, share, width), jnp.int16),
            pltpu.VMEM((128, 128), F32),
            dma((rounds, 4, 2)),
            dma((2, rounds, 2)),
            dma((2, rounds, 2)),
            dma((4, 2)),
            dma((4, 2)),
            dma((2, nsrc)),
            dma((2, nsrc)),
            dma((2, nsrc)),
            dma((2, nsrc)),
        ],
        compiler_params=pltpu.CompilerParams(
            collective_id=0, has_side_effects=True, vmem_limit_bytes=56 * 1024 * 1024
        ),
    )(sources, targets, target_potential.reshape(1, count), active)
    value, image = pl.pallas_call(
        functools.partial(decode, share),
        out_shape=(
            jax.ShapeDtypeStruct((sblocks, 128), F32),
            jax.ShapeDtypeStruct((rows, width), F32),
        ),
        compiler_params=pltpu.CompilerParams(vmem_limit_bytes=60 * 1024 * 1024),
    )(codes, notes)
    return value.reshape(rows), image


def solution(mesh):
    return jax.shard_map(
        per_device,
        mesh=mesh,
        in_specs=(P("tgt", None), P(("src", "tgt"), None), P(("src", "tgt")), P("tgt", None)),
        out_specs=(P("tgt"), P("tgt", None)),
        check_vma=False,
    )
```

```python
import functools
import math

import jax
import jax.numpy as jnp
from jax import lax
from jax.experimental import pallas as pl
from jax.experimental.pallas import tpu as pltpu
from jax.sharding import PartitionSpec as P

MESH = pl.DeviceIdType.MESH
F32 = jnp.float32
BF16 = jnp.bfloat16
LOWEST = -1e38


def kernel(sizes, src_hbm, tgt_hbm, pot_hbm, act_hbm, code_ref, note_ref,
           src, pot, act, local, held, scores, weights, crossed, top, rescale, total, turned, pairtop, pairturned, coded, mask, norm, stat,
           gotstat, gotnum, factor, recv, send_z, pair_recv, pair_send, end_recv, end_send, rs_recv, rs_send, ag_recv, ag_send):
    nsrc, ntgt, eps = sizes
    rows, width = src_hbm.shape
    piece = tgt_hbm.shape[0] // 2
    block = 128
    rounds = ntgt // 4
    nz = ntgt // 4
    share = rows // nsrc
    sblocks = rows // block
    parts = 4
    to_two = math.log2(math.e)

    s = lax.axis_index("src")
    t = lax.axis_index("tgt")
    half = nsrc // 2
    x_hi, y = s // half, s % half
    z, x_lo, core = t // 4, (t // 2) % 2, t % 2
    up = (s, (t + 4) % ntgt)
    down = (s, (t + ntgt - 4) % ntgt)
    twin = (s, z * 4 + x_lo * 2 + 1 - core)
    side_a = (s, z * 4 + (1 - x_lo) * 2 + core)
    side_b = ((1 - x_hi) * half + y, z * 4 + (1 - x_lo) * 2 + core)
    t_side = z * 4 + (1 - x_lo) * 2 + core
    others = [((s + d) % nsrc, t) for d in range(1, nsrc)] + [((s + d) % nsrc, t_side) for d in range(nsrc)]

    barrier = pltpu.get_barrier_semaphore()
    for device in [up, down, twin] + others:
        pl.semaphore_signal(barrier, inc=1, device_id=device, device_id_type=MESH)

    loads = [
        pltpu.make_async_copy(tgt_hbm.at[part * piece + h * block:part * piece + (h + 1) * block, :],
                              held.at[0, 1 - part, h * (block + 16):h * (block + 16) + block, :], local.at[part, h])
        for part in range(2) for h in range(2)
    ] + [
        pltpu.make_async_copy(pot_hbm, pot, local.at[2, 0]),
        pltpu.make_async_copy(src_hbm, src.at[0:rows, :], local.at[2, 1]),
        pltpu.make_async_copy(act_hbm, act.at[0], local.at[3, 0]),
    ]
    for load in loads:
        load.start()

    def remote(source, target, ssem, rsem, device):
        return pltpu.make_async_remote_copy(
            src_ref=source, dst_ref=target, send_sem=ssem, recv_sem=rsem, device_id=device, device_id_type=MESH
        )

    parts_of = (slice(0, block + 16), slice(block + 16, 2 * block + 16))

    def send_up(k, lane, to, g):
        return remote(held.at[k, lane, parts_of[g], :], held.at[to, 0, parts_of[g], :],
                      send_z.at[0, to, g], recv.at[to, 0, g], up)

    def send_down(k, lane, to, g):
        return remote(held.at[k, lane, parts_of[g], :], held.at[to, 1, parts_of[g], :],
                      send_z.at[1, to, g], recv.at[to, 1, g], down)

    def part_rows(part, g):
        return src.at[part * rows + g * (rows // 2):part * rows + (g + 1) * (rows // 2), :]

    def share_sources(part, g):
        device = (twin, (side_a, side_b)[g], twin)[part - 1]
        return remote(part_rows(2 if part == 3 else 0, g), part_rows(part, g),
                      pair_send.at[part, g], pair_recv.at[part, g], device)

    def share_active(part):
        device = (twin, side_a, twin)[part - 1]
        return remote(act.at[2 if part == 3 else 0], act.at[part], pair_send.at[part, 2], pair_recv.at[part, 2], device)

    def arrived(k, lane, g):
        here = held.at[k, lane, parts_of[g], :]
        remote(here, here, send_z.at[0, 0, g], recv.at[k, lane, g], up).wait_recv()

    def points(k, lane):
        return jnp.concatenate([held[k, lane, 0:block, :], held[k, lane, block + 16:2 * block + 16, :]], axis=0)

    ones = jnp.ones((8, width), BF16)
    across = (((1,), (1,)), ((), ()))

    def half_norms(block_rows):
        wide = block_rows.astype(F32)
        square = 0.5 * (wide * wide)
        high = square.astype(BF16)
        low = (square - high.astype(F32)).astype(BF16)
        return lax.dot_general(ones, high, across, preferred_element_type=F32) + lax.dot_general(
            ones, low, across, preferred_element_type=F32
        )

    own_row = lax.broadcasted_iota(jnp.int32, (8, piece), 0) == lax.broadcasted_iota(jnp.int32, (8, piece), 1) % 8
    chooser = jnp.where(
        lax.broadcasted_iota(jnp.int32, (piece, block), 0) // 8 == lax.broadcasted_iota(jnp.int32, (piece, block), 1),
        1.0, 0.0,
    ).astype(BF16)

    for part in range(2):
        loads[2 * part].wait()
        loads[2 * part + 1].wait()
        if part == 0:
            loads[4].wait()
        data = points(0, 1 - part)
        shifted = (pot[0:1, part * piece:(part + 1) * piece] - half_norms(data)[0:1, :]) * (1.0 / eps)
        high = shifted.astype(BF16).astype(F32)
        middle = (shifted - high).astype(BF16).astype(F32)
        low = shifted - high - middle
        spread_out = [
            jnp.dot(jnp.where(own_row, jnp.broadcast_to(value, (8, piece)), 0.0).astype(BF16), chooser,
                    preferred_element_type=F32)
            for value in (high, middle, low)
        ]
        extra = jnp.concatenate([
            jnp.concatenate([spread_out[0], spread_out[1]], axis=1),
            jnp.concatenate([spread_out[2], jnp.zeros((8, block), F32)], axis=1),
        ], axis=0)
        held[0, 1 - part, block:block + 16, :] = extra.astype(BF16)

    loads[5].wait()
    loads[6].wait()
    for b in range(sblocks):
        norm[b:b + 1, :] = half_norms(src[b * block:(b + 1) * block, :])[0:1, :]
    src[0:rows, :] = (src[0:rows, :].astype(F32) * (1.0 / eps)).astype(BF16)

    pl.semaphore_wait(barrier, 3 + 2 * nsrc - 1)
    for g in range(2):
        send_up(0, 1, 1, g).start()
        send_down(0, 0, 1, g).start()
    for g in range(2):
        share_sources(2, g).start()
    share_active(2).start()
    share_active(1).start()
    for g in range(2):
        share_sources(1, g).start()
        send_up(0, 0, 2, g).start()
        send_down(0, 1, 2, g).start()

    slots = rounds * 2 * 2
    place = lax.broadcasted_iota(jnp.int32, (slots, block), 0)
    part_h, kind, k = place % 2, (place // 2) % 2, place // 4
    odd = k % 2
    distance = (k + 1) // 2
    letter = jnp.where(kind == 0, 1 - odd, odd)
    z_from = (z + jnp.where(kind == 0, nz - distance, distance)) % nz
    owner = (x_hi * half + y) * ntgt + z_from * 4 + x_lo * 2 + core
    number = owner * 4 + letter * 2 + part_h

    def set_mask(part):
        for b in range(sblocks):
            hit = jnp.zeros((slots, block), F32)
            for e in range(act.shape[2] // block):
                hit = jnp.where(number == act[part, b:b + 1, e * block:(e + 1) * block], 1.0, hit)
            mask[part * sblocks + b] = jnp.broadcast_to(jnp.max(hit, axis=1, keepdims=True), (slots, block))

    set_mask(0)
    top[...] = jnp.full(top.shape, LOWEST, F32)
    rescale[...] = jnp.ones(rescale.shape, F32)
    total[...] = jnp.zeros(total.shape, F32)
    turned[...] = jnp.zeros(turned.shape, F32)

    tile = scores.shape[2]
    per = block // 8

    def bit(k, lane, h, b):
        return mask[b, pl.ds((k * 2 + lane) * 2 + h, 1), :] > 0.5

    def score_piece(k, lane, n, maxima):
        product = lax.dot_general(
            points(k, lane), src[n * tile:(n + 1) * tile, :], across, preferred_element_type=F32
        )
        extra = held[k, lane, block:block + 16, :].astype(F32)
        shift = extra[0:8, 0:block] + extra[0:8, block:2 * block] + extra[8:16, 0:block]
        for h in range(piece // block):
            shifts = jnp.concatenate(
                [jnp.broadcast_to(shift[:, h * per + q:h * per + q + 1], (8, block)) for q in range(per)], axis=0
            )
            for c in range(tile // block):
                score = product[h * block:(h + 1) * block, c * block:(c + 1) * block] + shifts
                spot = lane * piece + h * block
                scores[n, spot:spot + block, c * block:(c + 1) * block] = score
                best = jnp.max(score.reshape(per, 8, block), axis=0)
                best = jnp.where(bit(k, lane, h, n * (tile // block) + c), best, LOWEST)
                maxima[c] = jnp.maximum(maxima[c], best)

    def weigh_piece(k, lane, n, tops, sums):
        for h in range(piece // block):
            for c in range(tile // block):
                spot = lane * piece + h * block
                against = jnp.where(bit(k, lane, h, n * (tile // block) + c), tops[c], -LOWEST)
                score = scores[n, spot:spot + block, c * block:(c + 1) * block]
                weight = jnp.exp2((score - against) * to_two)
                sums[c] = sums[c] + jnp.sum(weight.reshape(per, 8, block), axis=0)
                weights[n, spot:spot + block, c * block:(c + 1) * block] = weight.astype(BF16)

    def columns(n, c):
        return slice(n * tile + c * block, n * tile + (c + 1) * block)

    tiles = parts * rows // tile

    def absorb(fresh, ready, tick=None, order=range(tiles), after=None):
        if ready is not None:
            for lane in range(2):
                crossed[:, lane * piece:(lane + 1) * piece] = points(ready, lane).T
        inside = range(tile // block)
        for n in order:
            if tick is not None:
                tick(n)
            tops = [top[0:1, columns(n, c)] for c in inside]
            maxima = list(tops)
            scales = [rescale[0:1, columns(n, c)] for c in inside]
            sums = [total[:, columns(n, c)] * scales[c] for c in inside]
            for lane in range(2):
                if ready is not None:
                    weigh_piece(ready, lane, n, tops, sums)
                if fresh is not None:
                    score_piece(fresh, lane, n, maxima)
            if ready is not None:
                added = jnp.dot(crossed[...], weights[n], preferred_element_type=F32)
            for c in inside:
                at = columns(n, c)
                if ready is not None:
                    total[:, at] = sums[c]
                    turned[:, at] = turned[:, at] * scales[c] + added[:, c * block:(c + 1) * block]
                if fresh is not None:
                    new = jnp.max(maxima[c], axis=0, keepdims=True)
                    rescale[0:1, at] = jnp.exp2((tops[c] - new) * to_two)
                    top[0:1, at] = new
            if after is not None:
                after(n)

    def pass_on(k, lane, g):
        onward = (send_up, send_down)[lane]
        arrived(k, lane, g)

        @pl.when(k + 2 < rounds)
        def _():
            onward(k, lane, k + 2, g).start()

    def tick_of(k):
        def tick(n):
            if n % (tiles // 2) == 0:
                for lane in range(2):
                    pass_on(k, lane, n // (tiles // 2))
        return tick

    share_active(2).wait_recv()
    share_active(3).start()
    for lane in range(2):
        pass_on(jnp.int32(1), lane, 0)
    for g in range(2):
        share_sources(2, g).wait_recv()
        share_sources(3, g).start()
    for lane in range(2):
        pass_on(jnp.int32(1), lane, 1)
    share_active(1).wait_recv()
    share_active(3).wait_recv()
    for part in range(1, parts):
        set_mask(part)
    for part in (1, 3):
        for g in range(2):
            share_sources(part, g).wait_recv()
    absorb(0, None, tick_of(jnp.int32(2)))

    def one_round(k, carry):
        absorb(k - 2, k - 3, tick_of(k))
        return carry

    lax.fori_loop(3, rounds, one_round, 0)
    absorb(rounds - 2, rounds - 3)
    absorb(rounds - 1, rounds - 2)

    per_part = rows // tile

    def pair_copies(part, i):
        at = slice((part + 1) * rows + i * tile, (part + 1) * rows + (i + 1) * tile)
        m = part // 2 * per_part + i
        return (
            remote(top.at[:, at], pairtop.at[m], end_send.at[0, m], end_recv.at[0, m], twin),
            remote(turned.at[:, at], pairturned.at[m], end_send.at[1, m], end_recv.at[1, m], twin),
        )

    def share_of(q):
        return pl.ds(pl.multiple_of(q * share, share), share)

    def give_stat(part, q, d):
        slot = d + part // 2 * nsrc
        return remote(stat.at[part // 2 * sblocks + q // 2], gotstat.at[slot], rs_send.at[0, slot], rs_recv.at[0, slot],
                      (q, t_side if part else t))

    def give_rows(part, q, d):
        slot = d + part // 2 * nsrc
        return remote(coded.at[pl.ds(pl.multiple_of(part // 2 * rows + q * share, share), share), :], gotnum.at[slot],
                      rs_send.at[1, slot], rs_recv.at[1, slot], (q, t_side if part else t))

    def merge(part, b):
        m, c = part // 2 * per_part + b // (tile // block), b % (tile // block)
        inside = slice(c * block, (c + 1) * block)
        at = slice(part * rows + b * block, part * rows + (b + 1) * block)
        best = jnp.maximum(top[0:1, at], pairtop[m, 0:1, inside])
        ours = jnp.exp2((top[0:1, at] - best) * to_two)
        theirs = jnp.exp2((pairtop[m, 0:1, inside] - best) * to_two)
        both = turned[:, at] * ours + pairturned[m, :, inside] * theirs
        largest = jnp.maximum(jnp.max(jnp.abs(both), axis=0, keepdims=True), 2e-38)
        spot = part // 2 * sblocks + b
        stat[spot, 0:1, :] = best
        stat[spot, 1:2, :] = top[1:2, at] * ours + pairtop[m, 1:2, inside] * theirs
        stat[spot, 2:3, :] = largest
        coded[spot * block:(spot + 1) * block, :] = jnp.round(
            (both * (1.0 / largest) * 32767.0).T
        ).astype(jnp.int32).astype(jnp.int16)
        for q in (2 * b, 2 * b + 1):
            d = (q - s + nsrc) % nsrc
            if part:
                give_stat(part, q, d).start()
                give_rows(part, q, d).start()
            else:
                @pl.when(q != s)
                def _():
                    give_stat(part, q, d).start()
                    give_rows(part, q, d).start()

    def after(n):
        part, i = n // per_part, n % per_part
        for c in range(tile // block):
            at = columns(n, c)
            top[1:2, at] = jnp.sum(total[:, at], axis=0, keepdims=True)
        if part % 2 == 1:
            for copy in pair_copies(part - 1, i):
                copy.start()
        else:
            for copy in pair_copies(part, i):
                copy.wait_recv()
            for c in range(tile // block):
                merge(part, i * (tile // block) + c)

    order = [part * per_part + i for part in (3, 1, 2, 0) for i in range(per_part)]
    absorb(None, rounds - 1, order=order, after=after)

    gotstat[0] = stat[s // 2]
    mine = share_of(s)
    for d in range(1, nsrc):
        give_stat(0, (s + d) % nsrc, d).wait_recv()
    for d in range(nsrc):
        give_stat(2, (s + d) % nsrc, d).wait_recv()
    slots = range(2 * nsrc)
    tops = jnp.concatenate([gotstat[d, 0:1, :] for d in slots], axis=0)
    dens = jnp.concatenate([gotstat[d, 1:2, :] for d in slots], axis=0)
    sizes_of = jnp.concatenate([gotstat[d, 2:3, :] for d in slots], axis=0)
    best = jnp.max(tops, axis=0, keepdims=True)
    scale = jnp.exp2((tops - best) * to_two)
    den = jnp.sum(scale * dens, axis=0, keepdims=True)
    value = norm[pl.ds(s // 2, 1), :] - eps * (best + jnp.log(den))
    ratio = scale / den * sizes_of
    bound = jnp.maximum(jnp.sum(ratio, axis=0, keepdims=True), 2e-38)
    note_ref[s] = jnp.concatenate([value, bound, jnp.zeros((6, block), F32)], axis=0)
    factor[...] = jnp.concatenate(
        [ratio, 1.0 / bound, jnp.zeros((block - 2 * nsrc - 1, block), F32)], axis=0
    ).T

    def spread_note(d):
        return remote(note_ref.at[s], note_ref.at[s], ag_send.at[0, d], ag_recv.at[0, d], ((s + d) % nsrc, t))

    def spread_rows(d):
        return remote(code_ref.at[mine, :], code_ref.at[mine, :], ag_send.at[1, d], ag_recv.at[1, d],
                      ((s + d) % nsrc, t))

    for d in range(1, nsrc):
        spread_note(d).start()
    column = factor[pl.ds(pl.multiple_of((s % 2) * share, share), share), :]

    def decoded(codes):
        return codes.astype(jnp.int32).astype(F32) * (1.0 / 32767.0)

    image = decoded(coded[mine, :]) * column[:, 0:1]
    for slot in [nsrc + d for d in range(nsrc)] + list(range(1, nsrc)):
        give_rows(slot // nsrc * 2, (s + slot) % nsrc, slot % nsrc).wait_recv()
        image = image + decoded(gotnum[slot]) * column[:, slot:slot + 1]
    code_ref[mine, :] = jnp.round(image * column[:, 2 * nsrc:2 * nsrc + 1] * 32767.0).astype(jnp.int32).astype(jnp.int16)

    for d in range(1, nsrc):
        spread_rows(d).start()

    for g in range(2):
        for to in (1, 2):
            send_up(0, 0, to, g).wait_send()
            send_down(0, 0, to, g).wait_send()

    def drain(k, carry):
        for g in range(2):
            @pl.when(k + 2 < rounds)
            def _():
                send_up(k, 0, k + 2, g).wait_send()
                send_down(k, 1, k + 2, g).wait_send()
        return carry

    lax.fori_loop(1, rounds, drain, 0)
    for part in range(1, parts):
        share_active(part).wait_send()
        for g in range(2):
            share_sources(part, g).wait_send()
    for part in (0, 2):
        for i in range(per_part):
            for copy in pair_copies(part, i):
                copy.wait_send()
    for d in range(1, nsrc):
        give_stat(0, (s + d) % nsrc, d).wait_send()
        give_rows(0, (s + d) % nsrc, d).wait_send()
    for d in range(nsrc):
        give_stat(2, (s + d) % nsrc, d).wait_send()
        give_rows(2, (s + d) % nsrc, d).wait_send()
    for d in range(1, nsrc):
        q = (s + nsrc - d) % nsrc
        remote(note_ref.at[q], note_ref.at[q], ag_send.at[0, d], ag_recv.at[0, d], (q, t)).wait_recv()
        remote(code_ref.at[share_of(q), :], code_ref.at[share_of(q), :], ag_send.at[1, d], ag_recv.at[1, d],
               (q, t)).wait_recv()
        spread_note(d).wait_send()
        spread_rows(d).wait_send()


def decode(share, code_ref, note_ref, val_ref, map_ref):
    block = 128
    lane = lax.broadcasted_iota(jnp.int32, (1, block), 1)
    blocks = range(val_ref.shape[0])
    bounds = []
    for b in blocks:
        first, second = note_ref[2 * b], note_ref[2 * b + 1]
        val_ref[b:b + 1, :] = jnp.where(lane < share, first[0:1, :], second[0:1, :])
        bounds.append(jnp.where(lane < share, first[1:2, :], second[1:2, :]))
    column = jnp.concatenate(bounds + [jnp.zeros((block - len(bounds), block), F32)], axis=0).T
    for b in blocks:
        at = slice(b * block, (b + 1) * block)
        map_ref[at, :] = code_ref[at, :].astype(jnp.int32).astype(F32) * (1.0 / 32767.0) * column[:, b:b + 1]


def per_device(sources, targets, target_potential, active):
    rows, width = sources.shape
    count = targets.shape[0]
    nsrc, ntgt = lax.axis_size("src"), lax.axis_size("tgt")
    eps = 0.5 * math.sqrt(width)
    piece = count // 2
    rounds = ntgt // 4
    share = rows // nsrc
    sblocks = rows // 128
    dma = pltpu.SemaphoreType.DMA
    vmem = pl.BlockSpec(memory_space=pltpu.VMEM)
    codes, notes = pl.pallas_call(
        functools.partial(kernel, (nsrc, ntgt, eps)),
        out_shape=(
            jax.ShapeDtypeStruct((rows, width), jnp.int16),
            jax.ShapeDtypeStruct((nsrc, 8, 128), F32),
        ),
        in_specs=[pl.BlockSpec(memory_space=pltpu.HBM)] * 4,
        out_specs=(vmem, vmem),
        scratch_shapes=[
            pltpu.VMEM((4 * rows, width), BF16),
            pltpu.VMEM((1, count), F32),
            pltpu.VMEM((4,) + active.shape, jnp.int32),
            dma((4, 2)),
            pltpu.VMEM((rounds, 2, piece + 16, width), BF16),
            pltpu.VMEM((4 * rows // 256, 2 * piece, 256), F32),
            pltpu.VMEM((4 * rows // 256, 2 * piece, 256), BF16),
            pltpu.VMEM((width, 2 * piece), BF16),
            pltpu.VMEM((8, 4 * rows), F32),
            pltpu.VMEM((8, 4 * rows), F32),
            pltpu.VMEM((8, 4 * rows), F32),
            pltpu.VMEM((width, 4 * rows), F32),
            pltpu.VMEM((2 * rows // 256, 8, 256), F32),
            pltpu.VMEM((2 * rows // 256, width, 256), F32),
            pltpu.VMEM((2 * rows, width), jnp.int16),
            pltpu.VMEM((4 * sblocks, rounds * 4, 128), F32),
            pltpu.VMEM((sblocks, 128), F32),
            pltpu.VMEM((2 * sblocks, 8, 128), F32),
            pltpu.VMEM((2 * nsrc, 8, 128), F32),
            pltpu.VMEM((2 * nsrc, share, width), jnp.int16),
            pltpu.VMEM((128, 128), F32),
            dma((rounds, 2, 2)),
            dma((2, rounds, 2)),
            dma((4, 3)),
            dma((4, 3)),
            dma((2, 2 * rows // 256)),
            dma((2, 2 * rows // 256)),
            dma((2, 2 * nsrc)),
            dma((2, 2 * nsrc)),
            dma((2, nsrc)),
            dma((2, nsrc)),
        ],
        compiler_params=pltpu.CompilerParams(
            collective_id=0, has_side_effects=True, vmem_limit_bytes=56 * 1024 * 1024
        ),
    )(sources, targets, target_potential.reshape(1, count), active)
    value, image = pl.pallas_call(
        functools.partial(decode, share),
        out_shape=(
            jax.ShapeDtypeStruct((sblocks, 128), F32),
            jax.ShapeDtypeStruct((rows, width), F32),
        ),
        compiler_params=pltpu.CompilerParams(vmem_limit_bytes=60 * 1024 * 1024),
    )(codes, notes)
    return value.reshape(rows), image


def solution(mesh):
    return jax.shard_map(
        per_device,
        mesh=mesh,
        in_specs=(P("tgt", None), P(("src", "tgt"), None), P(("src", "tgt")), P("tgt", None)),
        out_specs=(P("tgt"), P("tgt", None)),
        check_vma=False,
    )
```

```python
import functools
import math

import jax
import jax.numpy as jnp
from jax import lax
from jax.experimental import pallas as pl
from jax.experimental.pallas import tpu as pltpu
from jax.sharding import PartitionSpec as P

MESH = pl.DeviceIdType.MESH
F32 = jnp.float32
BF16 = jnp.bfloat16
LOWEST = -1e38
TILE = 512


def kernel(sizes, src_hbm, tgt_hbm, pot_hbm, act_hbm, code_ref, note_ref,
           src, pot, act, local, held, scores, weights, crossed, top, rescale, total, turned, pairtop, pairturned, coded, mask, norm, stat,
           gotstat, gotnum, factor, recv, send_z, pair_recv, pair_send, end_recv, end_send, rs_recv, rs_send, ag_recv, ag_send):
    nsrc, ntgt, eps = sizes
    rows, width = src_hbm.shape
    piece = tgt_hbm.shape[0] // 2
    block = 128
    rounds = ntgt // 4
    nz = ntgt // 4
    share = rows // nsrc
    sblocks = rows // block
    parts = 4
    to_two = math.log2(math.e)

    s = lax.axis_index("src")
    t = lax.axis_index("tgt")
    half = nsrc // 2
    x_hi, y = s // half, s % half
    z, x_lo, core = t // 4, (t // 2) % 2, t % 2
    up = (s, (t + 4) % ntgt)
    down = (s, (t + ntgt - 4) % ntgt)
    twin = (s, z * 4 + x_lo * 2 + 1 - core)
    side_a = (s, z * 4 + (1 - x_lo) * 2 + core)
    side_b = ((1 - x_hi) * half + y, z * 4 + (1 - x_lo) * 2 + core)
    t_side = z * 4 + (1 - x_lo) * 2 + core
    others = [((s + d) % nsrc, t) for d in range(1, nsrc)] + [((s + d) % nsrc, t_side) for d in range(nsrc)]

    barrier = pltpu.get_barrier_semaphore()
    for device in [up, down, twin] + others:
        pl.semaphore_signal(barrier, inc=1, device_id=device, device_id_type=MESH)

    loads = [
        pltpu.make_async_copy(tgt_hbm.at[part * piece + h * block:part * piece + (h + 1) * block, :],
                              held.at[0, 1 - part, h * (block + 16):h * (block + 16) + block, :], local.at[part, h])
        for part in range(2) for h in range(2)
    ] + [
        pltpu.make_async_copy(pot_hbm, pot, local.at[2, 0]),
        pltpu.make_async_copy(src_hbm, src.at[0:rows, :], local.at[2, 1]),
        pltpu.make_async_copy(act_hbm, act.at[0], local.at[3, 0]),
    ]
    for load in loads:
        load.start()

    def remote(source, target, ssem, rsem, device):
        return pltpu.make_async_remote_copy(
            src_ref=source, dst_ref=target, send_sem=ssem, recv_sem=rsem, device_id=device, device_id_type=MESH
        )

    parts_of = (slice(0, block + 16), slice(block + 16, 2 * block + 16))

    def send_up(k, lane, to, g):
        return remote(held.at[k, lane, parts_of[g], :], held.at[to, 0, parts_of[g], :],
                      send_z.at[0, to, g], recv.at[to, 0, g], up)

    def send_down(k, lane, to, g):
        return remote(held.at[k, lane, parts_of[g], :], held.at[to, 1, parts_of[g], :],
                      send_z.at[1, to, g], recv.at[to, 1, g], down)

    def part_rows(part, g):
        return src.at[part * rows + g * (rows // 2):part * rows + (g + 1) * (rows // 2), :]

    def share_sources(part, g):
        device = (twin, (side_a, side_b)[g], twin)[part - 1]
        return remote(part_rows(2 if part == 3 else 0, g), part_rows(part, g),
                      pair_send.at[part, g], pair_recv.at[part, g], device)

    def share_active(part):
        device = (twin, side_a, twin)[part - 1]
        return remote(act.at[2 if part == 3 else 0], act.at[part], pair_send.at[part, 2], pair_recv.at[part, 2], device)

    def arrived(k, lane, g):
        here = held.at[k, lane, parts_of[g], :]
        remote(here, here, send_z.at[0, 0, g], recv.at[k, lane, g], up).wait_recv()

    def points(k, lane):
        return jnp.concatenate([held[k, lane, 0:block, :], held[k, lane, block + 16:2 * block + 16, :]], axis=0)

    ones = jnp.ones((8, width), BF16)
    across = (((1,), (1,)), ((), ()))

    def half_norms(block_rows):
        wide = block_rows.astype(F32)
        square = 0.5 * (wide * wide)
        high = square.astype(BF16)
        low = (square - high.astype(F32)).astype(BF16)
        return lax.dot_general(ones, high, across, preferred_element_type=F32) + lax.dot_general(
            ones, low, across, preferred_element_type=F32
        )

    own_row = lax.broadcasted_iota(jnp.int32, (8, piece), 0) == lax.broadcasted_iota(jnp.int32, (8, piece), 1) % 8
    chooser = jnp.where(
        lax.broadcasted_iota(jnp.int32, (piece, block), 0) // 8 == lax.broadcasted_iota(jnp.int32, (piece, block), 1),
        1.0, 0.0,
    ).astype(BF16)

    for part in range(2):
        loads[2 * part].wait()
        loads[2 * part + 1].wait()
        if part == 0:
            loads[4].wait()
        data = points(0, 1 - part)
        shifted = (pot[0:1, part * piece:(part + 1) * piece] - half_norms(data)[0:1, :]) * (1.0 / eps)
        high = shifted.astype(BF16).astype(F32)
        middle = (shifted - high).astype(BF16).astype(F32)
        low = shifted - high - middle
        spread_out = [
            jnp.dot(jnp.where(own_row, jnp.broadcast_to(value, (8, piece)), 0.0).astype(BF16), chooser,
                    preferred_element_type=F32)
            for value in (high, middle, low)
        ]
        extra = jnp.concatenate([
            jnp.concatenate([spread_out[0], spread_out[1]], axis=1),
            jnp.concatenate([spread_out[2], jnp.zeros((8, block), F32)], axis=1),
        ], axis=0)
        held[0, 1 - part, block:block + 16, :] = extra.astype(BF16)

    loads[5].wait()
    loads[6].wait()
    for b in range(sblocks):
        norm[b:b + 1, :] = half_norms(src[b * block:(b + 1) * block, :])[0:1, :]
    src[0:rows, :] = (src[0:rows, :].astype(F32) * (1.0 / eps)).astype(BF16)

    pl.semaphore_wait(barrier, 3 + 2 * nsrc - 1)
    for g in range(2):
        send_up(0, 1, 1, g).start()
        send_down(0, 0, 1, g).start()
    for g in range(2):
        share_sources(2, g).start()
    share_active(2).start()
    share_active(1).start()
    for g in range(2):
        share_sources(1, g).start()
        send_up(0, 0, 2, g).start()
        send_down(0, 1, 2, g).start()

    slots = rounds * 2 * 2
    place = lax.broadcasted_iota(jnp.int32, (slots, block), 0)
    part_h, kind, k = place % 2, (place // 2) % 2, place // 4
    odd = k % 2
    distance = (k + 1) // 2
    letter = jnp.where(kind == 0, 1 - odd, odd)
    z_from = (z + jnp.where(kind == 0, nz - distance, distance)) % nz
    owner = (x_hi * half + y) * ntgt + z_from * 4 + x_lo * 2 + core
    number = owner * 4 + letter * 2 + part_h

    def set_mask(part):
        for b in range(sblocks):
            hit = jnp.zeros((slots, block), F32)
            for e in range(act.shape[2] // block):
                hit = jnp.where(number == act[part, b:b + 1, e * block:(e + 1) * block], 1.0, hit)
            mask[part * sblocks + b] = jnp.broadcast_to(jnp.max(hit, axis=1, keepdims=True), (slots, block))

    set_mask(0)
    top[...] = jnp.full(top.shape, LOWEST, F32)
    rescale[...] = jnp.ones(rescale.shape, F32)
    total[...] = jnp.zeros(total.shape, F32)
    turned[...] = jnp.zeros(turned.shape, F32)

    tile = scores.shape[2]
    per = block // 8

    def bit(k, lane, h, b):
        return mask[b, pl.ds((k * 2 + lane) * 2 + h, 1), :] > 0.5

    def score_piece(k, lane, n, maxima):
        product = lax.dot_general(
            points(k, lane), src[n * tile:(n + 1) * tile, :], across, preferred_element_type=F32
        )
        extra = held[k, lane, block:block + 16, :].astype(F32)
        shift = extra[0:8, 0:block] + extra[0:8, block:2 * block] + extra[8:16, 0:block]
        for h in range(piece // block):
            shifts = jnp.concatenate(
                [jnp.broadcast_to(shift[:, h * per + q:h * per + q + 1], (8, block)) for q in range(per)], axis=0
            )
            for c in range(tile // block):
                score = product[h * block:(h + 1) * block, c * block:(c + 1) * block] + shifts
                spot = lane * piece + h * block
                scores[n, spot:spot + block, c * block:(c + 1) * block] = score
                best = jnp.max(score.reshape(per, 8, block), axis=0)
                best = jnp.where(bit(k, lane, h, n * (tile // block) + c), best, LOWEST)
                maxima[c] = jnp.maximum(maxima[c], best)

    def weigh_piece(k, lane, n, tops, sums):
        for h in range(piece // block):
            for c in range(tile // block):
                spot = lane * piece + h * block
                against = jnp.where(bit(k, lane, h, n * (tile // block) + c), tops[c], -LOWEST)
                score = scores[n, spot:spot + block, c * block:(c + 1) * block]
                weight = jnp.exp2((score - against) * to_two)
                sums[c] = sums[c] + jnp.sum(weight.reshape(per, 8, block), axis=0)
                weights[n, spot:spot + block, c * block:(c + 1) * block] = weight.astype(BF16)

    def columns(n, c):
        return slice(n * tile + c * block, n * tile + (c + 1) * block)

    tiles = parts * rows // tile

    def absorb(fresh, ready, tick=None, order=range(tiles), after=None):
        if ready is not None:
            for lane in range(2):
                crossed[:, lane * piece:(lane + 1) * piece] = points(ready, lane).T
        inside = range(tile // block)
        for n in order:
            if tick is not None:
                tick(n)
            tops = [top[0:1, columns(n, c)] for c in inside]
            maxima = list(tops)
            scales = [rescale[0:1, columns(n, c)] for c in inside]
            sums = [total[:, columns(n, c)] * scales[c] for c in inside]
            for lane in range(2):
                if ready is not None:
                    weigh_piece(ready, lane, n, tops, sums)
                if fresh is not None:
                    score_piece(fresh, lane, n, maxima)
            if ready is not None:
                added = jnp.dot(crossed[...], weights[n], preferred_element_type=F32)
            for c in inside:
                at = columns(n, c)
                if ready is not None:
                    total[:, at] = sums[c]
                    turned[:, at] = turned[:, at] * scales[c] + added[:, c * block:(c + 1) * block]
                if fresh is not None:
                    new = jnp.max(maxima[c], axis=0, keepdims=True)
                    rescale[0:1, at] = jnp.exp2((tops[c] - new) * to_two)
                    top[0:1, at] = new
            if after is not None:
                after(n)

    def pass_on(k, lane, g):
        onward = (send_up, send_down)[lane]
        arrived(k, lane, g)

        @pl.when(k + 2 < rounds)
        def _():
            onward(k, lane, k + 2, g).start()

    def tick_of(k):
        def tick(n):
            if n % (tiles // 2) == 0:
                for lane in range(2):
                    pass_on(k, lane, n // (tiles // 2))
        return tick

    share_active(2).wait_recv()
    share_active(3).start()
    for lane in range(2):
        pass_on(jnp.int32(1), lane, 0)
    for g in range(2):
        share_sources(2, g).wait_recv()
        share_sources(3, g).start()
    for lane in range(2):
        pass_on(jnp.int32(1), lane, 1)
    share_active(1).wait_recv()
    share_active(3).wait_recv()
    for part in range(1, parts):
        set_mask(part)
    for part in (1, 3):
        for g in range(2):
            share_sources(part, g).wait_recv()
    absorb(0, None, tick_of(jnp.int32(2)))

    def one_round(k, carry):
        absorb(k - 2, k - 3, tick_of(k))
        return carry

    lax.fori_loop(3, rounds, one_round, 0)
    absorb(rounds - 2, rounds - 3)
    absorb(rounds - 1, rounds - 2)

    per_part = rows // tile

    def pair_copies(part, i):
        at = slice((part + 1) * rows + i * tile, (part + 1) * rows + (i + 1) * tile)
        m = part // 2 * per_part + i
        return (
            remote(top.at[:, at], pairtop.at[m], end_send.at[0, m], end_recv.at[0, m], twin),
            remote(turned.at[:, at], pairturned.at[m], end_send.at[1, m], end_recv.at[1, m], twin),
        )

    def share_of(q):
        return pl.ds(pl.multiple_of(q * share, share), share)

    def give_stat(part, q, d):
        slot = d + part // 2 * nsrc
        return remote(stat.at[part // 2 * sblocks + q // 2], gotstat.at[slot], rs_send.at[0, slot], rs_recv.at[0, slot],
                      (q, t_side if part else t))

    def give_rows(part, q, d):
        slot = d + part // 2 * nsrc
        return remote(coded.at[pl.ds(pl.multiple_of(part // 2 * rows + q * share, share), share), :], gotnum.at[slot],
                      rs_send.at[1, slot], rs_recv.at[1, slot], (q, t_side if part else t))

    def merge(part, b):
        m, c = part // 2 * per_part + b // (tile // block), b % (tile // block)
        inside = slice(c * block, (c + 1) * block)
        at = slice(part * rows + b * block, part * rows + (b + 1) * block)
        best = jnp.maximum(top[0:1, at], pairtop[m, 0:1, inside])
        ours = jnp.exp2((top[0:1, at] - best) * to_two)
        theirs = jnp.exp2((pairtop[m, 0:1, inside] - best) * to_two)
        both = turned[:, at] * ours + pairturned[m, :, inside] * theirs
        largest = jnp.maximum(jnp.max(jnp.abs(both), axis=0, keepdims=True), 2e-38)
        spot = part // 2 * sblocks + b
        stat[spot, 0:1, :] = best
        stat[spot, 1:2, :] = top[1:2, at] * ours + pairtop[m, 1:2, inside] * theirs
        stat[spot, 2:3, :] = largest
        coded[spot * block:(spot + 1) * block, :] = jnp.round(
            (both * (1.0 / largest) * 32767.0).T
        ).astype(jnp.int32).astype(jnp.int16)
        for q in (2 * b, 2 * b + 1):
            d = (q - s + nsrc) % nsrc
            if part:
                give_stat(part, q, d).start()
                give_rows(part, q, d).start()
            else:
                @pl.when(q != s)
                def _():
                    give_stat(part, q, d).start()
                    give_rows(part, q, d).start()

    def after(n):
        part, i = n // per_part, n % per_part
        for c in range(tile // block):
            at = columns(n, c)
            top[1:2, at] = jnp.sum(total[:, at], axis=0, keepdims=True)
        if part % 2 == 1:
            for copy in pair_copies(part - 1, i):
                copy.start()
        else:
            for copy in pair_copies(part, i):
                copy.wait_recv()
            for c in range(tile // block):
                merge(part, i * (tile // block) + c)

    order = [part * per_part + i for part in (3, 1, 2, 0) for i in range(per_part)]
    absorb(None, rounds - 1, order=order, after=after)

    gotstat[0] = stat[s // 2]
    mine = share_of(s)
    for d in range(1, nsrc):
        give_stat(0, (s + d) % nsrc, d).wait_recv()
    for d in range(nsrc):
        give_stat(2, (s + d) % nsrc, d).wait_recv()
    slots = range(2 * nsrc)
    tops = jnp.concatenate([gotstat[d, 0:1, :] for d in slots], axis=0)
    dens = jnp.concatenate([gotstat[d, 1:2, :] for d in slots], axis=0)
    sizes_of = jnp.concatenate([gotstat[d, 2:3, :] for d in slots], axis=0)
    best = jnp.max(tops, axis=0, keepdims=True)
    scale = jnp.exp2((tops - best) * to_two)
    den = jnp.sum(scale * dens, axis=0, keepdims=True)
    value = norm[pl.ds(s // 2, 1), :] - eps * (best + jnp.log(den))
    ratio = scale / den * sizes_of
    bound = jnp.maximum(jnp.sum(ratio, axis=0, keepdims=True), 2e-38)
    note_ref[s] = jnp.concatenate([value, bound, jnp.zeros((6, block), F32)], axis=0)
    factor[...] = jnp.concatenate(
        [ratio, 1.0 / bound, jnp.zeros((block - 2 * nsrc - 1, block), F32)], axis=0
    ).T

    def spread_note(d):
        return remote(note_ref.at[s], note_ref.at[s], ag_send.at[0, d], ag_recv.at[0, d], ((s + d) % nsrc, t))

    def spread_rows(d):
        return remote(code_ref.at[mine, :], code_ref.at[mine, :], ag_send.at[1, d], ag_recv.at[1, d],
                      ((s + d) % nsrc, t))

    for d in range(1, nsrc):
        spread_note(d).start()
    column = factor[pl.ds(pl.multiple_of((s % 2) * share, share), share), :]

    def decoded(codes):
        return codes.astype(jnp.int32).astype(F32) * (1.0 / 32767.0)

    image = decoded(coded[mine, :]) * column[:, 0:1]
    for slot in [nsrc + d for d in range(nsrc)] + list(range(1, nsrc)):
        give_rows(slot // nsrc * 2, (s + slot) % nsrc, slot % nsrc).wait_recv()
        image = image + decoded(gotnum[slot]) * column[:, slot:slot + 1]
    code_ref[mine, :] = jnp.round(image * column[:, 2 * nsrc:2 * nsrc + 1] * 32767.0).astype(jnp.int32).astype(jnp.int16)

    for d in range(1, nsrc):
        spread_rows(d).start()

    for g in range(2):
        for to in (1, 2):
            send_up(0, 0, to, g).wait_send()
            send_down(0, 0, to, g).wait_send()

    def drain(k, carry):
        for g in range(2):
            @pl.when(k + 2 < rounds)
            def _():
                send_up(k, 0, k + 2, g).wait_send()
                send_down(k, 1, k + 2, g).wait_send()
        return carry

    lax.fori_loop(1, rounds, drain, 0)
    for part in range(1, parts):
        share_active(part).wait_send()
        for g in range(2):
            share_sources(part, g).wait_send()
    for part in (0, 2):
        for i in range(per_part):
            for copy in pair_copies(part, i):
                copy.wait_send()
    for d in range(1, nsrc):
        give_stat(0, (s + d) % nsrc, d).wait_send()
        give_rows(0, (s + d) % nsrc, d).wait_send()
    for d in range(nsrc):
        give_stat(2, (s + d) % nsrc, d).wait_send()
        give_rows(2, (s + d) % nsrc, d).wait_send()
    for d in range(1, nsrc):
        q = (s + nsrc - d) % nsrc
        remote(note_ref.at[q], note_ref.at[q], ag_send.at[0, d], ag_recv.at[0, d], (q, t)).wait_recv()
        remote(code_ref.at[share_of(q), :], code_ref.at[share_of(q), :], ag_send.at[1, d], ag_recv.at[1, d],
               (q, t)).wait_recv()
        spread_note(d).wait_send()
        spread_rows(d).wait_send()


def decode(share, code_ref, note_ref, val_ref, map_ref):
    block = 128
    lane = lax.broadcasted_iota(jnp.int32, (1, block), 1)
    blocks = range(val_ref.shape[0])
    bounds = []
    for b in blocks:
        first, second = note_ref[2 * b], note_ref[2 * b + 1]
        val_ref[b:b + 1, :] = jnp.where(lane < share, first[0:1, :], second[0:1, :])
        bounds.append(jnp.where(lane < share, first[1:2, :], second[1:2, :]))
    column = jnp.concatenate(bounds + [jnp.zeros((block - len(bounds), block), F32)], axis=0).T
    for b in blocks:
        at = slice(b * block, (b + 1) * block)
        map_ref[at, :] = code_ref[at, :].astype(jnp.int32).astype(F32) * (1.0 / 32767.0) * column[:, b:b + 1]


def per_device(sources, targets, target_potential, active):
    rows, width = sources.shape
    count = targets.shape[0]
    nsrc, ntgt = lax.axis_size("src"), lax.axis_size("tgt")
    eps = 0.5 * math.sqrt(width)
    piece = count // 2
    rounds = ntgt // 4
    share = rows // nsrc
    sblocks = rows // 128
    dma = pltpu.SemaphoreType.DMA
    vmem = pl.BlockSpec(memory_space=pltpu.VMEM)
    codes, notes = pl.pallas_call(
        functools.partial(kernel, (nsrc, ntgt, eps)),
        out_shape=(
            jax.ShapeDtypeStruct((rows, width), jnp.int16),
            jax.ShapeDtypeStruct((nsrc, 8, 128), F32),
        ),
        in_specs=[pl.BlockSpec(memory_space=pltpu.HBM)] * 4,
        out_specs=(vmem, vmem),
        scratch_shapes=[
            pltpu.VMEM((4 * rows, width), BF16),
            pltpu.VMEM((1, count), F32),
            pltpu.VMEM((4,) + active.shape, jnp.int32),
            dma((4, 2)),
            pltpu.VMEM((rounds, 2, piece + 16, width), BF16),
            pltpu.VMEM((4 * rows // TILE, 2 * piece, TILE), F32),
            pltpu.VMEM((4 * rows // TILE, 2 * piece, TILE), BF16),
            pltpu.VMEM((width, 2 * piece), BF16),
            pltpu.VMEM((8, 4 * rows), F32),
            pltpu.VMEM((8, 4 * rows), F32),
            pltpu.VMEM((8, 4 * rows), F32),
            pltpu.VMEM((width, 4 * rows), F32),
            pltpu.VMEM((2 * rows // TILE, 8, TILE), F32),
            pltpu.VMEM((2 * rows // TILE, width, TILE), F32),
            pltpu.VMEM((2 * rows, width), jnp.int16),
            pltpu.VMEM((4 * sblocks, rounds * 4, 128), F32),
            pltpu.VMEM((sblocks, 128), F32),
            pltpu.VMEM((2 * sblocks, 8, 128), F32),
            pltpu.VMEM((2 * nsrc, 8, 128), F32),
            pltpu.VMEM((2 * nsrc, share, width), jnp.int16),
            pltpu.VMEM((128, 128), F32),
            dma((rounds, 2, 2)),
            dma((2, rounds, 2)),
            dma((4, 3)),
            dma((4, 3)),
            dma((2, 2 * rows // TILE)),
            dma((2, 2 * rows // TILE)),
            dma((2, 2 * nsrc)),
            dma((2, 2 * nsrc)),
            dma((2, nsrc)),
            dma((2, nsrc)),
        ],
        compiler_params=pltpu.CompilerParams(
            collective_id=0, has_side_effects=True, vmem_limit_bytes=56 * 1024 * 1024
        ),
    )(sources, targets, target_potential.reshape(1, count), active)
    value, image = pl.pallas_call(
        functools.partial(decode, share),
        out_shape=(
            jax.ShapeDtypeStruct((sblocks, 128), F32),
            jax.ShapeDtypeStruct((rows, width), F32),
        ),
        compiler_params=pltpu.CompilerParams(vmem_limit_bytes=60 * 1024 * 1024),
    )(codes, notes)
    return value.reshape(rows), image


def solution(mesh):
    return jax.shard_map(
        per_device,
        mesh=mesh,
        in_specs=(P("tgt", None), P(("src", "tgt"), None), P(("src", "tgt")), P("tgt", None)),
        out_specs=(P("tgt"), P("tgt", None)),
        check_vma=False,
    )
```

```python
import functools
import math

import jax
import jax.numpy as jnp
from jax import lax
from jax.experimental import pallas as pl
from jax.experimental.pallas import tpu as pltpu
from jax.sharding import PartitionSpec as P

MESH = pl.DeviceIdType.MESH
F32 = jnp.float32
BF16 = jnp.bfloat16
LOWEST = -1e38


def kernel(sizes, src_hbm, tgt_hbm, pot_hbm, act_hbm, code_ref, note_ref,
           src, pot, act, local, held, scores, weights, crossed, spread, top, rescale, total, turned, pairtop, pairturned, coded, mask, norm, stat,
           gotstat, gotnum, factor, recv, send_z, send_x, pair_recv, pair_send, rs_recv, rs_send, ag_recv, ag_send):
    nsrc, ntgt, eps = sizes
    rows, width = src_hbm.shape
    piece = tgt_hbm.shape[0] // 2
    block = 128
    rounds = ntgt // 4
    nz = ntgt // 4
    share = rows // nsrc
    sblocks = rows // block
    blocks = 2 * sblocks
    to_two = math.log2(math.e)

    s = lax.axis_index("src")
    t = lax.axis_index("tgt")
    half = nsrc // 2
    x_hi, y = s // half, s % half
    z, x_lo, core = t // 4, (t // 2) % 2, t % 2
    up = (s, (t + 4) % ntgt)
    down = (s, (t + ntgt - 4) % ntgt)
    twin = (s, z * 4 + x_lo * 2 + 1 - core)
    side_a = (s, z * 4 + (1 - x_lo) * 2 + core)
    side_b = ((1 - x_hi) * half + y, z * 4 + (1 - x_lo) * 2 + core)
    others = [((s + d) % nsrc, t) for d in range(1, nsrc)]

    barrier = pltpu.get_barrier_semaphore()
    for device in [up, down, twin, side_a, side_b] + others:
        pl.semaphore_signal(barrier, inc=1, device_id=device, device_id_type=MESH)

    loads = [
        pltpu.make_async_copy(tgt_hbm.at[part * piece + h * block:part * piece + (h + 1) * block, :],
                              held.at[0, 1 - part, h * (block + 16):h * (block + 16) + block, :], local.at[part, h])
        for part in range(2) for h in range(2)
    ] + [
        pltpu.make_async_copy(pot_hbm, pot, local.at[2, 0]),
        pltpu.make_async_copy(src_hbm, src.at[0:rows, :], local.at[2, 1]),
        pltpu.make_async_copy(act_hbm, act.at[0], local.at[3, 0]),
    ]
    for load in loads:
        load.start()

    def remote(source, target, ssem, rsem, device):
        return pltpu.make_async_remote_copy(
            src_ref=source, dst_ref=target, send_sem=ssem, recv_sem=rsem, device_id=device, device_id_type=MESH
        )

    parts_of = (slice(0, block + 16), slice(block + 16, 2 * block + 16))

    def send_up(k, lane, to, g):
        return remote(held.at[k, lane, parts_of[g], :], held.at[to, 0, parts_of[g], :],
                      send_z.at[0, to, g], recv.at[to, 0, g], up)

    def send_down(k, lane, to, g):
        return remote(held.at[k, lane, parts_of[g], :], held.at[to, 1, parts_of[g], :],
                      send_z.at[1, to, g], recv.at[to, 1, g], down)

    def send_a(k, lane, g):
        return remote(held.at[k, lane, parts_of[g], :], held.at[k + 1, 2, parts_of[g], :],
                      send_x.at[0, k, g], recv.at[k + 1, 2, g], side_a)

    def send_b(k, lane, g):
        return remote(held.at[k, lane, parts_of[g], :], held.at[k + 1, 3, parts_of[g], :],
                      send_x.at[1, k, g], recv.at[k + 1, 3, g], side_b)

    share_sources = remote(src_hbm, src.at[rows:2 * rows, :], pair_send.at[0, 0], pair_recv.at[0, 0], twin)
    share_active = remote(act_hbm, act.at[1], pair_send.at[1, 0], pair_recv.at[1, 0], twin)

    def arrived(k, lane, g):
        here = held.at[k, lane, parts_of[g], :]
        remote(here, here, send_z.at[0, 0, g], recv.at[k, lane, g], up).wait_recv()

    def points(k, lane):
        return jnp.concatenate([held[k, lane, 0:block, :], held[k, lane, block + 16:2 * block + 16, :]], axis=0)

    ones = jnp.ones((8, width), BF16)
    across = (((1,), (1,)), ((), ()))

    def half_norms(block_rows):
        wide = block_rows.astype(F32)
        square = 0.5 * (wide * wide)
        high = square.astype(BF16)
        low = (square - high.astype(F32)).astype(BF16)
        return lax.dot_general(ones, high, across, preferred_element_type=F32) + lax.dot_general(
            ones, low, across, preferred_element_type=F32
        )

    own_row = lax.broadcasted_iota(jnp.int32, (8, piece), 0) == lax.broadcasted_iota(jnp.int32, (8, piece), 1) % 8
    chooser = jnp.where(
        lax.broadcasted_iota(jnp.int32, (piece, block), 0) // 8 == lax.broadcasted_iota(jnp.int32, (piece, block), 1),
        1.0, 0.0,
    ).astype(BF16)

    for part in range(2):
        loads[2 * part].wait()
        loads[2 * part + 1].wait()
        if part == 0:
            loads[4].wait()
        data = points(0, 1 - part)
        shifted = (pot[0:1, part * piece:(part + 1) * piece] - half_norms(data)[0:1, :]) * (1.0 / eps)
        high = shifted.astype(BF16).astype(F32)
        middle = (shifted - high).astype(BF16).astype(F32)
        low = shifted - high - middle
        spread_out = [
            jnp.dot(jnp.where(own_row, jnp.broadcast_to(value, (8, piece)), 0.0).astype(BF16), chooser,
                    preferred_element_type=F32)
            for value in (high, middle, low)
        ]
        extra = jnp.concatenate([
            jnp.concatenate([spread_out[0], spread_out[1]], axis=1),
            jnp.concatenate([spread_out[2], jnp.zeros((8, block), F32)], axis=1),
        ], axis=0)
        held[0, 1 - part, block:block + 16, :] = extra.astype(BF16)

    pl.semaphore_wait(barrier, 5 + nsrc - 1)
    for g in range(2):
        send_up(0, 1, 1, g).start()
        send_down(0, 0, 1, g).start()
        send_a(0, 1, g).start()
        send_b(0, 0, g).start()
    share_sources.start()
    share_active.start()

    loads[5].wait()
    loads[6].wait()

    for b in range(sblocks):
        norm[b:b + 1, :] = half_norms(src[b * block:(b + 1) * block, :])[0:1, :]

    slots = (rounds + 1) * 4 * 2
    place = lax.broadcasted_iota(jnp.int32, (slots, block), 0)
    part_h, kind, k = place % 2, (place // 2) % 4, place // 8
    from_side = kind >= 2
    k = jnp.where(from_side, k - 1, k)
    odd = k % 2
    distance = (k + 1) // 2
    below = jnp.where(kind == 0, 1, jnp.where(kind == 1, 0, jnp.where(kind == 2, odd, 1 - odd)))
    letter = jnp.where(kind == 0, 1 - odd, jnp.where(kind == 1, odd, kind - 2))
    z_from = (z + jnp.where(below == 1, nz - distance, distance)) % nz
    x_lo_from = jnp.where(from_side, 1 - x_lo, x_lo)
    x_hi_from = jnp.where(kind == 3, 1 - x_hi, x_hi)
    owner = (x_hi_from * half + y) * ntgt + z_from * 4 + x_lo_from * 2 + core
    number = owner * 4 + letter * 2 + part_h

    def set_mask(part):
        for b in range(sblocks):
            hit = jnp.zeros((slots, block), F32)
            for e in range(act.shape[2] // block):
                hit = jnp.where(number == act[part, b:b + 1, e * block:(e + 1) * block], 1.0, hit)
            mask[part * sblocks + b] = jnp.broadcast_to(jnp.max(hit, axis=1, keepdims=True), (slots, block))

    set_mask(0)
    top[...] = jnp.full(top.shape, LOWEST, F32)
    rescale[...] = jnp.ones(rescale.shape, F32)
    total[...] = jnp.zeros(total.shape, F32)
    turned[...] = jnp.zeros(turned.shape, F32)
    for g in range(2):
        send_up(0, 1, 1, g).wait_send()
        send_up(0, 0, 2, g).start()
        send_down(0, 0, 1, g).wait_send()
        send_down(0, 1, 2, g).start()
    share_active.wait_recv()
    set_mask(1)
    share_sources.wait_recv()
    src[...] = (src[...].astype(F32) * (1.0 / eps)).astype(BF16)

    tile = scores.shape[2]
    per = block // 8

    def bit(k, lane, h, b):
        return mask[b, pl.ds((k * 4 + lane) * 2 + h, 1), :] > 0.5

    def score_piece(k, lane, n, maxima):
        product = lax.dot_general(
            points(k, lane), src[n * tile:(n + 1) * tile, :], across, preferred_element_type=F32
        )
        for h in range(piece // block):
            shifts = spread[lane * piece + h * block:lane * piece + (h + 1) * block, :]
            for c in range(tile // block):
                score = product[h * block:(h + 1) * block, c * block:(c + 1) * block] + shifts
                spot = lane * piece + h * block
                scores[n, spot:spot + block, c * block:(c + 1) * block] = score
                best = jnp.max(score.reshape(per, 8, block), axis=0)
                best = jnp.where(bit(k, lane, h, n * (tile // block) + c), best, LOWEST)
                maxima[c] = jnp.maximum(maxima[c], best)

    def spread_shifts(k, lane):
        extra = held[k, lane, block:block + 16, :].astype(F32)
        shift = extra[0:8, 0:block] + extra[0:8, block:2 * block] + extra[8:16, 0:block]
        for q in range(piece // 8):
            spread[lane * piece + 8 * q:lane * piece + 8 * q + 8, :] = jnp.broadcast_to(shift[:, q:q + 1], (8, block))

    def weigh_piece(k, lane, n, tops, sums):
        for h in range(piece // block):
            for c in range(tile // block):
                spot = lane * piece + h * block
                against = jnp.where(bit(k, lane, h, n * (tile // block) + c), tops[c], -LOWEST)
                score = scores[n, spot:spot + block, c * block:(c + 1) * block]
                weight = jnp.exp2((score - against) * to_two)
                sums[c] = sums[c] + jnp.sum(weight.reshape(per, 8, block), axis=0)
                weights[n, spot:spot + block, c * block:(c + 1) * block] = weight.astype(BF16)

    def columns(n, c):
        return slice(n * tile + c * block, n * tile + (c + 1) * block)

    everything = (0, 1, 2, 3)

    def cross(k, lanes):
        for lane in lanes:
            crossed[:, lane * piece:(lane + 1) * piece] = points(k, lane).T

    def absorb(fresh, ready, tick=None, fresh_lanes=everything, ready_lanes=everything):
        if ready is not None:
            cross(ready, ready_lanes)
        if fresh is not None:
            for lane in fresh_lanes:
                spread_shifts(fresh, lane)
        parts = range(tile // block)
        for n in range(2 * rows // tile):
            if tick is not None:
                tick(n)
            tops = [top[0:1, columns(n, c)] for c in parts]
            maxima = list(tops)
            scales = [rescale[0:1, columns(n, c)] for c in parts]
            sums = [total[:, columns(n, c)] * scales[c] for c in parts]
            added = None
            for lane in range(4):
                if ready is not None and lane in ready_lanes:
                    weigh_piece(ready, lane, n, tops, sums)
                if fresh is not None and lane in fresh_lanes:
                    score_piece(fresh, lane, n, maxima)
                if ready is not None and lane in ready_lanes and lane % 2 == 1:
                    span = slice((lane - 1) * piece, (lane + 1) * piece)
                    term = jnp.dot(crossed[:, span], weights[n, span, :], preferred_element_type=F32)
                    added = term if added is None else added + term
            for c in parts:
                at = columns(n, c)
                if ready is not None:
                    total[:, at] = sums[c]
                    turned[:, at] = turned[:, at] * scales[c] + added[:, c * block:(c + 1) * block]
                if fresh is not None:
                    new = jnp.max(maxima[c], axis=0, keepdims=True)
                    rescale[0:1, at] = jnp.exp2((tops[c] - new) * to_two)
                    top[0:1, at] = new

    def finish(k, after):
        cross(k, (2, 3))
        for lane in (2, 3):
            spread_shifts(k, lane)
        parts = range(tile // block)
        span = slice(2 * piece, 4 * piece)
        for n in (2, 3, 0, 1):
            tops = [top[0:1, columns(n, c)] for c in parts]
            maxima = list(tops)
            for lane in (2, 3):
                score_piece(k, lane, n, maxima)
            new = [jnp.max(maxima[c], axis=0, keepdims=True) for c in parts]
            scales = [jnp.exp2((tops[c] - new[c]) * to_two) for c in parts]
            sums = [total[:, columns(n, c)] * scales[c] for c in parts]
            for lane in (2, 3):
                weigh_piece(k, lane, n, new, sums)
            added = jnp.dot(crossed[:, span], weights[n, span, :], preferred_element_type=F32)
            for c in parts:
                at = columns(n, c)
                top[0:1, at] = new[c]
                top[1:2, at] = jnp.sum(sums[c], axis=0, keepdims=True)
                turned[:, at] = turned[:, at] * scales[c] + added[:, c * block:(c + 1) * block]
            after(n)

    def pass_on(k, lane, g):
        onward = (send_up, send_down)[lane]
        arrived(k, lane, g)

        @pl.when(k + 2 < rounds)
        def _():
            onward(k, lane, k + 2, g).start()

        @pl.when(k % 2 == 1 - lane)
        def _():
            send_a(k, lane, g).start()

        @pl.when(k % 2 == lane)
        def _():
            send_b(k, lane, g).start()

    def sides(k):
        for lane in (2, 3):
            for g in range(2):
                arrived(k, lane, g)

    def tick_of(k):
        def tick(n):
            if n % 2 == 0:
                for lane in range(2):
                    pass_on(k, lane, n // 2)
        return tick

    absorb(0, None, tick_of(jnp.int32(1)), fresh_lanes=(0, 1))
    sides(1)
    absorb(1, 0, tick_of(jnp.int32(2)), ready_lanes=(0, 1))

    def one_round(k, carry):
        sides(k - 1)
        absorb(k - 1, k - 2, tick_of(k))
        return carry

    lax.fori_loop(3, rounds, one_round, 0)
    sides(rounds - 1)
    absorb(rounds - 1, rounds - 2)
    absorb(None, rounds - 1)
    sides(rounds)

    def pair_copies(i):
        at = slice(rows + i * tile, rows + (i + 1) * tile)
        return (
            remote(top.at[:, at], pairtop.at[i], pair_send.at[2, i], pair_recv.at[2, i], twin),
            remote(turned.at[:, at], pairturned.at[i], pair_send.at[3, i], pair_recv.at[3, i], twin),
        )

    def share_of(q):
        return pl.ds(pl.multiple_of(q * share, share), share)

    def give_stat(q, d):
        return remote(stat.at[q // 2], gotstat.at[d], rs_send.at[0, d], rs_recv.at[0, d], (q, t))

    def give_rows(q, d):
        return remote(coded.at[share_of(q), :], gotnum.at[d], rs_send.at[1, d], rs_recv.at[1, d], (q, t))

    def merge(b):
        i, inside = b // (tile // block), slice(b % (tile // block) * block, (b % (tile // block) + 1) * block)
        at = slice(b * block, (b + 1) * block)
        best = jnp.maximum(top[0:1, at], pairtop[i, 0:1, inside])
        ours = jnp.exp2((top[0:1, at] - best) * to_two)
        theirs = jnp.exp2((pairtop[i, 0:1, inside] - best) * to_two)
        both = turned[:, at] * ours + pairturned[i, :, inside] * theirs
        largest = jnp.maximum(jnp.max(jnp.abs(both), axis=0, keepdims=True), 2e-38)
        stat[b, 0:1, :] = best
        stat[b, 1:2, :] = top[1:2, at] * ours + pairtop[i, 1:2, inside] * theirs
        stat[b, 2:3, :] = largest
        coded[at, :] = jnp.round((both * (1.0 / largest) * 32767.0).T).astype(jnp.int32).astype(jnp.int16)
        for q in (2 * b, 2 * b + 1):
            d = (q - s + nsrc) % nsrc

            @pl.when(q != s)
            def _():
                give_stat(q, d).start()
                give_rows(q, d).start()

    def after(n):
        own = rows // tile
        if n >= own:
            for copy in pair_copies(n - own):
                copy.start()
        else:
            for copy in pair_copies(n):
                copy.wait_recv()
            for c in range(tile // block):
                merge(n * (tile // block) + c)

    finish(rounds, after)

    gotstat[0] = stat[s // 2]
    mine = share_of(s)
    for d in range(1, nsrc):
        give_stat((s + d) % nsrc, d).wait_recv()
    tops = jnp.concatenate([gotstat[d, 0:1, :] for d in range(nsrc)], axis=0)
    dens = jnp.concatenate([gotstat[d, 1:2, :] for d in range(nsrc)], axis=0)
    sizes_of = jnp.concatenate([gotstat[d, 2:3, :] for d in range(nsrc)], axis=0)
    best = jnp.max(tops, axis=0, keepdims=True)
    scale = jnp.exp2((tops - best) * to_two)
    den = jnp.sum(scale * dens, axis=0, keepdims=True)
    value = norm[pl.ds(s // 2, 1), :] - eps * (best + jnp.log(den))
    ratio = scale / den * sizes_of
    bound = jnp.maximum(jnp.sum(ratio, axis=0, keepdims=True), 2e-38)
    note_ref[s] = jnp.concatenate([value, bound, jnp.zeros((6, block), F32)], axis=0)
    factor[...] = jnp.concatenate(
        [ratio, 1.0 / bound, jnp.zeros((block - nsrc - 1, block), F32)], axis=0
    ).T

    def spread_note(d):
        return remote(note_ref.at[s], note_ref.at[s], ag_send.at[0, d], ag_recv.at[0, d], ((s + d) % nsrc, t))

    def spread_rows(d):
        return remote(code_ref.at[mine, :], code_ref.at[mine, :], ag_send.at[1, d], ag_recv.at[1, d],
                      ((s + d) % nsrc, t))

    for d in range(1, nsrc):
        spread_note(d).start()
    column = factor[pl.ds(pl.multiple_of((s % 2) * share, share), share), :]

    def decoded(codes):
        return codes.astype(jnp.int32).astype(F32) * (1.0 / 32767.0)

    image = decoded(coded[mine, :]) * column[:, 0:1]
    for d in range(1, nsrc):
        give_rows((s + d) % nsrc, d).wait_recv()
        image = image + decoded(gotnum[d]) * column[:, d:d + 1]
    code_ref[mine, :] = jnp.round(image * column[:, nsrc:nsrc + 1] * 32767.0).astype(jnp.int32).astype(jnp.int16)

    for d in range(1, nsrc):
        spread_rows(d).start()

    for g in range(2):
        send_up(0, 0, 2, g).wait_send()
        send_down(0, 1, 2, g).wait_send()
        send_a(0, 1, g).wait_send()
        send_b(0, 0, g).wait_send()

    def drain(k, carry):
        for g in range(2):
            @pl.when(k + 2 < rounds)
            def _():
                send_up(k, 0, k + 2, g).wait_send()
                send_down(k, 1, k + 2, g).wait_send()
            send_a(k, 0, g).wait_send()
            send_b(k, 0, g).wait_send()
        return carry

    lax.fori_loop(1, rounds, drain, 0)
    for copy in (share_sources, share_active) + pair_copies(0) + pair_copies(1):
        copy.wait_send()
    for d in range(1, nsrc):
        give_stat((s + d) % nsrc, d).wait_send()
        give_rows((s + d) % nsrc, d).wait_send()
    for d in range(1, nsrc):
        q = (s + nsrc - d) % nsrc
        remote(note_ref.at[q], note_ref.at[q], ag_send.at[0, d], ag_recv.at[0, d], (q, t)).wait_recv()
        remote(code_ref.at[share_of(q), :], code_ref.at[share_of(q), :], ag_send.at[1, d], ag_recv.at[1, d],
               (q, t)).wait_recv()
        spread_note(d).wait_send()
        spread_rows(d).wait_send()


def decode(share, code_ref, note_ref, val_ref, map_ref):
    block = 128
    lane = lax.broadcasted_iota(jnp.int32, (1, block), 1)
    b = pl.program_id(0)

    @pl.when(b == 0)
    def _():
        for at in range(val_ref.shape[0]):
            val_ref[at:at + 1, :] = jnp.where(lane < share, note_ref[2 * at, 0:1, :], note_ref[2 * at + 1, 0:1, :])

    bound = jnp.where(lane < share, note_ref[2 * b, 1:2, :], note_ref[2 * b + 1, 1:2, :])
    column = jnp.broadcast_to(bound, (block, block)).T
    map_ref[...] = code_ref[...].astype(jnp.int32).astype(F32) * (1.0 / 32767.0) * column[:, 0:1]


def per_device(sources, targets, target_potential, active):
    rows, width = sources.shape
    count = targets.shape[0]
    nsrc, ntgt = lax.axis_size("src"), lax.axis_size("tgt")
    eps = 0.5 * math.sqrt(width)
    piece = count // 2
    rounds = ntgt // 4
    share = rows // nsrc
    sblocks = rows // 128
    dma = pltpu.SemaphoreType.DMA
    vmem = pl.BlockSpec(memory_space=pltpu.VMEM)
    codes, notes = pl.pallas_call(
        functools.partial(kernel, (nsrc, ntgt, eps)),
        out_shape=(
            jax.ShapeDtypeStruct((rows, width), jnp.int16),
            jax.ShapeDtypeStruct((nsrc, 8, 128), F32),
        ),
        in_specs=[pl.BlockSpec(memory_space=pltpu.HBM)] * 4,
        out_specs=(vmem, vmem),
        scratch_shapes=[
            pltpu.VMEM((2 * rows, width), BF16),
            pltpu.VMEM((1, count), F32),
            pltpu.VMEM((2,) + active.shape, jnp.int32),
            dma((4, 2)),
            pltpu.VMEM((rounds + 1, 4, piece + 16, width), BF16),
            pltpu.VMEM((2 * rows // 256, 4 * piece, 256), F32),
            pltpu.VMEM((2 * rows // 256, 4 * piece, 256), BF16),
            pltpu.VMEM((width, 4 * piece), BF16),
            pltpu.VMEM((4 * piece, 128), F32),
            pltpu.VMEM((8, 2 * rows), F32),
            pltpu.VMEM((8, 2 * rows), F32),
            pltpu.VMEM((8, 2 * rows), F32),
            pltpu.VMEM((width, 2 * rows), F32),
            pltpu.VMEM((rows // 256, 8, 256), F32),
            pltpu.VMEM((rows // 256, width, 256), F32),
            pltpu.VMEM((rows, width), jnp.int16),
            pltpu.VMEM((2 * sblocks, (rounds + 1) * 8, 128), F32),
            pltpu.VMEM((sblocks, 128), F32),
            pltpu.VMEM((sblocks, 8, 128), F32),
            pltpu.VMEM((nsrc, 8, 128), F32),
            pltpu.VMEM((nsrc, share, width), jnp.int16),
            pltpu.VMEM((128, 128), F32),
            dma((rounds + 1, 4, 2)),
            dma((2, rounds, 2)),
            dma((2, rounds, 2)),
            dma((4, 2)),
            dma((4, 2)),
            dma((2, nsrc)),
            dma((2, nsrc)),
            dma((2, nsrc)),
            dma((2, nsrc)),
        ],
        compiler_params=pltpu.CompilerParams(
            collective_id=0, has_side_effects=True, vmem_limit_bytes=56 * 1024 * 1024
        ),
    )(sources, targets, target_potential.reshape(1, count), active)
    value, image = pl.pallas_call(
        functools.partial(decode, share),
        out_shape=(
            jax.ShapeDtypeStruct((sblocks, 128), F32),
            jax.ShapeDtypeStruct((rows, width), F32),
        ),
        grid=(sblocks,),
        in_specs=[
            pl.BlockSpec((128, width), lambda b: (b, 0)),
            pl.BlockSpec((nsrc, 8, 128), lambda b: (0, 0, 0)),
        ],
        out_specs=(
            pl.BlockSpec((sblocks, 128), lambda b: (0, 0)),
            pl.BlockSpec((128, width), lambda b: (b, 0)),
        ),
        compiler_params=pltpu.CompilerParams(vmem_limit_bytes=60 * 1024 * 1024),
    )(codes, notes)
    return value.reshape(rows), image


def solution(mesh):
    return jax.shard_map(
        per_device,
        mesh=mesh,
        in_specs=(P("tgt", None), P(("src", "tgt"), None), P(("src", "tgt")), P("tgt", None)),
        out_specs=(P("tgt"), P("tgt", None)),
        check_vma=False,
    )
```

```python
import functools
import math

import jax
import jax.numpy as jnp
from jax import lax
from jax.experimental import pallas as pl
from jax.experimental.pallas import tpu as pltpu
from jax.sharding import PartitionSpec as P

MESH = pl.DeviceIdType.MESH
F32 = jnp.float32
BF16 = jnp.bfloat16
LOWEST = -1e38


def kernel(sizes, src_hbm, tgt_hbm, pot_hbm, act_hbm, code_ref, note_ref,
           src, flat, pot, act, local, held, scores, weights, crossed, spread, top, rescale, total, turned, pairtop, pairturned, coded, mask, norm, stat,
           gotstat, gotnum, factor, recv, send_z, send_x, pair_recv, pair_send, rs_recv, rs_send, ag_recv, ag_send):
    nsrc, ntgt, eps = sizes
    rows, width = src_hbm.shape
    piece = tgt_hbm.shape[0] // 2
    block = 128
    rounds = ntgt // 4
    nz = ntgt // 4
    share = rows // nsrc
    sblocks = rows // block
    blocks = 2 * sblocks
    to_two = math.log2(math.e)

    s = lax.axis_index("src")
    t = lax.axis_index("tgt")
    half = nsrc // 2
    x_hi, y = s // half, s % half
    z, x_lo, core = t // 4, (t // 2) % 2, t % 2
    up = (s, (t + 4) % ntgt)
    down = (s, (t + ntgt - 4) % ntgt)
    twin = (s, z * 4 + x_lo * 2 + 1 - core)
    side_a = (s, z * 4 + (1 - x_lo) * 2 + core)
    side_b = ((1 - x_hi) * half + y, z * 4 + (1 - x_lo) * 2 + core)
    others = [((s + d) % nsrc, t) for d in range(1, nsrc)]

    barrier = pltpu.get_barrier_semaphore()
    for device in [up, down, twin, side_a, side_b] + others:
        pl.semaphore_signal(barrier, inc=1, device_id=device, device_id_type=MESH)

    loads = [
        pltpu.make_async_copy(tgt_hbm.at[part * piece + h * block:part * piece + (h + 1) * block, :],
                              held.at[0, 1 - part, h * (block + 16):h * (block + 16) + block, :], local.at[part, h])
        for part in range(2) for h in range(2)
    ] + [
        pltpu.make_async_copy(pot_hbm, pot, local.at[2, 0]),
        pltpu.make_async_copy(src_hbm, src.at[0:rows, :], local.at[2, 1]),
        pltpu.make_async_copy(act_hbm, act.at[0], local.at[3, 0]),
    ]
    for load in loads:
        load.start()

    def remote(source, target, ssem, rsem, device):
        return pltpu.make_async_remote_copy(
            src_ref=source, dst_ref=target, send_sem=ssem, recv_sem=rsem, device_id=device, device_id_type=MESH
        )

    parts_of = (slice(0, block + 16), slice(block + 16, 2 * block + 16))

    def send_up(k, lane, to, g):
        return remote(held.at[k, lane, parts_of[g], :], held.at[to, 0, parts_of[g], :],
                      send_z.at[0, to, g], recv.at[to, 0, g], up)

    def send_down(k, lane, to, g):
        return remote(held.at[k, lane, parts_of[g], :], held.at[to, 1, parts_of[g], :],
                      send_z.at[1, to, g], recv.at[to, 1, g], down)

    def send_a(k, lane, g):
        return remote(held.at[k, lane, parts_of[g], :], held.at[k + 1, 2, parts_of[g], :],
                      send_x.at[0, k, g], recv.at[k + 1, 2, g], side_a)

    def send_b(k, lane, g):
        return remote(held.at[k, lane, parts_of[g], :], held.at[k + 1, 3, parts_of[g], :],
                      send_x.at[1, k, g], recv.at[k + 1, 3, g], side_b)

    share_sources = remote(src_hbm, src.at[rows:2 * rows, :], pair_send.at[0, 0], pair_recv.at[0, 0], twin)
    share_active = remote(act_hbm, act.at[1], pair_send.at[1, 0], pair_recv.at[1, 0], twin)

    def arrived(k, lane, g):
        here = held.at[k, lane, parts_of[g], :]
        remote(here, here, send_z.at[0, 0, g], recv.at[k, lane, g], up).wait_recv()

    def points(k, lane):
        return jnp.concatenate([held[k, lane, 0:block, :], held[k, lane, block + 16:2 * block + 16, :]], axis=0)

    ones = jnp.ones((8, width), BF16)
    across = (((1,), (1,)), ((), ()))
    along = (((1,), (0,)), ((), ()))

    def half_norms(block_rows):
        wide = block_rows.astype(F32)
        square = 0.5 * (wide * wide)
        high = square.astype(BF16)
        low = (square - high.astype(F32)).astype(BF16)
        return lax.dot_general(ones, high, across, preferred_element_type=F32) + lax.dot_general(
            ones, low, across, preferred_element_type=F32
        )

    own_row = lax.broadcasted_iota(jnp.int32, (8, piece), 0) == lax.broadcasted_iota(jnp.int32, (8, piece), 1) % 8
    chooser = jnp.where(
        lax.broadcasted_iota(jnp.int32, (piece, block), 0) // 8 == lax.broadcasted_iota(jnp.int32, (piece, block), 1),
        1.0, 0.0,
    ).astype(BF16)

    for part in range(2):
        loads[2 * part].wait()
        loads[2 * part + 1].wait()
        if part == 0:
            loads[4].wait()
        data = points(0, 1 - part)
        shifted = (pot[0:1, part * piece:(part + 1) * piece] - half_norms(data)[0:1, :]) * (1.0 / eps)
        high = shifted.astype(BF16).astype(F32)
        middle = (shifted - high).astype(BF16).astype(F32)
        low = shifted - high - middle
        spread_out = [
            jnp.dot(jnp.where(own_row, jnp.broadcast_to(value, (8, piece)), 0.0).astype(BF16), chooser,
                    preferred_element_type=F32)
            for value in (high, middle, low)
        ]
        extra = jnp.concatenate([
            jnp.concatenate([spread_out[0], spread_out[1]], axis=1),
            jnp.concatenate([spread_out[2], jnp.zeros((8, block), F32)], axis=1),
        ], axis=0)
        held[0, 1 - part, block:block + 16, :] = extra.astype(BF16)

    pl.semaphore_wait(barrier, 5 + nsrc - 1)
    for g in range(2):
        send_up(0, 1, 1, g).start()
        send_down(0, 0, 1, g).start()
        send_a(0, 1, g).start()
        send_b(0, 0, g).start()
    share_sources.start()
    share_active.start()

    loads[5].wait()
    loads[6].wait()

    for b in range(sblocks):
        norm[b:b + 1, :] = half_norms(src[b * block:(b + 1) * block, :])[0:1, :]

    slots = (rounds + 1) * 4 * 2
    place = lax.broadcasted_iota(jnp.int32, (slots, block), 0)
    part_h, kind, k = place % 2, (place // 2) % 4, place // 8
    from_side = kind >= 2
    k = jnp.where(from_side, k - 1, k)
    odd = k % 2
    distance = (k + 1) // 2
    below = jnp.where(kind == 0, 1, jnp.where(kind == 1, 0, jnp.where(kind == 2, odd, 1 - odd)))
    letter = jnp.where(kind == 0, 1 - odd, jnp.where(kind == 1, odd, kind - 2))
    z_from = (z + jnp.where(below == 1, nz - distance, distance)) % nz
    x_lo_from = jnp.where(from_side, 1 - x_lo, x_lo)
    x_hi_from = jnp.where(kind == 3, 1 - x_hi, x_hi)
    owner = (x_hi_from * half + y) * ntgt + z_from * 4 + x_lo_from * 2 + core
    number = owner * 4 + letter * 2 + part_h

    def set_mask(part):
        for b in range(sblocks):
            hit = jnp.zeros((slots, block), F32)
            for e in range(act.shape[2] // block):
                hit = jnp.where(number == act[part, b:b + 1, e * block:(e + 1) * block], 1.0, hit)
            mask[part * sblocks + b] = jnp.broadcast_to(jnp.max(hit, axis=1, keepdims=True), (slots, block))

    set_mask(0)
    top[...] = jnp.full(top.shape, LOWEST, F32)
    rescale[...] = jnp.ones(rescale.shape, F32)
    total[...] = jnp.zeros(total.shape, F32)
    turned[...] = jnp.zeros(turned.shape, F32)
    for g in range(2):
        send_up(0, 1, 1, g).wait_send()
        send_up(0, 0, 2, g).start()
        send_down(0, 0, 1, g).wait_send()
        send_down(0, 1, 2, g).start()
    share_active.wait_recv()
    set_mask(1)
    share_sources.wait_recv()
    for b in range(2 * sblocks):
        at = slice(b * block, (b + 1) * block)
        flat[:, at] = (src[at, :].astype(F32) * (1.0 / eps)).T.astype(BF16)

    tile = scores.shape[2]
    per = block // 8

    def bit(k, lane, h, b):
        return mask[b, pl.ds((k * 4 + lane) * 2 + h, 1), :] > 0.5

    def score_piece(k, lane, n, maxima):
        product = lax.dot_general(
            points(k, lane), flat[:, n * tile:(n + 1) * tile], along, preferred_element_type=F32
        )
        for h in range(piece // block):
            shifts = spread[lane * piece + h * block:lane * piece + (h + 1) * block, :]
            for c in range(tile // block):
                score = product[h * block:(h + 1) * block, c * block:(c + 1) * block] + shifts
                spot = lane * piece + h * block
                scores[n, spot:spot + block, c * block:(c + 1) * block] = score
                best = jnp.max(score.reshape(per, 8, block), axis=0)
                best = jnp.where(bit(k, lane, h, n * (tile // block) + c), best, LOWEST)
                maxima[c] = jnp.maximum(maxima[c], best)

    def spread_shifts(k, lane):
        extra = held[k, lane, block:block + 16, :].astype(F32)
        shift = extra[0:8, 0:block] + extra[0:8, block:2 * block] + extra[8:16, 0:block]
        for q in range(piece // 8):
            spread[lane * piece + 8 * q:lane * piece + 8 * q + 8, :] = jnp.broadcast_to(shift[:, q:q + 1], (8, block))

    def weigh_piece(k, lane, n, tops, sums):
        for h in range(piece // block):
            for c in range(tile // block):
                spot = lane * piece + h * block
                against = jnp.where(bit(k, lane, h, n * (tile // block) + c), tops[c] * to_two, -LOWEST)
                score = scores[n, spot:spot + block, c * block:(c + 1) * block]
                weight = jnp.exp2(score * to_two - against)
                sums[c] = sums[c] + jnp.sum(weight.reshape(per, 8, block), axis=0)
                weights[n, spot:spot + block, c * block:(c + 1) * block] = weight.astype(BF16)

    def columns(n, c):
        return slice(n * tile + c * block, n * tile + (c + 1) * block)

    everything = (0, 1, 2, 3)

    def cross(k, lanes):
        for lane in lanes:
            crossed[:, lane * piece:(lane + 1) * piece] = points(k, lane).T

    def absorb(fresh, ready, tick=None, fresh_lanes=everything, ready_lanes=everything):
        if ready is not None:
            cross(ready, ready_lanes)
        if fresh is not None:
            for lane in fresh_lanes:
                spread_shifts(fresh, lane)
        parts = range(tile // block)
        for n in range(2 * rows // tile):
            if tick is not None:
                tick(n)
            tops = [top[0:1, columns(n, c)] for c in parts]
            maxima = list(tops)
            scales = [rescale[0:1, columns(n, c)] for c in parts]
            sums = [total[:, columns(n, c)] * scales[c] for c in parts]
            added = None
            for lane in range(4):
                if ready is not None and lane in ready_lanes:
                    weigh_piece(ready, lane, n, tops, sums)
                if fresh is not None and lane in fresh_lanes:
                    score_piece(fresh, lane, n, maxima)
                if ready is not None and lane in ready_lanes and lane % 2 == 1:
                    span = slice((lane - 1) * piece, (lane + 1) * piece)
                    term = jnp.dot(crossed[:, span], weights[n, span, :], preferred_element_type=F32)
                    added = term if added is None else added + term
            for c in parts:
                at = columns(n, c)
                if ready is not None:
                    total[:, at] = sums[c]
                    turned[:, at] = turned[:, at] * scales[c] + added[:, c * block:(c + 1) * block]
                if fresh is not None:
                    new = jnp.max(maxima[c], axis=0, keepdims=True)
                    rescale[0:1, at] = jnp.exp2((tops[c] - new) * to_two)
                    top[0:1, at] = new

    def finish(k, after):
        cross(k, (2, 3))
        for lane in (2, 3):
            spread_shifts(k, lane)
        parts = range(tile // block)
        span = slice(2 * piece, 4 * piece)
        for n in (2, 3, 0, 1):
            tops = [top[0:1, columns(n, c)] for c in parts]
            maxima = list(tops)
            for lane in (2, 3):
                score_piece(k, lane, n, maxima)
            new = [jnp.max(maxima[c], axis=0, keepdims=True) for c in parts]
            scales = [jnp.exp2((tops[c] - new[c]) * to_two) for c in parts]
            sums = [total[:, columns(n, c)] * scales[c] for c in parts]
            for lane in (2, 3):
                weigh_piece(k, lane, n, new, sums)
            added = jnp.dot(crossed[:, span], weights[n, span, :], preferred_element_type=F32)
            for c in parts:
                at = columns(n, c)
                top[0:1, at] = new[c]
                top[1:2, at] = jnp.sum(sums[c], axis=0, keepdims=True)
                turned[:, at] = turned[:, at] * scales[c] + added[:, c * block:(c + 1) * block]
            after(n)

    def pass_on(k, lane, g):
        onward = (send_up, send_down)[lane]
        arrived(k, lane, g)

        @pl.when(k + 2 < rounds)
        def _():
            onward(k, lane, k + 2, g).start()

        @pl.when(k % 2 == 1 - lane)
        def _():
            send_a(k, lane, g).start()

        @pl.when(k % 2 == lane)
        def _():
            send_b(k, lane, g).start()

    def sides(k):
        for lane in (2, 3):
            for g in range(2):
                arrived(k, lane, g)

    def tick_of(k):
        def tick(n):
            if n % 2 == 0:
                for lane in range(2):
                    pass_on(k, lane, n // 2)
        return tick

    absorb(0, None, tick_of(jnp.int32(1)), fresh_lanes=(0, 1))
    sides(1)
    absorb(1, 0, tick_of(jnp.int32(2)), ready_lanes=(0, 1))

    def one_round(k, carry):
        sides(k - 1)
        absorb(k - 1, k - 2, tick_of(k))
        return carry

    lax.fori_loop(3, rounds, one_round, 0)
    sides(rounds - 1)
    absorb(rounds - 1, rounds - 2)
    absorb(None, rounds - 1)
    sides(rounds)

    def pair_copies(i):
        at = slice(rows + i * tile, rows + (i + 1) * tile)
        return (
            remote(top.at[:, at], pairtop.at[i], pair_send.at[2, i], pair_recv.at[2, i], twin),
            remote(turned.at[:, at], pairturned.at[i], pair_send.at[3, i], pair_recv.at[3, i], twin),
        )

    def share_of(q):
        return pl.ds(pl.multiple_of(q * share, share), share)

    def give_stat(q, d):
        return remote(stat.at[q // 2], gotstat.at[d], rs_send.at[0, d], rs_recv.at[0, d], (q, t))

    def give_rows(q, d):
        return remote(coded.at[share_of(q), :], gotnum.at[d], rs_send.at[1, d], rs_recv.at[1, d], (q, t))

    def merge(b):
        i, inside = b // (tile // block), slice(b % (tile // block) * block, (b % (tile // block) + 1) * block)
        at = slice(b * block, (b + 1) * block)
        best = jnp.maximum(top[0:1, at], pairtop[i, 0:1, inside])
        ours = jnp.exp2((top[0:1, at] - best) * to_two)
        theirs = jnp.exp2((pairtop[i, 0:1, inside] - best) * to_two)
        both = turned[:, at] * ours + pairturned[i, :, inside] * theirs
        largest = jnp.maximum(jnp.max(jnp.abs(both), axis=0, keepdims=True), 2e-38)
        stat[b, 0:1, :] = best
        stat[b, 1:2, :] = top[1:2, at] * ours + pairtop[i, 1:2, inside] * theirs
        stat[b, 2:3, :] = largest
        coded[at, :] = jnp.round((both * (1.0 / largest) * 32767.0).T).astype(jnp.int32).astype(jnp.int16)
        for q in (2 * b, 2 * b + 1):
            d = (q - s + nsrc) % nsrc

            @pl.when(q != s)
            def _():
                give_stat(q, d).start()
                give_rows(q, d).start()

    def after(n):
        own = rows // tile
        if n >= own:
            for copy in pair_copies(n - own):
                copy.start()
        else:
            for copy in pair_copies(n):
                copy.wait_recv()
            for c in range(tile // block):
                merge(n * (tile // block) + c)

    finish(rounds, after)

    gotstat[0] = stat[s // 2]
    mine = share_of(s)
    for d in range(1, nsrc):
        give_stat((s + d) % nsrc, d).wait_recv()
    tops = jnp.concatenate([gotstat[d, 0:1, :] for d in range(nsrc)], axis=0)
    dens = jnp.concatenate([gotstat[d, 1:2, :] for d in range(nsrc)], axis=0)
    sizes_of = jnp.concatenate([gotstat[d, 2:3, :] for d in range(nsrc)], axis=0)
    best = jnp.max(tops, axis=0, keepdims=True)
    scale = jnp.exp2((tops - best) * to_two)
    den = jnp.sum(scale * dens, axis=0, keepdims=True)
    value = norm[pl.ds(s // 2, 1), :] - eps * (best + jnp.log(den))
    ratio = scale / den * sizes_of
    bound = jnp.maximum(jnp.sum(ratio, axis=0, keepdims=True), 2e-38)
    note_ref[s] = jnp.concatenate([value, bound, jnp.zeros((6, block), F32)], axis=0)
    factor[...] = jnp.concatenate(
        [ratio, 1.0 / bound, jnp.zeros((block - nsrc - 1, block), F32)], axis=0
    ).T

    def spread_note(d):
        return remote(note_ref.at[s], note_ref.at[s], ag_send.at[0, d], ag_recv.at[0, d], ((s + d) % nsrc, t))

    def spread_rows(d):
        return remote(code_ref.at[mine, :], code_ref.at[mine, :], ag_send.at[1, d], ag_recv.at[1, d],
                      ((s + d) % nsrc, t))

    for d in range(1, nsrc):
        spread_note(d).start()
    column = factor[pl.ds(pl.multiple_of((s % 2) * share, share), share), :]

    def decoded(codes):
        return codes.astype(jnp.int32).astype(F32) * (1.0 / 32767.0)

    image = decoded(coded[mine, :]) * column[:, 0:1]
    for d in range(1, nsrc):
        give_rows((s + d) % nsrc, d).wait_recv()
        image = image + decoded(gotnum[d]) * column[:, d:d + 1]
    code_ref[mine, :] = jnp.round(image * column[:, nsrc:nsrc + 1] * 32767.0).astype(jnp.int32).astype(jnp.int16)

    for d in range(1, nsrc):
        spread_rows(d).start()

    for g in range(2):
        send_up(0, 0, 2, g).wait_send()
        send_down(0, 1, 2, g).wait_send()
        send_a(0, 1, g).wait_send()
        send_b(0, 0, g).wait_send()

    def drain(k, carry):
        for g in range(2):
            @pl.when(k + 2 < rounds)
            def _():
                send_up(k, 0, k + 2, g).wait_send()
                send_down(k, 1, k + 2, g).wait_send()
            send_a(k, 0, g).wait_send()
            send_b(k, 0, g).wait_send()
        return carry

    lax.fori_loop(1, rounds, drain, 0)
    for copy in (share_sources, share_active) + pair_copies(0) + pair_copies(1):
        copy.wait_send()
    for d in range(1, nsrc):
        give_stat((s + d) % nsrc, d).wait_send()
        give_rows((s + d) % nsrc, d).wait_send()
    for d in range(1, nsrc):
        q = (s + nsrc - d) % nsrc
        remote(note_ref.at[q], note_ref.at[q], ag_send.at[0, d], ag_recv.at[0, d], (q, t)).wait_recv()
        remote(code_ref.at[share_of(q), :], code_ref.at[share_of(q), :], ag_send.at[1, d], ag_recv.at[1, d],
               (q, t)).wait_recv()
        spread_note(d).wait_send()
        spread_rows(d).wait_send()


def decode(share, code_ref, note_ref, val_ref, map_ref):
    block = 128
    lane = lax.broadcasted_iota(jnp.int32, (1, block), 1)
    blocks = range(val_ref.shape[0])
    bounds = []
    for b in blocks:
        first, second = note_ref[2 * b], note_ref[2 * b + 1]
        val_ref[b:b + 1, :] = jnp.where(lane < share, first[0:1, :], second[0:1, :])
        bounds.append(jnp.where(lane < share, first[1:2, :], second[1:2, :]))
    column = jnp.concatenate(bounds + [jnp.zeros((block - len(bounds), block), F32)], axis=0).T
    for b in blocks:
        at = slice(b * block, (b + 1) * block)
        map_ref[at, :] = code_ref[at, :].astype(jnp.int32).astype(F32) * (1.0 / 32767.0) * column[:, b:b + 1]


def per_device(sources, targets, target_potential, active):
    rows, width = sources.shape
    count = targets.shape[0]
    nsrc, ntgt = lax.axis_size("src"), lax.axis_size("tgt")
    eps = 0.5 * math.sqrt(width)
    piece = count // 2
    rounds = ntgt // 4
    share = rows // nsrc
    sblocks = rows // 128
    dma = pltpu.SemaphoreType.DMA
    vmem = pl.BlockSpec(memory_space=pltpu.VMEM)
    codes, notes = pl.pallas_call(
        functools.partial(kernel, (nsrc, ntgt, eps)),
        out_shape=(
            jax.ShapeDtypeStruct((rows, width), jnp.int16),
            jax.ShapeDtypeStruct((nsrc, 8, 128), F32),
        ),
        in_specs=[pl.BlockSpec(memory_space=pltpu.HBM)] * 4,
        out_specs=(vmem, vmem),
        scratch_shapes=[
            pltpu.VMEM((2 * rows, width), BF16),
            pltpu.VMEM((width, 2 * rows), BF16),
            pltpu.VMEM((1, count), F32),
            pltpu.VMEM((2,) + active.shape, jnp.int32),
            dma((4, 2)),
            pltpu.VMEM((rounds + 1, 4, piece + 16, width), BF16),
            pltpu.VMEM((2 * rows // 256, 4 * piece, 256), F32),
            pltpu.VMEM((2 * rows // 256, 4 * piece, 256), BF16),
            pltpu.VMEM((width, 4 * piece), BF16),
            pltpu.VMEM((4 * piece, 128), F32),
            pltpu.VMEM((8, 2 * rows), F32),
            pltpu.VMEM((8, 2 * rows), F32),
            pltpu.VMEM((8, 2 * rows), F32),
            pltpu.VMEM((width, 2 * rows), F32),
            pltpu.VMEM((rows // 256, 8, 256), F32),
            pltpu.VMEM((rows // 256, width, 256), F32),
            pltpu.VMEM((rows, width), jnp.int16),
            pltpu.VMEM((2 * sblocks, (rounds + 1) * 8, 128), F32),
            pltpu.VMEM((sblocks, 128), F32),
            pltpu.VMEM((sblocks, 8, 128), F32),
            pltpu.VMEM((nsrc, 8, 128), F32),
            pltpu.VMEM((nsrc, share, width), jnp.int16),
            pltpu.VMEM((128, 128), F32),
            dma((rounds + 1, 4, 2)),
            dma((2, rounds, 2)),
            dma((2, rounds, 2)),
            dma((4, 2)),
            dma((4, 2)),
            dma((2, nsrc)),
            dma((2, nsrc)),
            dma((2, nsrc)),
            dma((2, nsrc)),
        ],
        compiler_params=pltpu.CompilerParams(
            collective_id=0, has_side_effects=True, vmem_limit_bytes=56 * 1024 * 1024
        ),
    )(sources, targets, target_potential.reshape(1, count), active)
    value, image = pl.pallas_call(
        functools.partial(decode, share),
        out_shape=(
            jax.ShapeDtypeStruct((sblocks, 128), F32),
            jax.ShapeDtypeStruct((rows, width), F32),
        ),
        compiler_params=pltpu.CompilerParams(vmem_limit_bytes=60 * 1024 * 1024),
    )(codes, notes)
    return value.reshape(rows), image


def solution(mesh):
    return jax.shard_map(
        per_device,
        mesh=mesh,
        in_specs=(P("tgt", None), P(("src", "tgt"), None), P(("src", "tgt")), P("tgt", None)),
        out_specs=(P("tgt"), P("tgt", None)),
        check_vma=False,
    )
```

```python
import functools
import math

import jax
import jax.numpy as jnp
from jax import lax
from jax.experimental import pallas as pl
from jax.experimental.pallas import tpu as pltpu
from jax.sharding import PartitionSpec as P

MESH = pl.DeviceIdType.MESH
F32 = jnp.float32
BF16 = jnp.bfloat16
LOWEST = -1e38


def kernel(sizes, src_hbm, tgt_hbm, pot_hbm, act_hbm, code_ref, note_ref,
           src, flat, pot, act, local, held, offsets, scores, weights, crossed, spread, top, rescale, total, turned, pairtop, pairturned, coded, mask, norm, stat,
           gotstat, gotnum, factor, recv, send_z, send_x, pair_recv, pair_send, rs_recv, rs_send, ag_recv, ag_send):
    nsrc, ntgt, eps = sizes
    rows, width = src_hbm.shape
    piece = tgt_hbm.shape[0] // 2
    block = 128
    rounds = ntgt // 4
    nz = ntgt // 4
    share = rows // nsrc
    sblocks = rows // block
    blocks = 2 * sblocks
    to_two = math.log2(math.e)

    s = lax.axis_index("src")
    t = lax.axis_index("tgt")
    half = nsrc // 2
    x_hi, y = s // half, s % half
    z, x_lo, core = t // 4, (t // 2) % 2, t % 2
    up = (s, (t + 4) % ntgt)
    down = (s, (t + ntgt - 4) % ntgt)
    twin = (s, z * 4 + x_lo * 2 + 1 - core)
    side_a = (s, z * 4 + (1 - x_lo) * 2 + core)
    side_b = ((1 - x_hi) * half + y, z * 4 + (1 - x_lo) * 2 + core)
    others = [((s + d) % nsrc, t) for d in range(1, nsrc)]

    barrier = pltpu.get_barrier_semaphore()
    for device in [up, down, twin, side_a, side_b] + others:
        pl.semaphore_signal(barrier, inc=1, device_id=device, device_id_type=MESH)

    loads = [
        pltpu.make_async_copy(tgt_hbm.at[part * piece + h * block:part * piece + (h + 1) * block, :],
                              held.at[0, 1 - part, h * block:(h + 1) * block, :], local.at[part, h])
        for part in range(2) for h in range(2)
    ] + [
        pltpu.make_async_copy(pot_hbm, pot, local.at[2, 0]),
        pltpu.make_async_copy(src_hbm, src.at[0:rows, :], local.at[2, 1]),
        pltpu.make_async_copy(act_hbm, act.at[0], local.at[3, 0]),
    ]
    for load in loads:
        load.start()

    def remote(source, target, ssem, rsem, device):
        return pltpu.make_async_remote_copy(
            src_ref=source, dst_ref=target, send_sem=ssem, recv_sem=rsem, device_id=device, device_id_type=MESH
        )

    def send(k, lane, to, to_lane, ssem, g, device):
        rsem = recv.at[to, to_lane, g]
        if g == 2:
            return remote(offsets.at[k, lane], offsets.at[to, to_lane], ssem, rsem, device)
        rows_of = slice(g * block, (g + 1) * block)
        source = held.at[k, lane, rows_of, :]
        if isinstance(k, int) and k == 0:
            first = (1 - lane) * piece + g * block
            source = tgt_hbm.at[first:first + block, :]
        return remote(source, held.at[to, to_lane, rows_of, :], ssem, rsem, device)

    def send_up(k, lane, to, g):
        return send(k, lane, to, 0, send_z.at[0, to, g], g, up)

    def send_down(k, lane, to, g):
        return send(k, lane, to, 1, send_z.at[1, to, g], g, down)

    def send_a(k, lane, g):
        return send(k, lane, k + 1, 2, send_x.at[0, k, g], g, side_a)

    def send_b(k, lane, g):
        return send(k, lane, k + 1, 3, send_x.at[1, k, g], g, side_b)

    share_sources = remote(src_hbm, src.at[rows:2 * rows, :], pair_send.at[0, 0], pair_recv.at[0, 0], twin)
    share_active = remote(act_hbm, act.at[1], pair_send.at[1, 0], pair_recv.at[1, 0], twin)

    def arrived(k, lane, g):
        here = offsets.at[k, lane] if g == 2 else held.at[k, lane, g * block:(g + 1) * block, :]
        remote(here, here, send_z.at[0, 0, g], recv.at[k, lane, g], up).wait_recv()

    pl.semaphore_wait(barrier, 5 + nsrc - 1)
    for g in range(2):
        send_up(0, 1, 1, g).start()
        send_down(0, 0, 1, g).start()
        send_a(0, 1, g).start()
        send_b(0, 0, g).start()
    share_sources.start()

    ones = jnp.ones((8, width), BF16)
    across = (((1,), (1,)), ((), ()))
    along = (((1,), (0,)), ((), ()))

    def half_norms(block_rows):
        wide = block_rows.astype(F32)
        square = 0.5 * (wide * wide)
        high = square.astype(BF16)
        low = (square - high.astype(F32)).astype(BF16)
        return lax.dot_general(ones, high, across, preferred_element_type=F32) + lax.dot_general(
            ones, low, across, preferred_element_type=F32
        )

    for part in range(2):
        loads[2 * part].wait()
        loads[2 * part + 1].wait()
        if part == 0:
            loads[4].wait()
        data = held[0, 1 - part, :, :]
        shifted = (pot[0:1, part * piece:(part + 1) * piece] - half_norms(data)[0:1, :]) * (1.0 / eps)
        for h in range(2):
            offsets[0, 1 - part, h:h + 1, :] = shifted[:, h * block:(h + 1) * block]

    send_up(0, 1, 1, 2).start()
    send_down(0, 0, 1, 2).start()
    send_a(0, 1, 2).start()
    send_b(0, 0, 2).start()
    share_active.start()

    loads[5].wait()
    loads[6].wait()

    for b in range(sblocks):
        norm[b:b + 1, :] = half_norms(src[b * block:(b + 1) * block, :])[0:1, :]

    slots = (rounds + 1) * 4 * 2
    place = lax.broadcasted_iota(jnp.int32, (slots, block), 0)
    part_h, kind, k = place % 2, (place // 2) % 4, place // 8
    from_side = kind >= 2
    k = jnp.where(from_side, k - 1, k)
    odd = k % 2
    distance = (k + 1) // 2
    below = jnp.where(kind == 0, 1, jnp.where(kind == 1, 0, jnp.where(kind == 2, odd, 1 - odd)))
    letter = jnp.where(kind == 0, 1 - odd, jnp.where(kind == 1, odd, kind - 2))
    z_from = (z + jnp.where(below == 1, nz - distance, distance)) % nz
    x_lo_from = jnp.where(from_side, 1 - x_lo, x_lo)
    x_hi_from = jnp.where(kind == 3, 1 - x_hi, x_hi)
    owner = (x_hi_from * half + y) * ntgt + z_from * 4 + x_lo_from * 2 + core
    number = owner * 4 + letter * 2 + part_h

    def set_mask(part):
        for b in range(sblocks):
            hit = jnp.zeros((slots, block), F32)
            for e in range(act.shape[2] // block):
                hit = jnp.where(number == act[part, b:b + 1, e * block:(e + 1) * block], 1.0, hit)
            mask[part * sblocks + b] = jnp.broadcast_to(jnp.max(hit, axis=1, keepdims=True), (slots, block))

    set_mask(0)
    top[...] = jnp.full(top.shape, LOWEST, F32)
    rescale[...] = jnp.ones(rescale.shape, F32)
    total[...] = jnp.zeros(total.shape, F32)
    turned[...] = jnp.zeros(turned.shape, F32)
    for g in (2, 0, 1):
        send_up(0, 1, 1, g).wait_send()
        send_up(0, 0, 2, g).start()
        send_down(0, 0, 1, g).wait_send()
        send_down(0, 1, 2, g).start()
    share_active.wait_recv()
    set_mask(1)
    share_sources.wait_recv()
    for b in range(2 * sblocks):
        at = slice(b * block, (b + 1) * block)
        flat[:, at] = (src[at, :].astype(F32) * (1.0 / eps)).T.astype(BF16)

    tile = scores.shape[2]
    per = block // 8

    def bit(k, lane, h, b):
        return mask[b, pl.ds((k * 4 + lane) * 2 + h, 1), :] > 0.5

    def score_piece(k, lane, n, maxima):
        product = lax.dot_general(
            held[k, lane, :, :], flat[:, n * tile:(n + 1) * tile], along, preferred_element_type=F32
        )
        for h in range(piece // block):
            shifts = spread[lane * piece + h * block:lane * piece + (h + 1) * block, :]
            for c in range(tile // block):
                score = product[h * block:(h + 1) * block, c * block:(c + 1) * block] + shifts
                spot = lane * piece + h * block
                scores[n, spot:spot + block, c * block:(c + 1) * block] = score
                best = jnp.max(score.reshape(per, 8, block), axis=0)
                best = jnp.where(bit(k, lane, h, n * (tile // block) + c), best, LOWEST)
                maxima[c] = jnp.maximum(maxima[c], best)

    def spread_shifts(k, lane):
        for h in range(piece // block):
            spot = lane * piece + h * block
            spread[spot:spot + block, :] = jnp.broadcast_to(offsets[k, lane, h:h + 1, :], (block, block)).T

    def weigh_piece(k, lane, n, tops, sums):
        for h in range(piece // block):
            for c in range(tile // block):
                spot = lane * piece + h * block
                against = jnp.where(bit(k, lane, h, n * (tile // block) + c), tops[c] * to_two, -LOWEST)
                score = scores[n, spot:spot + block, c * block:(c + 1) * block]
                weight = jnp.exp2(score * to_two - against)
                sums[c] = sums[c] + jnp.sum(weight.reshape(per, 8, block), axis=0)
                weights[n, spot:spot + block, c * block:(c + 1) * block] = weight.astype(BF16)

    def columns(n, c):
        return slice(n * tile + c * block, n * tile + (c + 1) * block)

    everything = (0, 1, 2, 3)

    def cross(k, lanes):
        for lane in lanes:
            crossed[:, lane * piece:(lane + 1) * piece] = held[k, lane, :, :].T

    def absorb(fresh, ready, tick=None, fresh_lanes=everything, ready_lanes=everything):
        if ready is not None:
            cross(ready, ready_lanes)
        if fresh is not None:
            for lane in fresh_lanes:
                spread_shifts(fresh, lane)
        parts = range(tile // block)
        for n in range(2 * rows // tile):
            if tick is not None:
                tick(n)
            tops = [top[0:1, columns(n, c)] for c in parts]
            maxima = list(tops)
            scales = [rescale[0:1, columns(n, c)] for c in parts]
            sums = [total[:, columns(n, c)] * scales[c] for c in parts]
            added = None
            for lane in range(4):
                if ready is not None and lane in ready_lanes:
                    weigh_piece(ready, lane, n, tops, sums)
                if fresh is not None and lane in fresh_lanes:
                    score_piece(fresh, lane, n, maxima)
                if ready is not None and lane in ready_lanes and lane % 2 == 1:
                    span = slice((lane - 1) * piece, (lane + 1) * piece)
                    term = jnp.dot(crossed[:, span], weights[n, span, :], preferred_element_type=F32)
                    added = term if added is None else added + term
            for c in parts:
                at = columns(n, c)
                if ready is not None:
                    total[:, at] = sums[c]
                    turned[:, at] = turned[:, at] * scales[c] + added[:, c * block:(c + 1) * block]
                if fresh is not None:
                    new = jnp.max(maxima[c], axis=0, keepdims=True)
                    rescale[0:1, at] = jnp.exp2((tops[c] - new) * to_two)
                    top[0:1, at] = new

    def finish(k, after):
        cross(k, (2, 3))
        for lane in (2, 3):
            spread_shifts(k, lane)
        parts = range(tile // block)
        span = slice(2 * piece, 4 * piece)
        for n in (2, 3, 0, 1):
            tops = [top[0:1, columns(n, c)] for c in parts]
            maxima = list(tops)
            for lane in (2, 3):
                score_piece(k, lane, n, maxima)
            new = [jnp.max(maxima[c], axis=0, keepdims=True) for c in parts]
            scales = [jnp.exp2((tops[c] - new[c]) * to_two) for c in parts]
            sums = [total[:, columns(n, c)] * scales[c] for c in parts]
            for lane in (2, 3):
                weigh_piece(k, lane, n, new, sums)
            added = jnp.dot(crossed[:, span], weights[n, span, :], preferred_element_type=F32)
            for c in parts:
                at = columns(n, c)
                top[0:1, at] = new[c]
                top[1:2, at] = jnp.sum(sums[c], axis=0, keepdims=True)
                turned[:, at] = turned[:, at] * scales[c] + added[:, c * block:(c + 1) * block]
            after(n)

    def pass_on(k, lane, g):
        onward = (send_up, send_down)[lane]
        arrived(k, lane, g)

        @pl.when(k + 2 < rounds)
        def _():
            onward(k, lane, k + 2, g).start()

        @pl.when(k % 2 == 1 - lane)
        def _():
            send_a(k, lane, g).start()

        @pl.when(k % 2 == lane)
        def _():
            send_b(k, lane, g).start()

    def sides(k):
        for lane in (2, 3):
            for g in (2, 0, 1):
                arrived(k, lane, g)

    def tick_of(k):
        def tick(n):
            for g in ((2, 0), (), (1,), ())[n]:
                for lane in range(2):
                    pass_on(k, lane, g)
        return tick

    absorb(0, None, tick_of(jnp.int32(1)), fresh_lanes=(0, 1))
    sides(1)
    absorb(1, 0, tick_of(jnp.int32(2)), ready_lanes=(0, 1))

    def one_round(k, carry):
        sides(k - 1)
        absorb(k - 1, k - 2, tick_of(k))
        return carry

    lax.fori_loop(3, rounds, one_round, 0)
    sides(rounds - 1)
    absorb(rounds - 1, rounds - 2)
    absorb(None, rounds - 1)
    sides(rounds)

    def pair_copies(i):
        at = slice(rows + i * tile, rows + (i + 1) * tile)
        return (
            remote(top.at[:, at], pairtop.at[i], pair_send.at[2, i], pair_recv.at[2, i], twin),
            remote(turned.at[:, at], pairturned.at[i], pair_send.at[3, i], pair_recv.at[3, i], twin),
        )

    def share_of(q):
        return pl.ds(pl.multiple_of(q * share, share), share)

    def give_stat(q, d):
        return remote(stat.at[q // 2], gotstat.at[d], rs_send.at[0, d], rs_recv.at[0, d], (q, t))

    def give_rows(q, d):
        return remote(coded.at[share_of(q), :], gotnum.at[d], rs_send.at[1, d], rs_recv.at[1, d], (q, t))

    def merge(b):
        i, inside = b // (tile // block), slice(b % (tile // block) * block, (b % (tile // block) + 1) * block)
        at = slice(b * block, (b + 1) * block)
        best = jnp.maximum(top[0:1, at], pairtop[i, 0:1, inside])
        ours = jnp.exp2((top[0:1, at] - best) * to_two)
        theirs = jnp.exp2((pairtop[i, 0:1, inside] - best) * to_two)
        both = turned[:, at] * ours + pairturned[i, :, inside] * theirs
        largest = jnp.maximum(jnp.max(jnp.abs(both), axis=0, keepdims=True), 2e-38)
        stat[b, 0:1, :] = best
        stat[b, 1:2, :] = top[1:2, at] * ours + pairtop[i, 1:2, inside] * theirs
        stat[b, 2:3, :] = largest
        coded[at, :] = jnp.round((both * (1.0 / largest) * 32767.0).T).astype(jnp.int32).astype(jnp.int16)
        for q in (2 * b, 2 * b + 1):
            d = (q - s + nsrc) % nsrc

            @pl.when(q != s)
            def _():
                give_stat(q, d).start()
                give_rows(q, d).start()

    def after(n):
        own = rows // tile
        if n >= own:
            for copy in pair_copies(n - own):
                copy.start()
        else:
            for copy in pair_copies(n):
                copy.wait_recv()
            for c in range(tile // block):
                merge(n * (tile // block) + c)

    finish(rounds, after)

    gotstat[0] = stat[s // 2]
    mine = share_of(s)
    for d in range(1, nsrc):
        give_stat((s + d) % nsrc, d).wait_recv()
    tops = jnp.concatenate([gotstat[d, 0:1, :] for d in range(nsrc)], axis=0)
    dens = jnp.concatenate([gotstat[d, 1:2, :] for d in range(nsrc)], axis=0)
    sizes_of = jnp.concatenate([gotstat[d, 2:3, :] for d in range(nsrc)], axis=0)
    best = jnp.max(tops, axis=0, keepdims=True)
    scale = jnp.exp2((tops - best) * to_two)
    den = jnp.sum(scale * dens, axis=0, keepdims=True)
    value = norm[pl.ds(s // 2, 1), :] - eps * (best + jnp.log(den))
    ratio = scale / den * sizes_of
    bound = jnp.maximum(jnp.sum(ratio, axis=0, keepdims=True), 2e-38)
    note_ref[s] = jnp.concatenate([value, bound, jnp.zeros((6, block), F32)], axis=0)
    factor[...] = jnp.concatenate(
        [ratio, 1.0 / bound, jnp.zeros((block - nsrc - 1, block), F32)], axis=0
    ).T

    def spread_note(d):
        return remote(note_ref.at[s], note_ref.at[s], ag_send.at[0, d], ag_recv.at[0, d], ((s + d) % nsrc, t))

    def spread_rows(d):
        return remote(code_ref.at[mine, :], code_ref.at[mine, :], ag_send.at[1, d], ag_recv.at[1, d],
                      ((s + d) % nsrc, t))

    for d in range(1, nsrc):
        spread_note(d).start()
    column = factor[pl.ds(pl.multiple_of((s % 2) * share, share), share), :]

    def decoded(codes):
        return codes.astype(jnp.int32).astype(F32) * (1.0 / 32767.0)

    image = decoded(coded[mine, :]) * column[:, 0:1]
    for d in range(1, nsrc):
        give_rows((s + d) % nsrc, d).wait_recv()
        image = image + decoded(gotnum[d]) * column[:, d:d + 1]
    code_ref[mine, :] = jnp.round(image * column[:, nsrc:nsrc + 1] * 32767.0).astype(jnp.int32).astype(jnp.int16)

    for d in range(1, nsrc):
        spread_rows(d).start()

    for g in range(3):
        send_up(0, 0, 2, g).wait_send()
        send_down(0, 1, 2, g).wait_send()
        send_a(0, 1, g).wait_send()
        send_b(0, 0, g).wait_send()

    def drain(k, carry):
        for g in range(3):
            @pl.when(k + 2 < rounds)
            def _():
                send_up(k, 0, k + 2, g).wait_send()
                send_down(k, 1, k + 2, g).wait_send()
            send_a(k, 0, g).wait_send()
            send_b(k, 0, g).wait_send()
        return carry

    lax.fori_loop(1, rounds, drain, 0)
    for copy in (share_sources, share_active) + pair_copies(0) + pair_copies(1):
        copy.wait_send()
    for d in range(1, nsrc):
        give_stat((s + d) % nsrc, d).wait_send()
        give_rows((s + d) % nsrc, d).wait_send()
    for d in range(1, nsrc):
        q = (s + nsrc - d) % nsrc
        remote(note_ref.at[q], note_ref.at[q], ag_send.at[0, d], ag_recv.at[0, d], (q, t)).wait_recv()
        remote(code_ref.at[share_of(q), :], code_ref.at[share_of(q), :], ag_send.at[1, d], ag_recv.at[1, d],
               (q, t)).wait_recv()
        spread_note(d).wait_send()
        spread_rows(d).wait_send()


def decode(share, code_ref, note_ref, val_ref, map_ref):
    block = 128
    lane = lax.broadcasted_iota(jnp.int32, (1, block), 1)
    blocks = range(val_ref.shape[0])
    bounds = []
    for b in blocks:
        first, second = note_ref[2 * b], note_ref[2 * b + 1]
        val_ref[b:b + 1, :] = jnp.where(lane < share, first[0:1, :], second[0:1, :])
        bounds.append(jnp.where(lane < share, first[1:2, :], second[1:2, :]))
    column = jnp.concatenate(bounds + [jnp.zeros((block - len(bounds), block), F32)], axis=0).T
    for b in blocks:
        at = slice(b * block, (b + 1) * block)
        map_ref[at, :] = code_ref[at, :].astype(jnp.int32).astype(F32) * (1.0 / 32767.0) * column[:, b:b + 1]


def per_device(sources, targets, target_potential, active):
    rows, width = sources.shape
    count = targets.shape[0]
    nsrc, ntgt = lax.axis_size("src"), lax.axis_size("tgt")
    eps = 0.5 * math.sqrt(width)
    piece = count // 2
    rounds = ntgt // 4
    share = rows // nsrc
    sblocks = rows // 128
    dma = pltpu.SemaphoreType.DMA
    vmem = pl.BlockSpec(memory_space=pltpu.VMEM)
    codes, notes = pl.pallas_call(
        functools.partial(kernel, (nsrc, ntgt, eps)),
        out_shape=(
            jax.ShapeDtypeStruct((rows, width), jnp.int16),
            jax.ShapeDtypeStruct((nsrc, 8, 128), F32),
        ),
        in_specs=[pl.BlockSpec(memory_space=pltpu.HBM)] * 4,
        out_specs=(vmem, vmem),
        scratch_shapes=[
            pltpu.VMEM((2 * rows, width), BF16),
            pltpu.VMEM((width, 2 * rows), BF16),
            pltpu.VMEM((1, count), F32),
            pltpu.VMEM((2,) + active.shape, jnp.int32),
            dma((4, 2)),
            pltpu.VMEM((rounds + 1, 4, piece, width), BF16),
            pltpu.VMEM((rounds + 1, 4, 2, 128), F32),
            pltpu.VMEM((2 * rows // 256, 4 * piece, 256), F32),
            pltpu.VMEM((2 * rows // 256, 4 * piece, 256), BF16),
            pltpu.VMEM((width, 4 * piece), BF16),
            pltpu.VMEM((4 * piece, 128), F32),
            pltpu.VMEM((8, 2 * rows), F32),
            pltpu.VMEM((8, 2 * rows), F32),
            pltpu.VMEM((8, 2 * rows), F32),
            pltpu.VMEM((width, 2 * rows), F32),
            pltpu.VMEM((rows // 256, 8, 256), F32),
            pltpu.VMEM((rows // 256, width, 256), F32),
            pltpu.VMEM((rows, width), jnp.int16),
            pltpu.VMEM((2 * sblocks, (rounds + 1) * 8, 128), F32),
            pltpu.VMEM((sblocks, 128), F32),
            pltpu.VMEM((sblocks, 8, 128), F32),
            pltpu.VMEM((nsrc, 8, 128), F32),
            pltpu.VMEM((nsrc, share, width), jnp.int16),
            pltpu.VMEM((128, 128), F32),
            dma((rounds + 1, 4, 3)),
            dma((2, rounds, 3)),
            dma((2, rounds, 3)),
            dma((4, 2)),
            dma((4, 2)),
            dma((2, nsrc)),
            dma((2, nsrc)),
            dma((2, nsrc)),
            dma((2, nsrc)),
        ],
        compiler_params=pltpu.CompilerParams(
            collective_id=0, has_side_effects=True, vmem_limit_bytes=56 * 1024 * 1024
        ),
    )(sources, targets, target_potential.reshape(1, count), active)
    value, image = pl.pallas_call(
        functools.partial(decode, share),
        out_shape=(
            jax.ShapeDtypeStruct((sblocks, 128), F32),
            jax.ShapeDtypeStruct((rows, width), F32),
        ),
        compiler_params=pltpu.CompilerParams(vmem_limit_bytes=60 * 1024 * 1024),
    )(codes, notes)
    return value.reshape(rows), image


def solution(mesh):
    return jax.shard_map(
        per_device,
        mesh=mesh,
        in_specs=(P("tgt", None), P(("src", "tgt"), None), P(("src", "tgt")), P("tgt", None)),
        out_specs=(P("tgt"), P("tgt", None)),
        check_vma=False,
    )
```

```python
import functools
import math

import jax
import jax.numpy as jnp
from jax import lax
from jax.experimental import pallas as pl
from jax.experimental.pallas import tpu as pltpu
from jax.sharding import PartitionSpec as P

MESH = pl.DeviceIdType.MESH
F32 = jnp.float32
BF16 = jnp.bfloat16
LOWEST = -1e38


def kernel(sizes, src_hbm, tgt_hbm, pot_hbm, act_hbm, code_ref, note_ref,
           src, flat, pot, act, local, held, offsets, scores, weights, crossed, spread, top, rescale, total, turned, pairtop, pairturned, coded, mask, norm, stat,
           gotstat, gotnum, factor, recv, send_z, send_x, pair_recv, pair_send, rs_recv, rs_send, ag_recv, ag_send):
    nsrc, ntgt, eps = sizes
    rows, width = src_hbm.shape
    piece = tgt_hbm.shape[0] // 2
    block = 128
    rounds = ntgt // 4
    nz = ntgt // 4
    share = rows // nsrc
    sblocks = rows // block
    blocks = 2 * sblocks
    to_two = math.log2(math.e)

    s = lax.axis_index("src")
    t = lax.axis_index("tgt")
    half = nsrc // 2
    x_hi, y = s // half, s % half
    z, x_lo, core = t // 4, (t // 2) % 2, t % 2
    up = (s, (t + 4) % ntgt)
    down = (s, (t + ntgt - 4) % ntgt)
    twin = (s, z * 4 + x_lo * 2 + 1 - core)
    side_a = (s, z * 4 + (1 - x_lo) * 2 + core)
    side_b = ((1 - x_hi) * half + y, z * 4 + (1 - x_lo) * 2 + core)
    others = [((s + d) % nsrc, t) for d in range(1, nsrc)]

    barrier = pltpu.get_barrier_semaphore()
    for device in [up, down, twin, side_a, side_b] + others:
        pl.semaphore_signal(barrier, inc=1, device_id=device, device_id_type=MESH)

    loads = [
        pltpu.make_async_copy(tgt_hbm.at[part * piece + h * block:part * piece + (h + 1) * block, :],
                              held.at[0, 1 - part, h * block:(h + 1) * block, :], local.at[part, h])
        for part in range(2) for h in range(2)
    ] + [
        pltpu.make_async_copy(pot_hbm, pot, local.at[2, 0]),
        pltpu.make_async_copy(src_hbm, src.at[0:rows, :], local.at[2, 1]),
        pltpu.make_async_copy(act_hbm, act.at[0], local.at[3, 0]),
    ]
    for load in loads:
        load.start()

    def remote(source, target, ssem, rsem, device):
        return pltpu.make_async_remote_copy(
            src_ref=source, dst_ref=target, send_sem=ssem, recv_sem=rsem, device_id=device, device_id_type=MESH
        )

    def send(k, lane, to, to_lane, ssem, g, device):
        rsem = recv.at[to, to_lane, g]
        if g == 2:
            return remote(offsets.at[k, lane], offsets.at[to, to_lane], ssem, rsem, device)
        rows_of = slice(g * block, (g + 1) * block)
        source = held.at[k, lane, rows_of, :]
        if isinstance(k, int) and k == 0:
            first = (1 - lane) * piece + g * block
            source = tgt_hbm.at[first:first + block, :]
        return remote(source, held.at[to, to_lane, rows_of, :], ssem, rsem, device)

    def send_up(k, lane, to, g):
        return send(k, lane, to, 0, send_z.at[0, to, g], g, up)

    def send_down(k, lane, to, g):
        return send(k, lane, to, 1, send_z.at[1, to, g], g, down)

    def send_a(k, lane, g):
        return send(k, lane, k + 1, 2, send_x.at[0, k, g], g, side_a)

    def send_b(k, lane, g):
        return send(k, lane, k + 1, 3, send_x.at[1, k, g], g, side_b)

    share_sources = remote(src_hbm, src.at[rows:2 * rows, :], pair_send.at[0, 0], pair_recv.at[0, 0], twin)
    share_active = remote(act_hbm, act.at[1], pair_send.at[1, 0], pair_recv.at[1, 0], twin)

    def arrived(k, lane, g):
        here = offsets.at[k, lane] if g == 2 else held.at[k, lane, g * block:(g + 1) * block, :]
        remote(here, here, send_z.at[0, 0, g], recv.at[k, lane, g], up).wait_recv()

    pl.semaphore_wait(barrier, 5 + nsrc - 1)
    for g in range(2):
        send_up(0, 1, 1, g).start()
        send_down(0, 0, 1, g).start()
        send_a(0, 1, g).start()
        send_b(0, 0, g).start()
    share_sources.start()

    ones = jnp.ones((8, width), BF16)
    across = (((1,), (1,)), ((), ()))
    along = (((1,), (0,)), ((), ()))

    def half_norms(block_rows):
        wide = block_rows.astype(F32)
        square = 0.5 * (wide * wide)
        high = square.astype(BF16)
        low = (square - high.astype(F32)).astype(BF16)
        return lax.dot_general(ones, high, across, preferred_element_type=F32) + lax.dot_general(
            ones, low, across, preferred_element_type=F32
        )

    for part in range(2):
        loads[2 * part].wait()
        loads[2 * part + 1].wait()
        if part == 0:
            loads[4].wait()
        data = held[0, 1 - part, :, :]
        shifted = (pot[0:1, part * piece:(part + 1) * piece] - half_norms(data)[0:1, :]) * (1.0 / eps)
        for h in range(2):
            offsets[0, 1 - part, h:h + 1, :] = shifted[:, h * block:(h + 1) * block]

    send_up(0, 1, 1, 2).start()
    send_down(0, 0, 1, 2).start()
    send_a(0, 1, 2).start()
    send_b(0, 0, 2).start()
    share_active.start()

    loads[5].wait()
    loads[6].wait()

    for b in range(sblocks):
        norm[b:b + 1, :] = half_norms(src[b * block:(b + 1) * block, :])[0:1, :]

    slots = (rounds + 1) * 4 * 2
    place = lax.broadcasted_iota(jnp.int32, (slots, block), 0)
    part_h, kind, k = place % 2, (place // 2) % 4, place // 8
    from_side = kind >= 2
    k = jnp.where(from_side, k - 1, k)
    odd = (k + 2) % 2
    distance = (k + 1) // 2
    below = jnp.where(kind == 0, 1, jnp.where(kind == 1, 0, jnp.where(kind == 2, odd, 1 - odd)))
    letter = jnp.where(kind == 0, 1 - odd, jnp.where(kind == 1, odd, kind - 2))
    z_from = (z + jnp.where(below == 1, nz - distance, distance)) % nz
    x_lo_from = jnp.where(from_side, 1 - x_lo, x_lo)
    x_hi_from = jnp.where(kind == 3, 1 - x_hi, x_hi)
    owner = (x_hi_from * half + y) * ntgt + z_from * 4 + x_lo_from * 2 + core
    number = jnp.where(k < 0, -1, owner * 4 + letter * 2 + part_h)

    def set_mask(part):
        for b in range(sblocks):
            hit = jnp.zeros((slots, block), F32)
            for e in range(act.shape[2] // block):
                hit = jnp.where(number == act[part, b:b + 1, e * block:(e + 1) * block], 1.0, hit)
            mask[part * sblocks + b] = jnp.broadcast_to(jnp.max(hit, axis=1, keepdims=True), (slots, block))

    set_mask(0)
    held[0, 2:4, :, :] = jnp.zeros((2, piece, width), BF16)
    offsets[0, 2:4, :, :] = jnp.zeros((2, 2, block), F32)
    top[...] = jnp.full(top.shape, LOWEST, F32)
    rescale[...] = jnp.ones(rescale.shape, F32)
    total[...] = jnp.zeros(total.shape, F32)
    turned[...] = jnp.zeros(turned.shape, F32)
    for g in (2, 0, 1):
        send_up(0, 1, 1, g).wait_send()
        send_up(0, 0, 2, g).start()
        send_down(0, 0, 1, g).wait_send()
        send_down(0, 1, 2, g).start()
    share_active.wait_recv()
    set_mask(1)
    share_sources.wait_recv()
    tile = scores.shape[2]
    tiles = 2 * rows // tile

    def flatten(n, carry):
        data = src[pl.ds(pl.multiple_of(n * tile, tile), tile), :]
        flat[n] = (data.astype(F32) * (1.0 / eps)).T.astype(BF16)
        return carry

    lax.fori_loop(0, tiles, flatten, 0)

    per = block // 8
    inside = range(tile // block)
    cut = [slice(c * block, (c + 1) * block) for c in inside]

    def bit(k, lane, h, b):
        return mask[b, pl.ds((k * 4 + lane) * 2 + h, 1), :] > 0.5

    def score_piece(k, lane, n, maxima):
        product = lax.dot_general(
            held[k, lane, :, :], flat[n], along, preferred_element_type=F32
        )
        for h in range(piece // block):
            shifts = spread[lane * piece + h * block:lane * piece + (h + 1) * block, :]
            for c in range(tile // block):
                score = product[h * block:(h + 1) * block, c * block:(c + 1) * block] + shifts
                spot = lane * piece + h * block
                scores[n, spot:spot + block, c * block:(c + 1) * block] = score
                best = jnp.max(score.reshape(per, 8, block), axis=0)
                best = jnp.where(bit(k, lane, h, n * (tile // block) + c), best, LOWEST)
                maxima[c] = jnp.maximum(maxima[c], best)

    def spread_shifts(k, lane):
        for h in range(piece // block):
            spot = lane * piece + h * block
            spread[spot:spot + block, :] = jnp.broadcast_to(offsets[k, lane, h:h + 1, :], (block, block)).T

    def weigh_piece(k, lane, n, tops, sums):
        for h in range(piece // block):
            for c in range(tile // block):
                spot = lane * piece + h * block
                against = jnp.where(bit(k, lane, h, n * (tile // block) + c), tops[c] * to_two, -LOWEST)
                score = scores[n, spot:spot + block, c * block:(c + 1) * block]
                weight = jnp.exp2(score * to_two - against)
                sums[c] = sums[c] + jnp.sum(weight.reshape(per, 8, block), axis=0)
                weights[n, spot:spot + block, c * block:(c + 1) * block] = weight.astype(BF16)

    def cross(k, lanes):
        for lane in lanes:
            crossed[:, lane * piece:(lane + 1) * piece] = held[k, lane, :, :].T

    def absorb(fresh, ready, tick=None):
        if ready is not None:
            cross(ready, range(4))
        if fresh is not None:
            for lane in range(4):
                spread_shifts(fresh, lane)

        def one_tile(n, carry):
            if tick is not None:
                tick(n)
            tops = [top[n, 0:1, cut[c]] for c in inside]
            maxima = list(tops)
            scales = [rescale[n, 0:1, cut[c]] for c in inside]
            sums = [total[n, :, cut[c]] * scales[c] for c in inside]
            added = None
            for lane in range(4):
                if ready is not None:
                    weigh_piece(ready, lane, n, tops, sums)
                if fresh is not None:
                    score_piece(fresh, lane, n, maxima)
                if ready is not None and lane % 2 == 1:
                    span = slice((lane - 1) * piece, (lane + 1) * piece)
                    term = jnp.dot(crossed[:, span], weights[n, span, :], preferred_element_type=F32)
                    added = term if added is None else added + term
            for c in inside:
                if ready is not None:
                    total[n, :, cut[c]] = sums[c]
                    turned[n, :, cut[c]] = turned[n, :, cut[c]] * scales[c] + added[:, cut[c]]
                if fresh is not None:
                    new = jnp.max(maxima[c], axis=0, keepdims=True)
                    rescale[n, 0:1, cut[c]] = jnp.exp2((tops[c] - new) * to_two)
                    top[n, 0:1, cut[c]] = new
            return carry

        lax.fori_loop(0, tiles, one_tile, 0)

    def finish(k, after):
        cross(k, (2, 3))
        for lane in (2, 3):
            spread_shifts(k, lane)
        span = slice(2 * piece, 4 * piece)

        def one_tile(i, carry):
            n = (i + tiles // 2) % tiles
            tops = [top[n, 0:1, cut[c]] for c in inside]
            maxima = list(tops)
            for lane in (2, 3):
                score_piece(k, lane, n, maxima)
            new = [jnp.max(maxima[c], axis=0, keepdims=True) for c in inside]
            scales = [jnp.exp2((tops[c] - new[c]) * to_two) for c in inside]
            sums = [total[n, :, cut[c]] * scales[c] for c in inside]
            for lane in (2, 3):
                weigh_piece(k, lane, n, new, sums)
            added = jnp.dot(crossed[:, span], weights[n, span, :], preferred_element_type=F32)
            for c in inside:
                top[n, 0:1, cut[c]] = new[c]
                top[n, 1:2, cut[c]] = jnp.sum(sums[c], axis=0, keepdims=True)
                turned[n, :, cut[c]] = turned[n, :, cut[c]] * scales[c] + added[:, cut[c]]
            after(n)
            return carry

        lax.fori_loop(0, tiles, one_tile, 0)

    def pass_on(k, lane, g):
        onward = (send_up, send_down)[lane]
        arrived(k, lane, g)

        @pl.when(k + 2 < rounds)
        def _():
            onward(k, lane, k + 2, g).start()

        @pl.when(k % 2 == 1 - lane)
        def _():
            send_a(k, lane, g).start()

        @pl.when(k % 2 == lane)
        def _():
            send_b(k, lane, g).start()

    def sides(k):
        for lane in (2, 3):
            for g in (2, 0, 1):
                arrived(k, lane, g)

    def tick_of(k):
        def tick(n):
            for when, gs in ((0, (2, 0)), (tiles // 2, (1,))):
                @pl.when(jnp.logical_and(n == when, k < rounds))
                def _():
                    for g in gs:
                        for lane in range(2):
                            pass_on(k, lane, g)
        return tick

    absorb(0, None, tick_of(jnp.int32(1)))

    def one_round(k, carry):
        sides(k - 1)
        absorb(k - 1, k - 2, tick_of(k))
        return carry

    lax.fori_loop(2, rounds + 1, one_round, 0)
    absorb(None, rounds - 1)
    sides(rounds)

    def pair_copies(i):
        return (
            remote(top.at[i + tiles // 2], pairtop.at[i], pair_send.at[2, i], pair_recv.at[2, i], twin),
            remote(turned.at[i + tiles // 2], pairturned.at[i], pair_send.at[3, i], pair_recv.at[3, i], twin),
        )

    def share_of(q):
        return pl.ds(pl.multiple_of(q * share, share), share)

    def give_stat(q, d):
        return remote(stat.at[q // 2], gotstat.at[d], rs_send.at[0, d], rs_recv.at[0, d], (q, t))

    def give_rows(q, d):
        return remote(coded.at[share_of(q), :], gotnum.at[d], rs_send.at[1, d], rs_recv.at[1, d], (q, t))

    def merge(n, c):
        b = n * (tile // block) + c
        best = jnp.maximum(top[n, 0:1, cut[c]], pairtop[n, 0:1, cut[c]])
        ours = jnp.exp2((top[n, 0:1, cut[c]] - best) * to_two)
        theirs = jnp.exp2((pairtop[n, 0:1, cut[c]] - best) * to_two)
        both = turned[n, :, cut[c]] * ours + pairturned[n, :, cut[c]] * theirs
        largest = jnp.maximum(jnp.max(jnp.abs(both), axis=0, keepdims=True), 2e-38)
        stat[b, 0:1, :] = best
        stat[b, 1:2, :] = top[n, 1:2, cut[c]] * ours + pairtop[n, 1:2, cut[c]] * theirs
        stat[b, 2:3, :] = largest
        coded[pl.ds(pl.multiple_of(b * block, block), block), :] = jnp.round(
            (both * (1.0 / largest) * 32767.0).T
        ).astype(jnp.int32).astype(jnp.int16)
        for q in (2 * b, 2 * b + 1):
            d = (q - s + nsrc) % nsrc

            @pl.when(q != s)
            def _():
                give_stat(q, d).start()
                give_rows(q, d).start()

    def after(n):
        own = tiles // 2

        @pl.when(n >= own)
        def _():
            for copy in pair_copies(n - own):
                copy.start()

        @pl.when(n < own)
        def _():
            for copy in pair_copies(n):
                copy.wait_recv()
            for c in inside:
                merge(n, c)

    finish(rounds, after)

    gotstat[0] = stat[s // 2]
    mine = share_of(s)
    for d in range(1, nsrc):
        give_stat((s + d) % nsrc, d).wait_recv()
    tops = jnp.concatenate([gotstat[d, 0:1, :] for d in range(nsrc)], axis=0)
    dens = jnp.concatenate([gotstat[d, 1:2, :] for d in range(nsrc)], axis=0)
    sizes_of = jnp.concatenate([gotstat[d, 2:3, :] for d in range(nsrc)], axis=0)
    best = jnp.max(tops, axis=0, keepdims=True)
    scale = jnp.exp2((tops - best) * to_two)
    den = jnp.sum(scale * dens, axis=0, keepdims=True)
    value = norm[pl.ds(s // 2, 1), :] - eps * (best + jnp.log(den))
    ratio = scale / den * sizes_of
    bound = jnp.maximum(jnp.sum(ratio, axis=0, keepdims=True), 2e-38)
    note_ref[s] = jnp.concatenate([value, bound, jnp.zeros((6, block), F32)], axis=0)
    factor[...] = jnp.concatenate(
        [ratio, 1.0 / bound, jnp.zeros((block - nsrc - 1, block), F32)], axis=0
    ).T

    def spread_note(d):
        return remote(note_ref.at[s], note_ref.at[s], ag_send.at[0, d], ag_recv.at[0, d], ((s + d) % nsrc, t))

    def spread_rows(d):
        return remote(code_ref.at[mine, :], code_ref.at[mine, :], ag_send.at[1, d], ag_recv.at[1, d],
                      ((s + d) % nsrc, t))

    for d in range(1, nsrc):
        spread_note(d).start()
    column = factor[pl.ds(pl.multiple_of((s % 2) * share, share), share), :]

    def decoded(codes):
        return codes.astype(jnp.int32).astype(F32) * (1.0 / 32767.0)

    image = decoded(coded[mine, :]) * column[:, 0:1]
    for d in range(1, nsrc):
        give_rows((s + d) % nsrc, d).wait_recv()
        image = image + decoded(gotnum[d]) * column[:, d:d + 1]
    code_ref[mine, :] = jnp.round(image * column[:, nsrc:nsrc + 1] * 32767.0).astype(jnp.int32).astype(jnp.int16)

    for d in range(1, nsrc):
        spread_rows(d).start()

    for g in range(3):
        send_up(0, 0, 2, g).wait_send()
        send_down(0, 1, 2, g).wait_send()
        send_a(0, 1, g).wait_send()
        send_b(0, 0, g).wait_send()

    def drain(k, carry):
        for g in range(3):
            @pl.when(k + 2 < rounds)
            def _():
                send_up(k, 0, k + 2, g).wait_send()
                send_down(k, 1, k + 2, g).wait_send()
            send_a(k, 0, g).wait_send()
            send_b(k, 0, g).wait_send()
        return carry

    lax.fori_loop(1, rounds, drain, 0)
    for copy in (share_sources, share_active) + pair_copies(0) + pair_copies(1):
        copy.wait_send()
    for d in range(1, nsrc):
        give_stat((s + d) % nsrc, d).wait_send()
        give_rows((s + d) % nsrc, d).wait_send()
    for d in range(1, nsrc):
        q = (s + nsrc - d) % nsrc
        remote(note_ref.at[q], note_ref.at[q], ag_send.at[0, d], ag_recv.at[0, d], (q, t)).wait_recv()
        remote(code_ref.at[share_of(q), :], code_ref.at[share_of(q), :], ag_send.at[1, d], ag_recv.at[1, d],
               (q, t)).wait_recv()
        spread_note(d).wait_send()
        spread_rows(d).wait_send()


def decode(share, code_ref, note_ref, val_ref, map_ref):
    block = 128
    lane = lax.broadcasted_iota(jnp.int32, (1, block), 1)
    blocks = range(val_ref.shape[0])
    bounds = []
    for b in blocks:
        first, second = note_ref[2 * b], note_ref[2 * b + 1]
        val_ref[b:b + 1, :] = jnp.where(lane < share, first[0:1, :], second[0:1, :])
        bounds.append(jnp.where(lane < share, first[1:2, :], second[1:2, :]))
    column = jnp.concatenate(bounds + [jnp.zeros((block - len(bounds), block), F32)], axis=0).T
    for b in blocks:
        at = slice(b * block, (b + 1) * block)
        map_ref[at, :] = code_ref[at, :].astype(jnp.int32).astype(F32) * (1.0 / 32767.0) * column[:, b:b + 1]


def per_device(sources, targets, target_potential, active):
    rows, width = sources.shape
    count = targets.shape[0]
    nsrc, ntgt = lax.axis_size("src"), lax.axis_size("tgt")
    eps = 0.5 * math.sqrt(width)
    piece = count // 2
    rounds = ntgt // 4
    share = rows // nsrc
    sblocks = rows // 128
    dma = pltpu.SemaphoreType.DMA
    vmem = pl.BlockSpec(memory_space=pltpu.VMEM)
    codes, notes = pl.pallas_call(
        functools.partial(kernel, (nsrc, ntgt, eps)),
        out_shape=(
            jax.ShapeDtypeStruct((rows, width), jnp.int16),
            jax.ShapeDtypeStruct((nsrc, 8, 128), F32),
        ),
        in_specs=[pl.BlockSpec(memory_space=pltpu.HBM)] * 4,
        out_specs=(vmem, vmem),
        scratch_shapes=[
            pltpu.VMEM((2 * rows, width), BF16),
            pltpu.VMEM((2 * rows // 256, width, 256), BF16),
            pltpu.VMEM((1, count), F32),
            pltpu.VMEM((2,) + active.shape, jnp.int32),
            dma((4, 2)),
            pltpu.VMEM((rounds + 1, 4, piece, width), BF16),
            pltpu.VMEM((rounds + 1, 4, 2, 128), F32),
            pltpu.VMEM((2 * rows // 256, 4 * piece, 256), F32),
            pltpu.VMEM((2 * rows // 256, 4 * piece, 256), BF16),
            pltpu.VMEM((width, 4 * piece), BF16),
            pltpu.VMEM((4 * piece, 128), F32),
            pltpu.VMEM((2 * rows // 256, 8, 256), F32),
            pltpu.VMEM((2 * rows // 256, 8, 256), F32),
            pltpu.VMEM((2 * rows // 256, 8, 256), F32),
            pltpu.VMEM((2 * rows // 256, width, 256), F32),
            pltpu.VMEM((rows // 256, 8, 256), F32),
            pltpu.VMEM((rows // 256, width, 256), F32),
            pltpu.VMEM((rows, width), jnp.int16),
            pltpu.VMEM((2 * sblocks, (rounds + 1) * 8, 128), F32),
            pltpu.VMEM((sblocks, 128), F32),
            pltpu.VMEM((sblocks, 8, 128), F32),
            pltpu.VMEM((nsrc, 8, 128), F32),
            pltpu.VMEM((nsrc, share, width), jnp.int16),
            pltpu.VMEM((128, 128), F32),
            dma((rounds + 1, 4, 3)),
            dma((2, rounds, 3)),
            dma((2, rounds, 3)),
            dma((4, 2)),
            dma((4, 2)),
            dma((2, nsrc)),
            dma((2, nsrc)),
            dma((2, nsrc)),
            dma((2, nsrc)),
        ],
        compiler_params=pltpu.CompilerParams(
            collective_id=0, has_side_effects=True, vmem_limit_bytes=56 * 1024 * 1024
        ),
    )(sources, targets, target_potential.reshape(1, count), active)
    value, image = pl.pallas_call(
        functools.partial(decode, share),
        out_shape=(
            jax.ShapeDtypeStruct((sblocks, 128), F32),
            jax.ShapeDtypeStruct((rows, width), F32),
        ),
        compiler_params=pltpu.CompilerParams(vmem_limit_bytes=60 * 1024 * 1024),
    )(codes, notes)
    return value.reshape(rows), image


def solution(mesh):
    return jax.shard_map(
        per_device,
        mesh=mesh,
        in_specs=(P("tgt", None), P(("src", "tgt"), None), P(("src", "tgt")), P("tgt", None)),
        out_specs=(P("tgt"), P("tgt", None)),
        check_vma=False,
    )
```

```python
import functools
import math

import jax
import jax.numpy as jnp
from jax import lax
from jax.experimental import pallas as pl
from jax.experimental.pallas import tpu as pltpu
from jax.sharding import PartitionSpec as P

MESH = pl.DeviceIdType.MESH
F32 = jnp.float32
BF16 = jnp.bfloat16
LOWEST = -1e38


def kernel(sizes, src_hbm, tgt_hbm, pot_hbm, act_hbm, code_ref, note_ref,
           src, flat, pot, act, local, held, offsets, scores, weights, crossed, spread, top, rescale, total, turned, pairtop, pairturned, coded, mask, norm, stat,
           gotstat, gotnum, factor, recv, send_z, send_x, pair_recv, pair_send, rs_recv, rs_send, ag_recv, ag_send):
    nsrc, ntgt, eps = sizes
    rows, width = src_hbm.shape
    piece = tgt_hbm.shape[0] // 2
    block = 128
    rounds = ntgt // 4
    nz = ntgt // 4
    share = rows // nsrc
    sblocks = rows // block
    blocks = 2 * sblocks
    to_two = math.log2(math.e)

    s = lax.axis_index("src")
    t = lax.axis_index("tgt")
    half = nsrc // 2
    x_hi, y = s // half, s % half
    z, x_lo, core = t // 4, (t // 2) % 2, t % 2
    up = (s, (t + 4) % ntgt)
    down = (s, (t + ntgt - 4) % ntgt)
    twin = (s, z * 4 + x_lo * 2 + 1 - core)
    side_a = (s, z * 4 + (1 - x_lo) * 2 + core)
    side_b = ((1 - x_hi) * half + y, z * 4 + (1 - x_lo) * 2 + core)
    others = [((s + d) % nsrc, t) for d in range(1, nsrc)]

    barrier = pltpu.get_barrier_semaphore()
    for device in [up, down, twin, side_a, side_b] + others:
        pl.semaphore_signal(barrier, inc=1, device_id=device, device_id_type=MESH)

    loads = [
        pltpu.make_async_copy(tgt_hbm.at[part * piece + h * block:part * piece + (h + 1) * block, :],
                              held.at[0, 1 - part, h * block:(h + 1) * block, :], local.at[part, h])
        for part in range(2) for h in range(2)
    ] + [
        pltpu.make_async_copy(pot_hbm, pot, local.at[2, 0]),
        pltpu.make_async_copy(src_hbm, src.at[0:rows, :], local.at[2, 1]),
        pltpu.make_async_copy(act_hbm, act.at[0], local.at[3, 0]),
    ]
    for load in loads:
        load.start()

    def remote(source, target, ssem, rsem, device):
        return pltpu.make_async_remote_copy(
            src_ref=source, dst_ref=target, send_sem=ssem, recv_sem=rsem, device_id=device, device_id_type=MESH
        )

    def send(k, lane, to, to_lane, ssem, g, device):
        rsem = recv.at[to, to_lane, g]
        if g == 2:
            return remote(offsets.at[k, lane], offsets.at[to, to_lane], ssem, rsem, device)
        rows_of = slice(g * block, (g + 1) * block)
        source = held.at[k, lane, rows_of, :]
        if isinstance(k, int) and k == 0:
            first = (1 - lane) * piece + g * block
            source = tgt_hbm.at[first:first + block, :]
        return remote(source, held.at[to, to_lane, rows_of, :], ssem, rsem, device)

    def send_up(k, lane, to, g):
        return send(k, lane, to, 0, send_z.at[0, to, g], g, up)

    def send_down(k, lane, to, g):
        return send(k, lane, to, 1, send_z.at[1, to, g], g, down)

    def send_a(k, lane, g):
        return send(k, lane, k + 1, 2, send_x.at[0, k, g], g, side_a)

    def send_b(k, lane, g):
        return send(k, lane, k + 1, 3, send_x.at[1, k, g], g, side_b)

    share_sources = remote(src_hbm, src.at[rows:2 * rows, :], pair_send.at[0, 0], pair_recv.at[0, 0], twin)
    share_active = remote(act_hbm, act.at[1], pair_send.at[1, 0], pair_recv.at[1, 0], twin)

    def arrived(k, lane, g):
        here = offsets.at[k, lane] if g == 2 else held.at[k, lane, g * block:(g + 1) * block, :]
        remote(here, here, send_z.at[0, 0, g], recv.at[k, lane, g], up).wait_recv()

    pl.semaphore_wait(barrier, 5 + nsrc - 1)
    for g in range(2):
        send_up(0, 1, 1, g).start()
        send_down(0, 0, 1, g).start()
        send_a(0, 1, g).start()
        send_b(0, 0, g).start()
    share_sources.start()

    ones = jnp.ones((8, width), BF16)
    across = (((1,), (1,)), ((), ()))
    along = (((1,), (0,)), ((), ()))

    def half_norms(block_rows):
        wide = block_rows.astype(F32)
        square = 0.5 * (wide * wide)
        high = square.astype(BF16)
        low = (square - high.astype(F32)).astype(BF16)
        return lax.dot_general(ones, high, across, preferred_element_type=F32) + lax.dot_general(
            ones, low, across, preferred_element_type=F32
        )

    for part in range(2):
        loads[2 * part].wait()
        loads[2 * part + 1].wait()
        if part == 0:
            loads[4].wait()
        data = held[0, 1 - part, :, :]
        shifted = (pot[0:1, part * piece:(part + 1) * piece] - half_norms(data)[0:1, :]) * (1.0 / eps)
        for h in range(2):
            offsets[0, 1 - part, h:h + 1, :] = shifted[:, h * block:(h + 1) * block]

    send_up(0, 1, 1, 2).start()
    send_down(0, 0, 1, 2).start()
    send_a(0, 1, 2).start()
    send_b(0, 0, 2).start()
    share_active.start()

    loads[5].wait()
    loads[6].wait()

    for b in range(sblocks):
        norm[b:b + 1, :] = half_norms(src[b * block:(b + 1) * block, :])[0:1, :]

    slots = (rounds + 1) * 4 * 2
    place = lax.broadcasted_iota(jnp.int32, (slots, block), 0)
    part_h, kind, k = place % 2, (place // 2) % 4, place // 8
    from_side = kind >= 2
    k = jnp.where(from_side, k - 1, k)
    odd = k % 2
    distance = (k + 1) // 2
    below = jnp.where(kind == 0, 1, jnp.where(kind == 1, 0, jnp.where(kind == 2, odd, 1 - odd)))
    letter = jnp.where(kind == 0, 1 - odd, jnp.where(kind == 1, odd, kind - 2))
    z_from = (z + jnp.where(below == 1, nz - distance, distance)) % nz
    x_lo_from = jnp.where(from_side, 1 - x_lo, x_lo)
    x_hi_from = jnp.where(kind == 3, 1 - x_hi, x_hi)
    owner = (x_hi_from * half + y) * ntgt + z_from * 4 + x_lo_from * 2 + core
    number = owner * 4 + letter * 2 + part_h

    def set_mask(part):
        for b in range(sblocks):
            hit = jnp.zeros((slots, block), F32)
            for e in range(act.shape[2] // block):
                hit = jnp.where(number == act[part, b:b + 1, e * block:(e + 1) * block], 1.0, hit)
            mask[part * sblocks + b] = jnp.broadcast_to(jnp.max(hit, axis=1, keepdims=True), (slots, block))

    set_mask(0)
    top[...] = jnp.full(top.shape, LOWEST, F32)
    rescale[...] = jnp.ones(rescale.shape, F32)
    total[...] = jnp.zeros(total.shape, F32)
    turned[...] = jnp.zeros(turned.shape, F32)
    for g in (2, 0, 1):
        send_up(0, 1, 1, g).wait_send()
        send_up(0, 0, 2, g).start()
        send_down(0, 0, 1, g).wait_send()
        send_down(0, 1, 2, g).start()
    share_active.wait_recv()
    set_mask(1)
    share_sources.wait_recv()
    for b in range(2 * sblocks):
        at = slice(b * block, (b + 1) * block)
        flat[:, at] = (src[at, :].astype(F32) * (1.0 / eps)).T.astype(BF16)

    tile = scores.shape[2]
    per = block // 8

    def bit(k, lane, h, b):
        return mask[b, pl.ds((k * 4 + lane) * 2 + h, 1), :] > 0.5

    def score_pair(k, lane, n, maxima):
        data = held[k, lane:lane + 2, :, :].reshape(2 * piece, width)
        product = lax.dot_general(
            data, flat[:, n * tile:(n + 1) * tile], along, preferred_element_type=F32
        )
        for near in (lane, lane + 1):
            for h in range(piece // block):
                spot = near * piece + h * block
                shifts = spread[spot:spot + block, :]
                for c in range(tile // block):
                    down = spot - lane * piece
                    score = product[down:down + block, c * block:(c + 1) * block] + shifts
                    scores[n, spot:spot + block, c * block:(c + 1) * block] = score
                    best = jnp.max(score.reshape(per, 8, block), axis=0)
                    best = jnp.where(bit(k, near, h, n * (tile // block) + c), best, LOWEST)
                    maxima[c] = jnp.maximum(maxima[c], best)

    def spread_shifts(k, lane):
        for h in range(piece // block):
            spot = lane * piece + h * block
            spread[spot:spot + block, :] = jnp.broadcast_to(offsets[k, lane, h:h + 1, :], (block, block)).T

    def weigh_piece(k, lane, n, tops, sums):
        for h in range(piece // block):
            for c in range(tile // block):
                spot = lane * piece + h * block
                against = jnp.where(bit(k, lane, h, n * (tile // block) + c), tops[c] * to_two, -LOWEST)
                score = scores[n, spot:spot + block, c * block:(c + 1) * block]
                weight = jnp.exp2(score * to_two - against)
                sums[c] = sums[c] + jnp.sum(weight.reshape(per, 8, block), axis=0)
                weights[n, spot:spot + block, c * block:(c + 1) * block] = weight.astype(BF16)

    def columns(n, c):
        return slice(n * tile + c * block, n * tile + (c + 1) * block)

    everything = (0, 1, 2, 3)

    def cross(k, lanes):
        for lane in lanes:
            crossed[:, lane * piece:(lane + 1) * piece] = held[k, lane, :, :].T

    def absorb(fresh, ready, tick=None, fresh_lanes=everything, ready_lanes=everything):
        if ready is not None:
            cross(ready, ready_lanes)
        if fresh is not None:
            for lane in fresh_lanes:
                spread_shifts(fresh, lane)
        parts = range(tile // block)
        for n in range(2 * rows // tile):
            if tick is not None:
                tick(n)
            tops = [top[0:1, columns(n, c)] for c in parts]
            maxima = list(tops)
            scales = [rescale[0:1, columns(n, c)] for c in parts]
            sums = [total[:, columns(n, c)] * scales[c] for c in parts]
            added = None
            for lane in (0, 2):
                if ready is not None and lane in ready_lanes:
                    weigh_piece(ready, lane, n, tops, sums)
                    weigh_piece(ready, lane + 1, n, tops, sums)
                if fresh is not None and lane in fresh_lanes:
                    score_pair(fresh, lane, n, maxima)
                if ready is not None and lane in ready_lanes:
                    span = slice(lane * piece, (lane + 2) * piece)
                    term = jnp.dot(crossed[:, span], weights[n, span, :], preferred_element_type=F32)
                    added = term if added is None else added + term
            for c in parts:
                at = columns(n, c)
                if ready is not None:
                    total[:, at] = sums[c]
                    turned[:, at] = turned[:, at] * scales[c] + added[:, c * block:(c + 1) * block]
                if fresh is not None:
                    new = jnp.max(maxima[c], axis=0, keepdims=True)
                    rescale[0:1, at] = jnp.exp2((tops[c] - new) * to_two)
                    top[0:1, at] = new

    def finish(k, after):
        cross(k, (2, 3))
        for lane in (2, 3):
            spread_shifts(k, lane)
        parts = range(tile // block)
        span = slice(2 * piece, 4 * piece)
        for n in (2, 3, 0, 1):
            tops = [top[0:1, columns(n, c)] for c in parts]
            maxima = list(tops)
            score_pair(k, 2, n, maxima)
            new = [jnp.max(maxima[c], axis=0, keepdims=True) for c in parts]
            scales = [jnp.exp2((tops[c] - new[c]) * to_two) for c in parts]
            sums = [total[:, columns(n, c)] * scales[c] for c in parts]
            for lane in (2, 3):
                weigh_piece(k, lane, n, new, sums)
            added = jnp.dot(crossed[:, span], weights[n, span, :], preferred_element_type=F32)
            for c in parts:
                at = columns(n, c)
                top[0:1, at] = new[c]
                top[1:2, at] = jnp.sum(sums[c], axis=0, keepdims=True)
                turned[:, at] = turned[:, at] * scales[c] + added[:, c * block:(c + 1) * block]
            after(n)

    def pass_on(k, lane, g):
        onward = (send_up, send_down)[lane]
        arrived(k, lane, g)

        @pl.when(k + 2 < rounds)
        def _():
            onward(k, lane, k + 2, g).start()

        @pl.when(k % 2 == 1 - lane)
        def _():
            send_a(k, lane, g).start()

        @pl.when(k % 2 == lane)
        def _():
            send_b(k, lane, g).start()

    def sides(k):
        for lane in (2, 3):
            for g in (2, 0, 1):
                arrived(k, lane, g)

    def tick_of(k):
        def tick(n):
            for g in ((2, 0), (), (1,), ())[n]:
                for lane in range(2):
                    pass_on(k, lane, g)
        return tick

    absorb(0, None, tick_of(jnp.int32(1)), fresh_lanes=(0, 1))
    sides(1)
    absorb(1, 0, tick_of(jnp.int32(2)), ready_lanes=(0, 1))

    def one_round(k, carry):
        sides(k - 1)
        absorb(k - 1, k - 2, tick_of(k))
        return carry

    lax.fori_loop(3, rounds, one_round, 0)
    sides(rounds - 1)
    absorb(rounds - 1, rounds - 2)
    absorb(None, rounds - 1)
    sides(rounds)

    def pair_copies(i):
        at = slice(rows + i * tile, rows + (i + 1) * tile)
        return (
            remote(top.at[:, at], pairtop.at[i], pair_send.at[2, i], pair_recv.at[2, i], twin),
            remote(turned.at[:, at], pairturned.at[i], pair_send.at[3, i], pair_recv.at[3, i], twin),
        )

    def share_of(q):
        return pl.ds(pl.multiple_of(q * share, share), share)

    def give_stat(q, d):
        return remote(stat.at[q // 2], gotstat.at[d], rs_send.at[0, d], rs_recv.at[0, d], (q, t))

    def give_rows(q, d):
        return remote(coded.at[share_of(q), :], gotnum.at[d], rs_send.at[1, d], rs_recv.at[1, d], (q, t))

    def merge(b):
        i, inside = b // (tile // block), slice(b % (tile // block) * block, (b % (tile // block) + 1) * block)
        at = slice(b * block, (b + 1) * block)
        best = jnp.maximum(top[0:1, at], pairtop[i, 0:1, inside])
        ours = jnp.exp2((top[0:1, at] - best) * to_two)
        theirs = jnp.exp2((pairtop[i, 0:1, inside] - best) * to_two)
        both = turned[:, at] * ours + pairturned[i, :, inside] * theirs
        largest = jnp.maximum(jnp.max(jnp.abs(both), axis=0, keepdims=True), 2e-38)
        stat[b, 0:1, :] = best
        stat[b, 1:2, :] = top[1:2, at] * ours + pairtop[i, 1:2, inside] * theirs
        stat[b, 2:3, :] = largest
        coded[at, :] = jnp.round((both * (1.0 / largest) * 32767.0).T).astype(jnp.int32).astype(jnp.int16)
        for q in (2 * b, 2 * b + 1):
            d = (q - s + nsrc) % nsrc

            @pl.when(q != s)
            def _():
                give_stat(q, d).start()
                give_rows(q, d).start()

    def after(n):
        own = rows // tile
        if n >= own:
            for copy in pair_copies(n - own):
                copy.start()
        else:
            for copy in pair_copies(n):
                copy.wait_recv()
            for c in range(tile // block):
                merge(n * (tile // block) + c)

    finish(rounds, after)

    gotstat[0] = stat[s // 2]
    mine = share_of(s)
    for d in range(1, nsrc):
        give_stat((s + d) % nsrc, d).wait_recv()
    tops = jnp.concatenate([gotstat[d, 0:1, :] for d in range(nsrc)], axis=0)
    dens = jnp.concatenate([gotstat[d, 1:2, :] for d in range(nsrc)], axis=0)
    sizes_of = jnp.concatenate([gotstat[d, 2:3, :] for d in range(nsrc)], axis=0)
    best = jnp.max(tops, axis=0, keepdims=True)
    scale = jnp.exp2((tops - best) * to_two)
    den = jnp.sum(scale * dens, axis=0, keepdims=True)
    value = norm[pl.ds(s // 2, 1), :] - eps * (best + jnp.log(den))
    ratio = scale / den * sizes_of
    bound = jnp.maximum(jnp.sum(ratio, axis=0, keepdims=True), 2e-38)
    note_ref[s] = jnp.concatenate([value, bound, jnp.zeros((6, block), F32)], axis=0)
    factor[...] = jnp.concatenate(
        [ratio, 1.0 / bound, jnp.zeros((block - nsrc - 1, block), F32)], axis=0
    ).T

    def spread_note(d):
        return remote(note_ref.at[s], note_ref.at[s], ag_send.at[0, d], ag_recv.at[0, d], ((s + d) % nsrc, t))

    def spread_rows(d):
        return remote(code_ref.at[mine, :], code_ref.at[mine, :], ag_send.at[1, d], ag_recv.at[1, d],
                      ((s + d) % nsrc, t))

    for d in range(1, nsrc):
        spread_note(d).start()
    column = factor[pl.ds(pl.multiple_of((s % 2) * share, share), share), :]

    def decoded(codes):
        return codes.astype(jnp.int32).astype(F32) * (1.0 / 32767.0)

    image = decoded(coded[mine, :]) * column[:, 0:1]
    for d in range(1, nsrc):
        give_rows((s + d) % nsrc, d).wait_recv()
        image = image + decoded(gotnum[d]) * column[:, d:d + 1]
    code_ref[mine, :] = jnp.round(image * column[:, nsrc:nsrc + 1] * 32767.0).astype(jnp.int32).astype(jnp.int16)

    for d in range(1, nsrc):
        spread_rows(d).start()

    for g in range(3):
        send_up(0, 0, 2, g).wait_send()
        send_down(0, 1, 2, g).wait_send()
        send_a(0, 1, g).wait_send()
        send_b(0, 0, g).wait_send()

    def drain(k, carry):
        for g in range(3):
            @pl.when(k + 2 < rounds)
            def _():
                send_up(k, 0, k + 2, g).wait_send()
                send_down(k, 1, k + 2, g).wait_send()
            send_a(k, 0, g).wait_send()
            send_b(k, 0, g).wait_send()
        return carry

    lax.fori_loop(1, rounds, drain, 0)
    for copy in (share_sources, share_active) + pair_copies(0) + pair_copies(1):
        copy.wait_send()
    for d in range(1, nsrc):
        give_stat((s + d) % nsrc, d).wait_send()
        give_rows((s + d) % nsrc, d).wait_send()
    for d in range(1, nsrc):
        q = (s + nsrc - d) % nsrc
        remote(note_ref.at[q], note_ref.at[q], ag_send.at[0, d], ag_recv.at[0, d], (q, t)).wait_recv()
        remote(code_ref.at[share_of(q), :], code_ref.at[share_of(q), :], ag_send.at[1, d], ag_recv.at[1, d],
               (q, t)).wait_recv()
        spread_note(d).wait_send()
        spread_rows(d).wait_send()


def decode(share, code_ref, note_ref, val_ref, map_ref):
    block = 128
    lane = lax.broadcasted_iota(jnp.int32, (1, block), 1)
    blocks = range(val_ref.shape[0])
    bounds = []
    for b in blocks:
        first, second = note_ref[2 * b], note_ref[2 * b + 1]
        val_ref[b:b + 1, :] = jnp.where(lane < share, first[0:1, :], second[0:1, :])
        bounds.append(jnp.where(lane < share, first[1:2, :], second[1:2, :]))
    column = jnp.concatenate(bounds + [jnp.zeros((block - len(bounds), block), F32)], axis=0).T
    for b in blocks:
        at = slice(b * block, (b + 1) * block)
        map_ref[at, :] = code_ref[at, :].astype(jnp.int32).astype(F32) * (1.0 / 32767.0) * column[:, b:b + 1]


def per_device(sources, targets, target_potential, active):
    rows, width = sources.shape
    count = targets.shape[0]
    nsrc, ntgt = lax.axis_size("src"), lax.axis_size("tgt")
    eps = 0.5 * math.sqrt(width)
    piece = count // 2
    rounds = ntgt // 4
    share = rows // nsrc
    sblocks = rows // 128
    dma = pltpu.SemaphoreType.DMA
    vmem = pl.BlockSpec(memory_space=pltpu.VMEM)
    codes, notes = pl.pallas_call(
        functools.partial(kernel, (nsrc, ntgt, eps)),
        out_shape=(
            jax.ShapeDtypeStruct((rows, width), jnp.int16),
            jax.ShapeDtypeStruct((nsrc, 8, 128), F32),
        ),
        in_specs=[pl.BlockSpec(memory_space=pltpu.HBM)] * 4,
        out_specs=(vmem, vmem),
        scratch_shapes=[
            pltpu.VMEM((2 * rows, width), BF16),
            pltpu.VMEM((width, 2 * rows), BF16),
            pltpu.VMEM((1, count), F32),
            pltpu.VMEM((2,) + active.shape, jnp.int32),
            dma((4, 2)),
            pltpu.VMEM((rounds + 1, 4, piece, width), BF16),
            pltpu.VMEM((rounds + 1, 4, 2, 128), F32),
            pltpu.VMEM((2 * rows // 256, 4 * piece, 256), F32),
            pltpu.VMEM((2 * rows // 256, 4 * piece, 256), BF16),
            pltpu.VMEM((width, 4 * piece), BF16),
            pltpu.VMEM((4 * piece, 128), F32),
            pltpu.VMEM((8, 2 * rows), F32),
            pltpu.VMEM((8, 2 * rows), F32),
            pltpu.VMEM((8, 2 * rows), F32),
            pltpu.VMEM((width, 2 * rows), F32),
            pltpu.VMEM((rows // 256, 8, 256), F32),
            pltpu.VMEM((rows // 256, width, 256), F32),
            pltpu.VMEM((rows, width), jnp.int16),
            pltpu.VMEM((2 * sblocks, (rounds + 1) * 8, 128), F32),
            pltpu.VMEM((sblocks, 128), F32),
            pltpu.VMEM((sblocks, 8, 128), F32),
            pltpu.VMEM((nsrc, 8, 128), F32),
            pltpu.VMEM((nsrc, share, width), jnp.int16),
            pltpu.VMEM((128, 128), F32),
            dma((rounds + 1, 4, 3)),
            dma((2, rounds, 3)),
            dma((2, rounds, 3)),
            dma((4, 2)),
            dma((4, 2)),
            dma((2, nsrc)),
            dma((2, nsrc)),
            dma((2, nsrc)),
            dma((2, nsrc)),
        ],
        compiler_params=pltpu.CompilerParams(
            collective_id=0, has_side_effects=True, vmem_limit_bytes=56 * 1024 * 1024
        ),
    )(sources, targets, target_potential.reshape(1, count), active)
    value, image = pl.pallas_call(
        functools.partial(decode, share),
        out_shape=(
            jax.ShapeDtypeStruct((sblocks, 128), F32),
            jax.ShapeDtypeStruct((rows, width), F32),
        ),
        compiler_params=pltpu.CompilerParams(vmem_limit_bytes=60 * 1024 * 1024),
    )(codes, notes)
    return value.reshape(rows), image


def solution(mesh):
    return jax.shard_map(
        per_device,
        mesh=mesh,
        in_specs=(P("tgt", None), P(("src", "tgt"), None), P(("src", "tgt")), P("tgt", None)),
        out_specs=(P("tgt"), P("tgt", None)),
        check_vma=False,
    )
```

```python
import functools
import math

import jax
import jax.numpy as jnp
from jax import lax
from jax.experimental import pallas as pl
from jax.experimental.pallas import tpu as pltpu
from jax.sharding import PartitionSpec as P

MESH = pl.DeviceIdType.MESH
F32 = jnp.float32
BF16 = jnp.bfloat16
LOWEST = -1e38


def kernel(sizes, src_hbm, tgt_hbm, pot_hbm, act_hbm, code_ref, note_ref,
           src, flat, pot, act, local, held, offsets, scores, weights, crossed, spread, top, rescale, total, turned, pairtop, pairturned, coded, mask, norm, stat,
           gotstat, gotnum, factor, recv, send_z, send_x, pair_recv, pair_send, rs_recv, rs_send, ag_recv, ag_send):
    nsrc, ntgt, eps = sizes
    rows, width = src_hbm.shape
    piece = tgt_hbm.shape[0] // 2
    block = 128
    rounds = ntgt // 4
    nz = ntgt // 4
    share = rows // nsrc
    sblocks = rows // block
    blocks = 2 * sblocks
    to_two = math.log2(math.e)

    s = lax.axis_index("src")
    t = lax.axis_index("tgt")
    half = nsrc // 2
    x_hi, y = s // half, s % half
    z, x_lo, core = t // 4, (t // 2) % 2, t % 2
    up = (s, (t + 4) % ntgt)
    down = (s, (t + ntgt - 4) % ntgt)
    twin = (s, z * 4 + x_lo * 2 + 1 - core)
    side_a = (s, z * 4 + (1 - x_lo) * 2 + core)
    side_b = ((1 - x_hi) * half + y, z * 4 + (1 - x_lo) * 2 + core)
    others = [((s + d) % nsrc, t) for d in range(1, nsrc)]

    barrier = pltpu.get_barrier_semaphore()
    for device in [up, down, twin, side_a, side_b] + others:
        pl.semaphore_signal(barrier, inc=1, device_id=device, device_id_type=MESH)

    loads = [
        pltpu.make_async_copy(tgt_hbm.at[part * piece + h * block:part * piece + (h + 1) * block, :],
                              held.at[0, 1 - part, h * block:(h + 1) * block, :], local.at[part, h])
        for part in range(2) for h in range(2)
    ] + [
        pltpu.make_async_copy(pot_hbm, pot, local.at[2, 0]),
        pltpu.make_async_copy(src_hbm, src.at[0:rows, :], local.at[2, 1]),
        pltpu.make_async_copy(act_hbm, act.at[0], local.at[3, 0]),
    ]
    for load in loads:
        load.start()

    def remote(source, target, ssem, rsem, device):
        return pltpu.make_async_remote_copy(
            src_ref=source, dst_ref=target, send_sem=ssem, recv_sem=rsem, device_id=device, device_id_type=MESH
        )

    def send(k, lane, to, to_lane, ssem, g, device):
        rsem = recv.at[to, to_lane, g]
        if g == 2:
            return remote(offsets.at[k, lane], offsets.at[to, to_lane], ssem, rsem, device)
        rows_of = slice(g * block, (g + 1) * block)
        source = held.at[k, lane, rows_of, :]
        if isinstance(k, int) and k == 0:
            first = (1 - lane) * piece + g * block
            source = tgt_hbm.at[first:first + block, :]
        return remote(source, held.at[to, to_lane, rows_of, :], ssem, rsem, device)

    def send_up(k, lane, to, g):
        return send(k, lane, to, 0, send_z.at[0, to, g], g, up)

    def send_down(k, lane, to, g):
        return send(k, lane, to, 1, send_z.at[1, to, g], g, down)

    def send_a(k, lane, g):
        return send(k, lane, k + 1, 2, send_x.at[0, k, g], g, side_a)

    def send_b(k, lane, g):
        return send(k, lane, k + 1, 3, send_x.at[1, k, g], g, side_b)

    share_sources = remote(src_hbm, src.at[rows:2 * rows, :], pair_send.at[0, 0], pair_recv.at[0, 0], twin)
    share_active = remote(act_hbm, act.at[1], pair_send.at[1, 0], pair_recv.at[1, 0], twin)

    def arrived(k, lane, g):
        here = offsets.at[k, lane] if g == 2 else held.at[k, lane, g * block:(g + 1) * block, :]
        remote(here, here, send_z.at[0, 0, g], recv.at[k, lane, g], up).wait_recv()

    pl.semaphore_wait(barrier, 5 + nsrc - 1)
    for g in range(2):
        send_up(0, 1, 1, g).start()
        send_down(0, 0, 1, g).start()
        send_a(0, 1, g).start()
        send_b(0, 0, g).start()
    share_sources.start()
    for g in range(2):
        send_up(0, 0, 2, g).start()
        send_down(0, 1, 2, g).start()

    ones = jnp.ones((8, width), BF16)
    across = (((1,), (1,)), ((), ()))
    along = (((1,), (0,)), ((), ()))

    def half_norms(block_rows):
        wide = block_rows.astype(F32)
        square = 0.5 * (wide * wide)
        high = square.astype(BF16)
        low = (square - high.astype(F32)).astype(BF16)
        return lax.dot_general(ones, high, across, preferred_element_type=F32) + lax.dot_general(
            ones, low, across, preferred_element_type=F32
        )

    for part in range(2):
        loads[2 * part].wait()
        loads[2 * part + 1].wait()
        if part == 0:
            loads[4].wait()
        data = held[0, 1 - part, :, :]
        shifted = (pot[0:1, part * piece:(part + 1) * piece] - half_norms(data)[0:1, :]) * (1.0 / eps)
        for h in range(2):
            offsets[0, 1 - part, h:h + 1, :] = shifted[:, h * block:(h + 1) * block]

    send_up(0, 1, 1, 2).start()
    send_down(0, 0, 1, 2).start()
    send_a(0, 1, 2).start()
    send_b(0, 0, 2).start()
    send_up(0, 0, 2, 2).start()
    send_down(0, 1, 2, 2).start()
    share_active.start()

    loads[5].wait()
    loads[6].wait()

    for b in range(sblocks):
        norm[b:b + 1, :] = half_norms(src[b * block:(b + 1) * block, :])[0:1, :]

    slots = (rounds + 1) * 4 * 2
    place = lax.broadcasted_iota(jnp.int32, (slots, block), 0)
    part_h, kind, k = place % 2, (place // 2) % 4, place // 8
    from_side = kind >= 2
    k = jnp.where(from_side, k - 1, k)
    odd = k % 2
    distance = (k + 1) // 2
    below = jnp.where(kind == 0, 1, jnp.where(kind == 1, 0, jnp.where(kind == 2, odd, 1 - odd)))
    letter = jnp.where(kind == 0, 1 - odd, jnp.where(kind == 1, odd, kind - 2))
    z_from = (z + jnp.where(below == 1, nz - distance, distance)) % nz
    x_lo_from = jnp.where(from_side, 1 - x_lo, x_lo)
    x_hi_from = jnp.where(kind == 3, 1 - x_hi, x_hi)
    owner = (x_hi_from * half + y) * ntgt + z_from * 4 + x_lo_from * 2 + core
    number = owner * 4 + letter * 2 + part_h

    def set_mask(part):
        for b in range(sblocks):
            hit = jnp.zeros((slots, block), F32)
            for e in range(act.shape[2] // block):
                hit = jnp.where(number == act[part, b:b + 1, e * block:(e + 1) * block], 1.0, hit)
            mask[part * sblocks + b] = jnp.broadcast_to(jnp.max(hit, axis=1, keepdims=True), (slots, block))

    set_mask(0)
    top[...] = jnp.full(top.shape, LOWEST, F32)
    rescale[...] = jnp.ones(rescale.shape, F32)
    total[...] = jnp.zeros(total.shape, F32)
    turned[...] = jnp.zeros(turned.shape, F32)
    share_active.wait_recv()
    set_mask(1)
    share_sources.wait_recv()
    for b in range(2 * sblocks):
        at = slice(b * block, (b + 1) * block)
        flat[:, at] = (src[at, :].astype(F32) * (1.0 / eps)).T.astype(BF16)

    tile = scores.shape[2]
    per = block // 8

    def bit(k, lane, h, b):
        return mask[b, pl.ds((k * 4 + lane) * 2 + h, 1), :] > 0.5

    def score_piece(k, lane, n, maxima):
        product = lax.dot_general(
            held[k, lane, :, :], flat[:, n * tile:(n + 1) * tile], along, preferred_element_type=F32
        )
        for h in range(piece // block):
            shifts = spread[lane * piece + h * block:lane * piece + (h + 1) * block, :]
            for c in range(tile // block):
                score = product[h * block:(h + 1) * block, c * block:(c + 1) * block] + shifts
                spot = lane * piece + h * block
                scores[n, spot:spot + block, c * block:(c + 1) * block] = score
                best = jnp.max(score.reshape(per, 8, block), axis=0)
                best = jnp.where(bit(k, lane, h, n * (tile // block) + c), best, LOWEST)
                maxima[c] = jnp.maximum(maxima[c], best)

    def spread_shifts(k, lane):
        for h in range(piece // block):
            spot = lane * piece + h * block
            spread[spot:spot + block, :] = jnp.broadcast_to(offsets[k, lane, h:h + 1, :], (block, block)).T

    def weigh_piece(k, lane, n, tops, sums):
        for h in range(piece // block):
            for c in range(tile // block):
                spot = lane * piece + h * block
                against = jnp.where(bit(k, lane, h, n * (tile // block) + c), tops[c] * to_two, -LOWEST)
                score = scores[n, spot:spot + block, c * block:(c + 1) * block]
                weight = jnp.exp2(score * to_two - against)
                sums[c] = sums[c] + jnp.sum(weight.reshape(per, 8, block), axis=0)
                weights[n, spot:spot + block, c * block:(c + 1) * block] = weight.astype(BF16)

    def columns(n, c):
        return slice(n * tile + c * block, n * tile + (c + 1) * block)

    everything = (0, 1, 2, 3)

    def cross(k, lanes):
        for lane in lanes:
            crossed[:, lane * piece:(lane + 1) * piece] = held[k, lane, :, :].T

    def absorb(fresh, ready, tick=None, fresh_lanes=everything, ready_lanes=everything):
        if ready is not None:
            cross(ready, ready_lanes)
        if fresh is not None:
            for lane in fresh_lanes:
                spread_shifts(fresh, lane)
        parts = range(tile // block)
        for n in range(2 * rows // tile):
            if tick is not None:
                tick(n)
            tops = [top[0:1, columns(n, c)] for c in parts]
            maxima = list(tops)
            scales = [rescale[0:1, columns(n, c)] for c in parts]
            sums = [total[:, columns(n, c)] * scales[c] for c in parts]
            added = None
            for lane in range(4):
                if ready is not None and lane in ready_lanes:
                    weigh_piece(ready, lane, n, tops, sums)
                if fresh is not None and lane in fresh_lanes:
                    score_piece(fresh, lane, n, maxima)
                if ready is not None and lane in ready_lanes and lane % 2 == 1:
                    span = slice((lane - 1) * piece, (lane + 1) * piece)
                    term = jnp.dot(crossed[:, span], weights[n, span, :], preferred_element_type=F32)
                    added = term if added is None else added + term
            for c in parts:
                at = columns(n, c)
                if ready is not None:
                    total[:, at] = sums[c]
                    turned[:, at] = turned[:, at] * scales[c] + added[:, c * block:(c + 1) * block]
                if fresh is not None:
                    new = jnp.max(maxima[c], axis=0, keepdims=True)
                    rescale[0:1, at] = jnp.exp2((tops[c] - new) * to_two)
                    top[0:1, at] = new

    def finish(k, after):
        cross(k, (2, 3))
        for lane in (2, 3):
            spread_shifts(k, lane)
        parts = range(tile // block)
        span = slice(2 * piece, 4 * piece)
        for n in (2, 3, 0, 1):
            tops = [top[0:1, columns(n, c)] for c in parts]
            maxima = list(tops)
            for lane in (2, 3):
                score_piece(k, lane, n, maxima)
            new = [jnp.max(maxima[c], axis=0, keepdims=True) for c in parts]
            scales = [jnp.exp2((tops[c] - new[c]) * to_two) for c in parts]
            sums = [total[:, columns(n, c)] * scales[c] for c in parts]
            for lane in (2, 3):
                weigh_piece(k, lane, n, new, sums)
            added = jnp.dot(crossed[:, span], weights[n, span, :], preferred_element_type=F32)
            for c in parts:
                at = columns(n, c)
                top[0:1, at] = new[c]
                top[1:2, at] = jnp.sum(sums[c], axis=0, keepdims=True)
                turned[:, at] = turned[:, at] * scales[c] + added[:, c * block:(c + 1) * block]
            after(n)

    def pass_on(k, lane, g):
        onward = (send_up, send_down)[lane]
        arrived(k, lane, g)

        @pl.when(k + 2 < rounds)
        def _():
            onward(k, lane, k + 2, g).start()

        @pl.when(k % 2 == 1 - lane)
        def _():
            send_a(k, lane, g).start()

        @pl.when(k % 2 == lane)
        def _():
            send_b(k, lane, g).start()

    def sides(k):
        for lane in (2, 3):
            for g in (2, 0, 1):
                arrived(k, lane, g)

    def tick_of(k):
        def tick(n):
            for g in ((2, 0), (), (1,), ())[n]:
                for lane in range(2):
                    pass_on(k, lane, g)
        return tick

    absorb(0, None, fresh_lanes=(0, 1))
    for g in (2, 0, 1):
        for lane in range(2):
            pass_on(jnp.int32(1), lane, g)
    sides(1)
    absorb(1, 0, tick_of(jnp.int32(2)), ready_lanes=(0, 1))

    def one_round(k, carry):
        sides(k - 1)
        absorb(k - 1, k - 2, tick_of(k))
        return carry

    lax.fori_loop(3, rounds, one_round, 0)
    sides(rounds - 1)
    absorb(rounds - 1, rounds - 2)
    absorb(None, rounds - 1)
    sides(rounds)

    def pair_copies(i):
        at = slice(rows + i * tile, rows + (i + 1) * tile)
        return (
            remote(top.at[:, at], pairtop.at[i], pair_send.at[2, i], pair_recv.at[2, i], twin),
            remote(turned.at[:, at], pairturned.at[i], pair_send.at[3, i], pair_recv.at[3, i], twin),
        )

    def share_of(q):
        return pl.ds(pl.multiple_of(q * share, share), share)

    def give_stat(q, d):
        return remote(stat.at[q // 2], gotstat.at[d], rs_send.at[0, d], rs_recv.at[0, d], (q, t))

    def give_rows(q, d):
        return remote(coded.at[share_of(q), :], gotnum.at[d], rs_send.at[1, d], rs_recv.at[1, d], (q, t))

    def merge(b):
        i, inside = b // (tile // block), slice(b % (tile // block) * block, (b % (tile // block) + 1) * block)
        at = slice(b * block, (b + 1) * block)
        best = jnp.maximum(top[0:1, at], pairtop[i, 0:1, inside])
        ours = jnp.exp2((top[0:1, at] - best) * to_two)
        theirs = jnp.exp2((pairtop[i, 0:1, inside] - best) * to_two)
        both = turned[:, at] * ours + pairturned[i, :, inside] * theirs
        largest = jnp.maximum(jnp.max(jnp.abs(both), axis=0, keepdims=True), 2e-38)
        stat[b, 0:1, :] = best
        stat[b, 1:2, :] = top[1:2, at] * ours + pairtop[i, 1:2, inside] * theirs
        stat[b, 2:3, :] = largest
        coded[at, :] = jnp.round((both * (1.0 / largest) * 32767.0).T).astype(jnp.int32).astype(jnp.int16)
        for q in (2 * b, 2 * b + 1):
            d = (q - s + nsrc) % nsrc

            @pl.when(q != s)
            def _():
                give_stat(q, d).start()
                give_rows(q, d).start()

    def after(n):
        own = rows // tile
        if n >= own:
            for copy in pair_copies(n - own):
                copy.start()
        else:
            for copy in pair_copies(n):
                copy.wait_recv()
            for c in range(tile // block):
                merge(n * (tile // block) + c)

    finish(rounds, after)

    gotstat[0] = stat[s // 2]
    mine = share_of(s)
    for d in range(1, nsrc):
        give_stat((s + d) % nsrc, d).wait_recv()
    tops = jnp.concatenate([gotstat[d, 0:1, :] for d in range(nsrc)], axis=0)
    dens = jnp.concatenate([gotstat[d, 1:2, :] for d in range(nsrc)], axis=0)
    sizes_of = jnp.concatenate([gotstat[d, 2:3, :] for d in range(nsrc)], axis=0)
    best = jnp.max(tops, axis=0, keepdims=True)
    scale = jnp.exp2((tops - best) * to_two)
    den = jnp.sum(scale * dens, axis=0, keepdims=True)
    value = norm[pl.ds(s // 2, 1), :] - eps * (best + jnp.log(den))
    ratio = scale / den * sizes_of
    bound = jnp.maximum(jnp.sum(ratio, axis=0, keepdims=True), 2e-38)
    note_ref[s] = jnp.concatenate([value, bound, jnp.zeros((6, block), F32)], axis=0)
    factor[...] = jnp.concatenate(
        [ratio, 1.0 / bound, jnp.zeros((block - nsrc - 1, block), F32)], axis=0
    ).T

    def spread_note(d):
        return remote(note_ref.at[s], note_ref.at[s], ag_send.at[0, d], ag_recv.at[0, d], ((s + d) % nsrc, t))

    def spread_rows(d):
        return remote(code_ref.at[mine, :], code_ref.at[mine, :], ag_send.at[1, d], ag_recv.at[1, d],
                      ((s + d) % nsrc, t))

    for d in range(1, nsrc):
        spread_note(d).start()
    column = factor[pl.ds(pl.multiple_of((s % 2) * share, share), share), :]

    def decoded(codes):
        return codes.astype(jnp.int32).astype(F32) * (1.0 / 32767.0)

    image = decoded(coded[mine, :]) * column[:, 0:1]
    for d in range(1, nsrc):
        give_rows((s + d) % nsrc, d).wait_recv()
        image = image + decoded(gotnum[d]) * column[:, d:d + 1]
    code_ref[mine, :] = jnp.round(image * column[:, nsrc:nsrc + 1] * 32767.0).astype(jnp.int32).astype(jnp.int16)

    for d in range(1, nsrc):
        spread_rows(d).start()

    for g in range(3):
        send_up(0, 1, 1, g).wait_send()
        send_down(0, 0, 1, g).wait_send()
        send_up(0, 0, 2, g).wait_send()
        send_down(0, 1, 2, g).wait_send()
        send_a(0, 1, g).wait_send()
        send_b(0, 0, g).wait_send()

    def drain(k, carry):
        for g in range(3):
            @pl.when(k + 2 < rounds)
            def _():
                send_up(k, 0, k + 2, g).wait_send()
                send_down(k, 1, k + 2, g).wait_send()
            send_a(k, 0, g).wait_send()
            send_b(k, 0, g).wait_send()
        return carry

    lax.fori_loop(1, rounds, drain, 0)
    for copy in (share_sources, share_active) + pair_copies(0) + pair_copies(1):
        copy.wait_send()
    for d in range(1, nsrc):
        give_stat((s + d) % nsrc, d).wait_send()
        give_rows((s + d) % nsrc, d).wait_send()
    for d in range(1, nsrc):
        q = (s + nsrc - d) % nsrc
        remote(note_ref.at[q], note_ref.at[q], ag_send.at[0, d], ag_recv.at[0, d], (q, t)).wait_recv()
        remote(code_ref.at[share_of(q), :], code_ref.at[share_of(q), :], ag_send.at[1, d], ag_recv.at[1, d],
               (q, t)).wait_recv()
        spread_note(d).wait_send()
        spread_rows(d).wait_send()


def decode(share, code_ref, note_ref, val_ref, map_ref):
    block = 128
    lane = lax.broadcasted_iota(jnp.int32, (1, block), 1)
    blocks = range(val_ref.shape[0])
    bounds = []
    for b in blocks:
        first, second = note_ref[2 * b], note_ref[2 * b + 1]
        val_ref[b:b + 1, :] = jnp.where(lane < share, first[0:1, :], second[0:1, :])
        bounds.append(jnp.where(lane < share, first[1:2, :], second[1:2, :]))
    column = jnp.concatenate(bounds + [jnp.zeros((block - len(bounds), block), F32)], axis=0).T
    for b in blocks:
        at = slice(b * block, (b + 1) * block)
        map_ref[at, :] = code_ref[at, :].astype(jnp.int32).astype(F32) * (1.0 / 32767.0) * column[:, b:b + 1]


def per_device(sources, targets, target_potential, active):
    rows, width = sources.shape
    count = targets.shape[0]
    nsrc, ntgt = lax.axis_size("src"), lax.axis_size("tgt")
    eps = 0.5 * math.sqrt(width)
    piece = count // 2
    rounds = ntgt // 4
    share = rows // nsrc
    sblocks = rows // 128
    dma = pltpu.SemaphoreType.DMA
    vmem = pl.BlockSpec(memory_space=pltpu.VMEM)
    codes, notes = pl.pallas_call(
        functools.partial(kernel, (nsrc, ntgt, eps)),
        out_shape=(
            jax.ShapeDtypeStruct((rows, width), jnp.int16),
            jax.ShapeDtypeStruct((nsrc, 8, 128), F32),
        ),
        in_specs=[pl.BlockSpec(memory_space=pltpu.HBM)] * 4,
        out_specs=(vmem, vmem),
        scratch_shapes=[
            pltpu.VMEM((2 * rows, width), BF16),
            pltpu.VMEM((width, 2 * rows), BF16),
            pltpu.VMEM((1, count), F32),
            pltpu.VMEM((2,) + active.shape, jnp.int32),
            dma((4, 2)),
            pltpu.VMEM((rounds + 1, 4, piece, width), BF16),
            pltpu.VMEM((rounds + 1, 4, 2, 128), F32),
            pltpu.VMEM((2 * rows // 256, 4 * piece, 256), F32),
            pltpu.VMEM((2 * rows // 256, 4 * piece, 256), BF16),
            pltpu.VMEM((width, 4 * piece), BF16),
            pltpu.VMEM((4 * piece, 128), F32),
            pltpu.VMEM((8, 2 * rows), F32),
            pltpu.VMEM((8, 2 * rows), F32),
            pltpu.VMEM((8, 2 * rows), F32),
            pltpu.VMEM((width, 2 * rows), F32),
            pltpu.VMEM((rows // 256, 8, 256), F32),
            pltpu.VMEM((rows // 256, width, 256), F32),
            pltpu.VMEM((rows, width), jnp.int16),
            pltpu.VMEM((2 * sblocks, (rounds + 1) * 8, 128), F32),
            pltpu.VMEM((sblocks, 128), F32),
            pltpu.VMEM((sblocks, 8, 128), F32),
            pltpu.VMEM((nsrc, 8, 128), F32),
            pltpu.VMEM((nsrc, share, width), jnp.int16),
            pltpu.VMEM((128, 128), F32),
            dma((rounds + 1, 4, 3)),
            dma((2, rounds, 3)),
            dma((2, rounds, 3)),
            dma((4, 2)),
            dma((4, 2)),
            dma((2, nsrc)),
            dma((2, nsrc)),
            dma((2, nsrc)),
            dma((2, nsrc)),
        ],
        compiler_params=pltpu.CompilerParams(
            collective_id=0, has_side_effects=True, vmem_limit_bytes=56 * 1024 * 1024
        ),
    )(sources, targets, target_potential.reshape(1, count), active)
    value, image = pl.pallas_call(
        functools.partial(decode, share),
        out_shape=(
            jax.ShapeDtypeStruct((sblocks, 128), F32),
            jax.ShapeDtypeStruct((rows, width), F32),
        ),
        compiler_params=pltpu.CompilerParams(vmem_limit_bytes=60 * 1024 * 1024),
    )(codes, notes)
    return value.reshape(rows), image


def solution(mesh):
    return jax.shard_map(
        per_device,
        mesh=mesh,
        in_specs=(P("tgt", None), P(("src", "tgt"), None), P(("src", "tgt")), P("tgt", None)),
        out_specs=(P("tgt"), P("tgt", None)),
        check_vma=False,
    )
```

```python
import functools
import math

import jax
import jax.numpy as jnp
from jax import lax
from jax.experimental import pallas as pl
from jax.experimental.pallas import tpu as pltpu
from jax.sharding import PartitionSpec as P

MESH = pl.DeviceIdType.MESH
F32 = jnp.float32
BF16 = jnp.bfloat16
LOWEST = -1e38


def kernel(sizes, src_hbm, tgt_hbm, pot_hbm, act_hbm, code_ref, note_ref,
           src, flat, pot, act, local, held, offsets, scores, weights, crossed, spread, top, rescale, total, turned, pairtop, pairturned, coded, mask, norm, stat,
           gotstat, gotnum, factor, recv, send_z, send_x, pair_recv, pair_send, rs_recv, rs_send, ag_recv, ag_send):
    nsrc, ntgt, eps = sizes
    rows, width = src_hbm.shape
    piece = tgt_hbm.shape[0] // 2
    block = 128
    rounds = ntgt // 4
    nz = ntgt // 4
    share = rows // nsrc
    sblocks = rows // block
    blocks = 2 * sblocks
    to_two = math.log2(math.e)

    s = lax.axis_index("src")
    t = lax.axis_index("tgt")
    half = nsrc // 2
    x_hi, y = s // half, s % half
    z, x_lo, core = t // 4, (t // 2) % 2, t % 2
    up = (s, (t + 4) % ntgt)
    down = (s, (t + ntgt - 4) % ntgt)
    twin = (s, z * 4 + x_lo * 2 + 1 - core)
    side_a = (s, z * 4 + (1 - x_lo) * 2 + core)
    side_b = ((1 - x_hi) * half + y, z * 4 + (1 - x_lo) * 2 + core)
    others = [((s + d) % nsrc, t) for d in range(1, nsrc)]

    barrier = pltpu.get_barrier_semaphore()
    for device in [up, down, twin, side_a, side_b] + others:
        pl.semaphore_signal(barrier, inc=1, device_id=device, device_id_type=MESH)

    loads = [
        pltpu.make_async_copy(tgt_hbm.at[part * piece + h * block:part * piece + (h + 1) * block, :],
                              held.at[0, 1 - part, h * block:(h + 1) * block, :], local.at[part, h])
        for part in range(2) for h in range(2)
    ] + [
        pltpu.make_async_copy(pot_hbm, pot, local.at[2, 0]),
        pltpu.make_async_copy(src_hbm, src.at[0:rows, :], local.at[2, 1]),
        pltpu.make_async_copy(act_hbm, act.at[0], local.at[3, 0]),
    ]
    for load in loads:
        load.start()

    def remote(source, target, ssem, rsem, device):
        return pltpu.make_async_remote_copy(
            src_ref=source, dst_ref=target, send_sem=ssem, recv_sem=rsem, device_id=device, device_id_type=MESH
        )

    def send(k, lane, to, to_lane, ssem, g, device):
        rsem = recv.at[to, to_lane, g]
        if g == 2:
            return remote(offsets.at[k, lane], offsets.at[to, to_lane], ssem, rsem, device)
        rows_of = slice(g * block, (g + 1) * block)
        source = held.at[k, lane, rows_of, :]
        if isinstance(k, int) and k == 0:
            first = (1 - lane) * piece + g * block
            source = tgt_hbm.at[first:first + block, :]
        return remote(source, held.at[to, to_lane, rows_of, :], ssem, rsem, device)

    def send_up(k, lane, to, g):
        return send(k, lane, to, 0, send_z.at[0, to, g], g, up)

    def send_down(k, lane, to, g):
        return send(k, lane, to, 1, send_z.at[1, to, g], g, down)

    def send_a(k, lane, g):
        return send(k, lane, k + 1, 2, send_x.at[0, k, g], g, side_a)

    def send_b(k, lane, g):
        return send(k, lane, k + 1, 3, send_x.at[1, k, g], g, side_b)

    share_sources = remote(src_hbm, src.at[rows:2 * rows, :], pair_send.at[0, 0], pair_recv.at[0, 0], twin)
    share_active = remote(act_hbm, act.at[1], pair_send.at[1, 0], pair_recv.at[1, 0], twin)

    def arrived(k, lane, g):
        here = offsets.at[k, lane] if g == 2 else held.at[k, lane, g * block:(g + 1) * block, :]
        remote(here, here, send_z.at[0, 0, g], recv.at[k, lane, g], up).wait_recv()

    pl.semaphore_wait(barrier, 5 + nsrc - 1)
    for g in range(2):
        send_up(0, 1, 1, g).start()
        send_down(0, 0, 1, g).start()
        send_a(0, 1, g).start()
        send_b(0, 0, g).start()
    share_sources.start()

    ones = jnp.ones((8, width), BF16)
    across = (((1,), (1,)), ((), ()))
    along = (((1,), (0,)), ((), ()))

    def half_norms(block_rows):
        wide = block_rows.astype(F32)
        square = 0.5 * (wide * wide)
        high = square.astype(BF16)
        low = (square - high.astype(F32)).astype(BF16)
        return lax.dot_general(ones, high, across, preferred_element_type=F32) + lax.dot_general(
            ones, low, across, preferred_element_type=F32
        )

    for part in range(2):
        loads[2 * part].wait()
        loads[2 * part + 1].wait()
        if part == 0:
            loads[4].wait()
        data = held[0, 1 - part, :, :]
        shifted = (pot[0:1, part * piece:(part + 1) * piece] - half_norms(data)[0:1, :]) * (1.0 / eps)
        for h in range(2):
            offsets[0, 1 - part, h:h + 1, :] = shifted[:, h * block:(h + 1) * block]

    send_up(0, 1, 1, 2).start()
    send_down(0, 0, 1, 2).start()
    send_a(0, 1, 2).start()
    send_b(0, 0, 2).start()
    share_active.start()

    loads[5].wait()
    loads[6].wait()

    for b in range(sblocks):
        norm[b:b + 1, :] = half_norms(src[b * block:(b + 1) * block, :])[0:1, :]

    slots = (rounds + 1) * 4 * 2
    place = lax.broadcasted_iota(jnp.int32, (slots, block), 0)
    part_h, kind, k = place % 2, (place // 2) % 4, place // 8
    from_side = kind >= 2
    k = jnp.where(from_side, k - 1, k)
    odd = k % 2
    distance = (k + 1) // 2
    below = jnp.where(kind == 0, 1, jnp.where(kind == 1, 0, jnp.where(kind == 2, odd, 1 - odd)))
    letter = jnp.where(kind == 0, 1 - odd, jnp.where(kind == 1, odd, kind - 2))
    z_from = (z + jnp.where(below == 1, nz - distance, distance)) % nz
    x_lo_from = jnp.where(from_side, 1 - x_lo, x_lo)
    x_hi_from = jnp.where(kind == 3, 1 - x_hi, x_hi)
    owner = (x_hi_from * half + y) * ntgt + z_from * 4 + x_lo_from * 2 + core
    number = owner * 4 + letter * 2 + part_h

    def set_mask(part):
        for b in range(sblocks):
            hit = jnp.zeros((slots, block), F32)
            for e in range(act.shape[2] // block):
                hit = jnp.where(number == act[part, b:b + 1, e * block:(e + 1) * block], 1.0, hit)
            mask[part * sblocks + b] = jnp.broadcast_to(jnp.max(hit, axis=1, keepdims=True), (slots, block))

    set_mask(0)
    top[...] = jnp.full(top.shape, LOWEST, F32)
    rescale[...] = jnp.ones(rescale.shape, F32)
    total[...] = jnp.zeros(total.shape, F32)
    turned[...] = jnp.zeros(turned.shape, F32)
    for g in (2, 0, 1):
        send_up(0, 1, 1, g).wait_send()
        send_up(0, 0, 2, g).start()
        send_down(0, 0, 1, g).wait_send()
        send_down(0, 1, 2, g).start()
    share_active.wait_recv()
    set_mask(1)
    share_sources.wait_recv()
    for b in range(2 * sblocks):
        at = slice(b * block, (b + 1) * block)
        flat[:, at] = (src[at, :].astype(F32) * (1.0 / eps)).T.astype(BF16)

    tile = scores.shape[2]
    per = block // 8

    def bit(k, lane, h, b):
        return mask[b, pl.ds((k * 4 + lane) * 2 + h, 1), :] > 0.5

    def score_piece(k, lane, n, maxima):
        product = lax.dot_general(
            held[k, lane, :, :], flat[:, n * tile:(n + 1) * tile], along, preferred_element_type=F32
        )
        for h in range(piece // block):
            shifts = spread[lane * piece + h * block:lane * piece + (h + 1) * block, :]
            for c in range(tile // block):
                score = product[h * block:(h + 1) * block, c * block:(c + 1) * block] + shifts
                spot = lane * piece + h * block
                scores[n, spot:spot + block, c * block:(c + 1) * block] = score
                best = jnp.max(score.reshape(per, 8, block), axis=0)
                best = jnp.where(bit(k, lane, h, n * (tile // block) + c), best, LOWEST)
                maxima[c] = jnp.maximum(maxima[c], best)

    def spread_shifts(k, lane):
        for h in range(piece // block):
            spot = lane * piece + h * block
            spread[spot:spot + block, :] = jnp.broadcast_to(offsets[k, lane, h:h + 1, :], (block, block)).T

    def weigh_piece(k, lane, n, tops, sums):
        for h in range(piece // block):
            for c in range(tile // block):
                spot = lane * piece + h * block
                against = jnp.where(bit(k, lane, h, n * (tile // block) + c), tops[c] * to_two, -LOWEST)
                score = scores[n, spot:spot + block, c * block:(c + 1) * block]
                weight = jnp.exp2(score * to_two - against)
                sums[c] = sums[c] + jnp.sum(weight.reshape(per, 8, block), axis=0)
                weights[n, spot:spot + block, c * block:(c + 1) * block] = weight.astype(BF16)

    def columns(n, c):
        return slice(n * tile + c * block, n * tile + (c + 1) * block)

    everything = (0, 1, 2, 3)

    def cross(k, lanes):
        for lane in lanes:
            crossed[:, lane * piece:(lane + 1) * piece] = held[k, lane, :, :].T

    def absorb(fresh, ready, tick=None, fresh_lanes=everything, ready_lanes=everything):
        if ready is not None:
            cross(ready, ready_lanes)
        if fresh is not None:
            for lane in fresh_lanes:
                spread_shifts(fresh, lane)
        parts = range(tile // block)
        for n in range(2 * rows // tile):
            if tick is not None:
                tick(n)
            tops = [top[0:1, columns(n, c)] for c in parts]
            maxima = list(tops)
            scales = [rescale[0:1, columns(n, c)] for c in parts]
            sums = [total[:, columns(n, c)] * scales[c] for c in parts]
            added = None
            for lane in range(4):
                if ready is not None and lane in ready_lanes:
                    weigh_piece(ready, lane, n, tops, sums)
                if fresh is not None and lane in fresh_lanes:
                    score_piece(fresh, lane, n, maxima)
                if ready is not None and lane in ready_lanes and lane % 2 == 1:
                    span = slice((lane - 1) * piece, (lane + 1) * piece)
                    term = jnp.dot(crossed[:, span], weights[n, span, :], preferred_element_type=F32)
                    added = term if added is None else added + term
            for c in parts:
                at = columns(n, c)
                if ready is not None:
                    total[:, at] = sums[c]
                    turned[:, at] = turned[:, at] * scales[c] + added[:, c * block:(c + 1) * block]
                if fresh is not None:
                    new = jnp.max(maxima[c], axis=0, keepdims=True)
                    rescale[0:1, at] = jnp.exp2((tops[c] - new) * to_two)
                    top[0:1, at] = new

    def finish(k, after):
        cross(k, (2, 3))
        for lane in (2, 3):
            spread_shifts(k, lane)
        parts = range(tile // block)
        span = slice(2 * piece, 4 * piece)
        for n in (2, 3, 0, 1):
            tops = [top[0:1, columns(n, c)] for c in parts]
            maxima = list(tops)
            for lane in (2, 3):
                score_piece(k, lane, n, maxima)
            new = [jnp.max(maxima[c], axis=0, keepdims=True) for c in parts]
            scales = [jnp.exp2((tops[c] - new[c]) * to_two) for c in parts]
            sums = [total[:, columns(n, c)] * scales[c] for c in parts]
            for lane in (2, 3):
                weigh_piece(k, lane, n, new, sums)
            added = jnp.dot(crossed[:, span], weights[n, span, :], preferred_element_type=F32)
            for c in parts:
                at = columns(n, c)
                top[0:1, at] = new[c]
                top[1:2, at] = jnp.sum(sums[c], axis=0, keepdims=True)
                turned[:, at] = turned[:, at] * scales[c] + added[:, c * block:(c + 1) * block]
            after(n)

    def pass_on(k, lane, g):
        onward = (send_up, send_down)[lane]
        arrived(k, lane, g)

        @pl.when(k + 2 < rounds)
        def _():
            onward(k, lane, k + 2, g).start()

        @pl.when(k % 2 == 1 - lane)
        def _():
            send_a(k, lane, g).start()

        @pl.when(k % 2 == lane)
        def _():
            send_b(k, lane, g).start()

    def sides(k):
        for lane in (2, 3):
            for g in (2, 0, 1):
                arrived(k, lane, g)

    def tick_of(k):
        def tick(n):
            for g in ((2, 0), (1,), (), ())[n]:
                for lane in range(2):
                    pass_on(k, lane, g)
        return tick

    absorb(0, None, tick_of(jnp.int32(1)), fresh_lanes=(0, 1))
    sides(1)
    absorb(1, 0, tick_of(jnp.int32(2)), ready_lanes=(0, 1))

    def one_round(k, carry):
        sides(k - 1)
        absorb(k - 1, k - 2, tick_of(k))
        return carry

    lax.fori_loop(3, rounds, one_round, 0)
    sides(rounds - 1)
    absorb(rounds - 1, rounds - 2)
    absorb(None, rounds - 1)
    sides(rounds)

    def pair_copies(i):
        at = slice(rows + i * tile, rows + (i + 1) * tile)
        return (
            remote(top.at[:, at], pairtop.at[i], pair_send.at[2, i], pair_recv.at[2, i], twin),
            remote(turned.at[:, at], pairturned.at[i], pair_send.at[3, i], pair_recv.at[3, i], twin),
        )

    def share_of(q):
        return pl.ds(pl.multiple_of(q * share, share), share)

    def give_stat(q, d):
        return remote(stat.at[q // 2], gotstat.at[d], rs_send.at[0, d], rs_recv.at[0, d], (q, t))

    def give_rows(q, d):
        return remote(coded.at[share_of(q), :], gotnum.at[d], rs_send.at[1, d], rs_recv.at[1, d], (q, t))

    def merge(b):
        i, inside = b // (tile // block), slice(b % (tile // block) * block, (b % (tile // block) + 1) * block)
        at = slice(b * block, (b + 1) * block)
        best = jnp.maximum(top[0:1, at], pairtop[i, 0:1, inside])
        ours = jnp.exp2((top[0:1, at] - best) * to_two)
        theirs = jnp.exp2((pairtop[i, 0:1, inside] - best) * to_two)
        both = turned[:, at] * ours + pairturned[i, :, inside] * theirs
        largest = jnp.maximum(jnp.max(jnp.abs(both), axis=0, keepdims=True), 2e-38)
        stat[b, 0:1, :] = best
        stat[b, 1:2, :] = top[1:2, at] * ours + pairtop[i, 1:2, inside] * theirs
        stat[b, 2:3, :] = largest
        coded[at, :] = jnp.round((both * (1.0 / largest) * 32767.0).T).astype(jnp.int32).astype(jnp.int16)
        for q in (2 * b, 2 * b + 1):
            d = (q - s + nsrc) % nsrc

            @pl.when(q != s)
            def _():
                give_stat(q, d).start()
                give_rows(q, d).start()

    def after(n):
        own = rows // tile
        if n >= own:
            for copy in pair_copies(n - own):
                copy.start()
        else:
            for copy in pair_copies(n):
                copy.wait_recv()
            for c in range(tile // block):
                merge(n * (tile // block) + c)

    finish(rounds, after)

    gotstat[0] = stat[s // 2]
    mine = share_of(s)
    for d in range(1, nsrc):
        give_stat((s + d) % nsrc, d).wait_recv()
    tops = jnp.concatenate([gotstat[d, 0:1, :] for d in range(nsrc)], axis=0)
    dens = jnp.concatenate([gotstat[d, 1:2, :] for d in range(nsrc)], axis=0)
    sizes_of = jnp.concatenate([gotstat[d, 2:3, :] for d in range(nsrc)], axis=0)
    best = jnp.max(tops, axis=0, keepdims=True)
    scale = jnp.exp2((tops - best) * to_two)
    den = jnp.sum(scale * dens, axis=0, keepdims=True)
    value = norm[pl.ds(s // 2, 1), :] - eps * (best + jnp.log(den))
    ratio = scale / den * sizes_of
    bound = jnp.maximum(jnp.sum(ratio, axis=0, keepdims=True), 2e-38)
    note_ref[s] = jnp.concatenate([value, bound, jnp.zeros((6, block), F32)], axis=0)
    factor[...] = jnp.concatenate(
        [ratio, 1.0 / bound, jnp.zeros((block - nsrc - 1, block), F32)], axis=0
    ).T

    def spread_note(d):
        return remote(note_ref.at[s], note_ref.at[s], ag_send.at[0, d], ag_recv.at[0, d], ((s + d) % nsrc, t))

    def spread_rows(d):
        return remote(code_ref.at[mine, :], code_ref.at[mine, :], ag_send.at[1, d], ag_recv.at[1, d],
                      ((s + d) % nsrc, t))

    for d in range(1, nsrc):
        spread_note(d).start()
    column = factor[pl.ds(pl.multiple_of((s % 2) * share, share), share), :]

    def decoded(codes):
        return codes.astype(jnp.int32).astype(F32) * (1.0 / 32767.0)

    image = decoded(coded[mine, :]) * column[:, 0:1]
    for d in range(1, nsrc):
        give_rows((s + d) % nsrc, d).wait_recv()
        image = image + decoded(gotnum[d]) * column[:, d:d + 1]
    code_ref[mine, :] = jnp.round(image * column[:, nsrc:nsrc + 1] * 32767.0).astype(jnp.int32).astype(jnp.int16)

    for d in range(1, nsrc):
        spread_rows(d).start()

    for g in range(3):
        send_up(0, 0, 2, g).wait_send()
        send_down(0, 1, 2, g).wait_send()
        send_a(0, 1, g).wait_send()
        send_b(0, 0, g).wait_send()

    def drain(k, carry):
        for g in range(3):
            @pl.when(k + 2 < rounds)
            def _():
                send_up(k, 0, k + 2, g).wait_send()
                send_down(k, 1, k + 2, g).wait_send()
            send_a(k, 0, g).wait_send()
            send_b(k, 0, g).wait_send()
        return carry

    lax.fori_loop(1, rounds, drain, 0)
    for copy in (share_sources, share_active) + pair_copies(0) + pair_copies(1):
        copy.wait_send()
    for d in range(1, nsrc):
        give_stat((s + d) % nsrc, d).wait_send()
        give_rows((s + d) % nsrc, d).wait_send()
    for d in range(1, nsrc):
        q = (s + nsrc - d) % nsrc
        remote(note_ref.at[q], note_ref.at[q], ag_send.at[0, d], ag_recv.at[0, d], (q, t)).wait_recv()
        remote(code_ref.at[share_of(q), :], code_ref.at[share_of(q), :], ag_send.at[1, d], ag_recv.at[1, d],
               (q, t)).wait_recv()
        spread_note(d).wait_send()
        spread_rows(d).wait_send()


def decode(share, code_ref, note_ref, val_ref, map_ref):
    block = 128
    lane = lax.broadcasted_iota(jnp.int32, (1, block), 1)
    blocks = range(val_ref.shape[0])
    bounds = []
    for b in blocks:
        first, second = note_ref[2 * b], note_ref[2 * b + 1]
        val_ref[b:b + 1, :] = jnp.where(lane < share, first[0:1, :], second[0:1, :])
        bounds.append(jnp.where(lane < share, first[1:2, :], second[1:2, :]))
    column = jnp.concatenate(bounds + [jnp.zeros((block - len(bounds), block), F32)], axis=0).T
    for b in blocks:
        at = slice(b * block, (b + 1) * block)
        map_ref[at, :] = code_ref[at, :].astype(jnp.int32).astype(F32) * (1.0 / 32767.0) * column[:, b:b + 1]


def per_device(sources, targets, target_potential, active):
    rows, width = sources.shape
    count = targets.shape[0]
    nsrc, ntgt = lax.axis_size("src"), lax.axis_size("tgt")
    eps = 0.5 * math.sqrt(width)
    piece = count // 2
    rounds = ntgt // 4
    share = rows // nsrc
    sblocks = rows // 128
    dma = pltpu.SemaphoreType.DMA
    vmem = pl.BlockSpec(memory_space=pltpu.VMEM)
    codes, notes = pl.pallas_call(
        functools.partial(kernel, (nsrc, ntgt, eps)),
        out_shape=(
            jax.ShapeDtypeStruct((rows, width), jnp.int16),
            jax.ShapeDtypeStruct((nsrc, 8, 128), F32),
        ),
        in_specs=[pl.BlockSpec(memory_space=pltpu.HBM)] * 4,
        out_specs=(vmem, vmem),
        scratch_shapes=[
            pltpu.VMEM((2 * rows, width), BF16),
            pltpu.VMEM((width, 2 * rows), BF16),
            pltpu.VMEM((1, count), F32),
            pltpu.VMEM((2,) + active.shape, jnp.int32),
            dma((4, 2)),
            pltpu.VMEM((rounds + 1, 4, piece, width), BF16),
            pltpu.VMEM((rounds + 1, 4, 2, 128), F32),
            pltpu.VMEM((2 * rows // 256, 4 * piece, 256), F32),
            pltpu.VMEM((2 * rows // 256, 4 * piece, 256), BF16),
            pltpu.VMEM((width, 4 * piece), BF16),
            pltpu.VMEM((4 * piece, 128), F32),
            pltpu.VMEM((8, 2 * rows), F32),
            pltpu.VMEM((8, 2 * rows), F32),
            pltpu.VMEM((8, 2 * rows), F32),
            pltpu.VMEM((width, 2 * rows), F32),
            pltpu.VMEM((rows // 256, 8, 256), F32),
            pltpu.VMEM((rows // 256, width, 256), F32),
            pltpu.VMEM((rows, width), jnp.int16),
            pltpu.VMEM((2 * sblocks, (rounds + 1) * 8, 128), F32),
            pltpu.VMEM((sblocks, 128), F32),
            pltpu.VMEM((sblocks, 8, 128), F32),
            pltpu.VMEM((nsrc, 8, 128), F32),
            pltpu.VMEM((nsrc, share, width), jnp.int16),
            pltpu.VMEM((128, 128), F32),
            dma((rounds + 1, 4, 3)),
            dma((2, rounds, 3)),
            dma((2, rounds, 3)),
            dma((4, 2)),
            dma((4, 2)),
            dma((2, nsrc)),
            dma((2, nsrc)),
            dma((2, nsrc)),
            dma((2, nsrc)),
        ],
        compiler_params=pltpu.CompilerParams(
            collective_id=0, has_side_effects=True, vmem_limit_bytes=56 * 1024 * 1024
        ),
    )(sources, targets, target_potential.reshape(1, count), active)
    value, image = pl.pallas_call(
        functools.partial(decode, share),
        out_shape=(
            jax.ShapeDtypeStruct((sblocks, 128), F32),
            jax.ShapeDtypeStruct((rows, width), F32),
        ),
        compiler_params=pltpu.CompilerParams(vmem_limit_bytes=60 * 1024 * 1024),
    )(codes, notes)
    return value.reshape(rows), image


def solution(mesh):
    return jax.shard_map(
        per_device,
        mesh=mesh,
        in_specs=(P("tgt", None), P(("src", "tgt"), None), P(("src", "tgt")), P("tgt", None)),
        out_specs=(P("tgt"), P("tgt", None)),
        check_vma=False,
    )
```
